128 devices in a mesh: seq: 16 (over x, z), roll: 2 (over y_lo), head: 4 (over y_hi, core).
Axes of the slice: x: 4, y: 4 (y_hi: 2, y_lo: 2; y = y_hi * 2 + y_lo), z: 4, core: 2. Of those that a mesh axis runs over, the one named last changes fastest.
Arguments:
- queries: bfloat16 [2, 3072, 64, 128], P('roll', 'seq', 'head'), may hold values from -7 to 7
- rollout_keys: bfloat16 [2, 3072, 8, 128], P('roll', 'seq', 'head'), may hold values from -6 to 6
- rollout_values: bfloat16 [2, 3072, 8, 128], P('roll', 'seq', 'head'), may hold values from -24 to 24
- prompt_keys: bfloat16 [1024, 8, 128], P(('seq', 'roll'), 'head'), may hold values from -4.5 to 4.5
- prompt_values: bfloat16 [1024, 8, 128], P(('seq', 'roll'), 'head'), may hold values from -24 to 24
- grad_out: bfloat16 [2, 3072, 64, 128], P('roll', 'seq', 'head'), may hold values from -24 to 24
- lengths: int32 [2], P('roll'), may hold values from 768 to 3072, as said below
Outputs:
- attention_out: bfloat16 [2, 3072, 64, 128], P('roll', 'seq', 'head')
- grad_queries: bfloat16 [2, 3072, 64, 128], P('roll', 'seq', 'head')
- grad_rollout_keys: bfloat16 [2, 3072, 8, 128], P('roll', 'seq', 'head')
- grad_rollout_values: bfloat16 [2, 3072, 8, 128], P('roll', 'seq', 'head')
- grad_prompt_keys: bfloat16 [1024, 8, 128], P(('seq', 'roll'), 'head')
- grad_prompt_values: bfloat16 [1024, 8, 128], P(('seq', 'roll'), 'head')
The draws below stay inside these ranges and needn't reach their ends.
Inputs may be any that keep to these rules, and one draw needn't show every extreme that they name: `lengths`: every rollout's length is at least 768, and one rollout of each draw has all 3072 positions live.
All inputs are finite; a program needn't handle non-finite values.
Results may differ from the reference program's by a relative error of at most 0.007.
Values may be sent and summed in bfloat16 or wider, within the bound.
A program may use at most 128 MiB of HBM per device.

```python
import jax
import jax.numpy as jnp
from jax import lax

HD = 128
QH = 64
KVH = 8
R = 3072
P_SIZE = 1024
ROLLS = 2


def draw_queries(key, part):
    key = jax.random.fold_in(key, 11)
    values = jnp.clip(1.5 * jax.random.normal(key, (ROLLS, R, QH, HD), jnp.float32), -7.0, 7.0)
    return values.astype(jnp.bfloat16)


def draw_prompt_keys(key, part):
    key = jax.random.fold_in(key, 23)
    values = jnp.clip(jax.random.normal(key, (P_SIZE, KVH, HD), jnp.float32), -4.5, 4.5)
    return values.astype(jnp.bfloat16)


def draw_lengths(key, part):
    key = jax.random.fold_in(key, 5)
    first_key, second_key = jax.random.split(key)
    full_member = jax.random.randint(first_key, (), 0, ROLLS)
    others = jax.random.randint(second_key, (ROLLS,), R // 4, R + 1)
    return jnp.where(jnp.arange(ROLLS) == full_member, R, others).astype(jnp.int32)


def level_of(key, dims, cuts, smallest, top_value):
    factor_of, own = 1.0, jax.random.fold_in(key, 6)
    for dim, parts in cuts:
        heights = jnp.exp(jax.random.uniform(jax.random.fold_in(own, dim), (parts,), jnp.float32, smallest / len(cuts), top_value / len(cuts)))
        factor_of = factor_of * jnp.repeat(heights, dims[dim] // parts).reshape([-1 if axis == dim else 1 for axis in range(len(dims))])
    return factor_of


def normal_values(rng, shape, spread, most, cuts=(), kind=jnp.bfloat16):
    values = jax.random.normal(rng, shape, jnp.float32) * spread
    if len(cuts) > 0:
        values = level_of(rng, shape, cuts, -0.22, 0.18) * values
    return jnp.clip(values, min=-most, max=most).astype(kind)


def setup_inputs(seed: int = 0) -> dict:
    keys = jax.random.split(jax.random.key(seed), 8)
    queries = draw_queries(jax.random.fold_in(keys[7], 71), 0)
    rollout_keys = normal_values(keys[1], (ROLLS, R, KVH, HD), 1.0, 6.0, ((0, 2), (1, 16), (2, 4)))
    rollout_values = normal_values(keys[2], (ROLLS, R, KVH, HD), 4.0, 24.0, ((0, 2), (1, 16), (2, 4)))
    prompt_keys = draw_prompt_keys(jax.random.fold_in(keys[7], 71), 0)
    prompt_values = normal_values(keys[4], (P_SIZE, KVH, HD), 4.0, 24.0, ((0, 32), (1, 4)))
    grad_out = normal_values(keys[5], (ROLLS, R, QH, HD), 4.0, 24.0, ((0, 2), (1, 16), (2, 4)))
    lengths = draw_lengths(jax.random.fold_in(keys[7], 71), 0)
    return {"queries": queries, "rollout_keys": rollout_keys, "rollout_values": rollout_values, "prompt_keys": prompt_keys, "prompt_values": prompt_values, "grad_out": grad_out, "lengths": lengths}


def rollout_pass(queries_one, keys_one, values_one, prompt_keys, prompt_values, cot_one, seq_length):
    total_rows = queries_one.shape[0]
    head_count = queries_one.shape[1]
    head_dim = queries_one.shape[2]
    group_count = keys_one.shape[1]
    per_group = head_count // group_count
    prompt_rows = prompt_keys.shape[0]
    all_keys = jnp.concatenate([prompt_keys, keys_one], axis=0).astype(jnp.float32)
    all_values = jnp.concatenate([prompt_values, values_one], axis=0).astype(jnp.float32)
    key_pos = jnp.concatenate([jnp.full((prompt_rows,), -1, jnp.int32), jnp.arange(total_rows, dtype=jnp.int32)])
    span_rows = min(256, total_rows)
    span_count = total_rows // span_rows
    score_scale = head_dim ** -0.5
    shaped_queries = queries_one.reshape(span_count, span_rows, group_count, per_group, head_dim)
    shaped_cot = cot_one.reshape(span_count, span_rows, group_count, per_group, head_dim)
    highest = lax.Precision.HIGHEST

    def one_span(carried, inputs):
        key_grads, value_grads = carried
        query_span, cot_span, span_index = inputs
        query_pos = span_index * span_rows + jnp.arange(span_rows, dtype=jnp.int32)
        query_float = query_span.astype(jnp.float32)
        scores = jnp.einsum('ngqd,kgd->gqnk', query_float, all_keys, precision=highest) * score_scale
        allowed = key_pos[None, :] <= query_pos[:, None]
        scores = jnp.where(allowed[None, None], scores, -jnp.inf)
        maxima = jnp.max(scores, -1)
        lifted = jnp.exp(scores - maxima[..., None])
        totals = jnp.sum(lifted, -1)
        lifted_low = lax.optimization_barrier(lifted.astype(jnp.bfloat16)).astype(jnp.float32)
        normalized = jnp.einsum('gqnk,kgd->gqnd', lifted_low, all_values, precision=highest) / totals[..., None]
        row_valid = query_pos < seq_length
        out_rows = jnp.where(row_valid[:, None, None, None], normalized.transpose(2, 0, 1, 3), 0.0)
        out_rows = out_rows.reshape(span_rows, head_count, head_dim).astype(jnp.bfloat16)
        log_total = maxima + jnp.log(totals)
        cot_live = jnp.where(row_valid[:, None, None, None], cot_span, jnp.zeros_like(cot_span)).astype(jnp.float32)
        offsets = jnp.sum(cot_live.transpose(1, 2, 0, 3) * normalized, -1)
        weights = jnp.exp(scores - log_total[..., None])
        grad_weights = jnp.einsum('ngqd,kgd->gqnk', cot_live, all_values, precision=highest)
        grad_scores = lax.optimization_barrier((weights * (grad_weights - offsets[..., None]) * score_scale).astype(jnp.bfloat16)).astype(jnp.float32)
        grad_query = jnp.einsum('gqnk,kgd->ngqd', grad_scores, all_keys, precision=highest)
        key_grads = key_grads + jnp.einsum('gqnk,ngqd->kgd', grad_scores, query_float, precision=highest)
        weights_low = lax.optimization_barrier(weights.astype(jnp.bfloat16)).astype(jnp.float32)
        value_grads = value_grads + jnp.einsum('gqnk,ngqd->kgd', weights_low, cot_live, precision=highest)
        grad_rows = grad_query.reshape(span_rows, head_count, head_dim).astype(jnp.bfloat16)
        return (key_grads, value_grads), (out_rows, grad_rows)

    zero_grads = jnp.zeros(all_keys.shape, jnp.float32)
    span_ids = jnp.arange(span_count, dtype=jnp.int32)
    (key_grads, value_grads), (out_spans, grad_spans) = lax.scan(one_span, (zero_grads, zero_grads), (shaped_queries, shaped_cot, span_ids))
    attention_one = out_spans.reshape(total_rows, head_count, head_dim)
    grad_one = grad_spans.reshape(total_rows, head_count, head_dim)
    return attention_one, grad_one, key_grads, value_grads


def reference(queries, rollout_keys, rollout_values, prompt_keys, prompt_values, grad_out, lengths):
    prompt_rows = prompt_keys.shape[0]
    results = [rollout_pass(queries[member], rollout_keys[member], rollout_values[member], prompt_keys, prompt_values, grad_out[member], lengths[member]) for member in range(ROLLS)]
    attention_out = jnp.stack([item[0] for item in results])
    grad_queries = jnp.stack([item[1] for item in results])
    grad_rollout_keys = jnp.stack([item[2][prompt_rows:] for item in results]).astype(jnp.bfloat16)
    grad_rollout_values = jnp.stack([item[3][prompt_rows:] for item in results]).astype(jnp.bfloat16)
    prompt_key_sum = results[0][2][:prompt_rows]
    prompt_value_sum = results[0][3][:prompt_rows]
    for item in results[1:]:
        prompt_key_sum = prompt_key_sum + item[2][:prompt_rows]
        prompt_value_sum = prompt_value_sum + item[3][:prompt_rows]
    return (attention_out, grad_queries, grad_rollout_keys, grad_rollout_values, prompt_key_sum.astype(jnp.bfloat16), prompt_value_sum.astype(jnp.bfloat16))
```

```python
import math

import jax
import jax.numpy as jnp
from jax import lax
from jax.experimental import pallas as pl
from jax.experimental.pallas import tpu as pltpu
from jax.sharding import PartitionSpec as P

f32, bf16 = jnp.float32, jnp.bfloat16
N = 16
BLK = 192
PRM = 1024
PB = 64
HD = 128
PG = 8
RB = BLK * PG
TILE = 4 * BLK
HALF = 2 * BLK
RC = RB // 2
SCALE = HD**-0.5
SCALE2 = SCALE * math.log2(math.e)
NEG = -1e30
MESH = pl.DeviceIdType.MESH

NN = (((1,), (0,)), ((), ()))
NT = (((1,), (1,)), ((), ()))
TN = (((0,), (0,)), ((), ()))


def dot(a, b, dims=NN):
    return lax.dot_general(a, b, dims, preferred_element_type=f32)


def kernel(
    q_in, do_in, kv_in, pk_in,
    out, dq, dkv_out, dp_out,
    q2, do2, kv, p64, acc, mx, tot, lse, off, o16, dk, dv, g16, recv, recvp, psum, prem,
    lsem, psem, kvs, kvr, pps, ppr, qsem, osem, gs, gr, gps, gpr, fsem,
):
    s = lax.axis_index("seq")
    r = lax.axis_index("roll")
    hs = s // 8
    partner = N - 1 - s
    high = jnp.maximum(s, partner)
    need = (high // 2) * 2 + 1

    barrier = pltpu.get_barrier_semaphore()
    for d in range(1, N):
        pl.semaphore_signal(barrier, inc=1, device_id={"seq": (s + d) % N}, device_id_type=MESH)
    pl.semaphore_signal(barrier, inc=1, device_id={"roll": 1 - r}, device_id_type=MESH)
    pl.semaphore_wait(barrier, N)

    def remote(src, dst, ssem, rsem, **where):
        return pltpu.make_async_remote_copy(
            src_ref=src, dst_ref=dst, send_sem=ssem, recv_sem=rsem,
            device_id=where, device_id_type=MESH,
        )

    rows32 = pl.ds(pl.multiple_of(r * 32, 32), 32)
    p_out = remote(pk_in, p64.at[:, :, rows32, :], psem.at[0], psem.at[1], roll=1 - r)
    p_out.start()
    p_own = pltpu.make_async_copy(pk_in, p64.at[:, :, rows32, :], psem.at[2])
    p_own.start()
    own_q = pltpu.make_async_copy(q_in.at[hs], q2.at[0], lsem.at[0])
    own_q.start()
    own_do = pltpu.make_async_copy(do_in.at[hs], do2.at[0], lsem.at[1])
    own_do.start()

    def kv_rows(j):
        return kv.at[:, pl.ds(pl.multiple_of(PRM + j * BLK, 64), BLK), :]

    def kv_copy(t):
        return remote(kv_in.at[t // 8], kv_rows(s), kvs.at[t], kvr.at[s], seq=t)

    def kv_wanted(t):
        return s <= (jnp.maximum(t, N - 1 - t) // 2) * 2 + 1

    own_kv = pltpu.make_async_copy(kv_in.at[hs], kv_rows(s), lsem.at[2])
    own_kv.start()

    def p_rows(j):
        return kv.at[:, pl.ds(pl.multiple_of(j * PB, PB), PB), :]

    def p_copy(t):
        return remote(p64.at[t // 8], p_rows(s), pps.at[t], ppr.at[s], seq=t)

    p_own.wait()
    p_out.wait_recv()
    own_p = pltpu.make_async_copy(p64.at[hs], p_rows(s), lsem.at[3])
    own_p.start()

    @pl.loop(1, N)
    def _(d):
        p_copy((s + d) % N).start()

    q_out = remote(q_in.at[1 - hs], q2.at[1], qsem.at[0], qsem.at[1], seq=partner)
    q_out.start()

    @pl.loop(1, N)
    def _(d):
        t = (s + d) % N

        @pl.when(kv_wanted(t))
        def _():
            kv_copy(t).start()

    do_out = remote(do_in.at[1 - hs], do2.at[1], qsem.at[2], qsem.at[3], seq=partner)
    do_out.start()

    def block_of(b):
        return jnp.where(b == 0, s, partner)

    def masked_scores(scores, k0, q0):
        key_pos = k0 - PRM + lax.broadcasted_iota(jnp.int32, scores.shape, 0)
        query_pos = q0 + lax.broadcasted_iota(jnp.int32, scores.shape, 1) // PG
        return jnp.where(key_pos <= query_pos, scores, NEG)

    def forward_tile(b, k0, size, masked):
        rows = pl.ds(pl.multiple_of(k0, 64), size)
        scores = dot(kv[0, rows, :], q2[b], NT) * SCALE2
        if masked:
            scores = masked_scores(scores, k0, block_of(b) * BLK)
        old = mx[b]
        new = jnp.maximum(old, jnp.max(scores, 0, keepdims=True))
        lifted = jnp.exp2(scores - new)
        shrink = jnp.exp2(old - new)
        mx[b] = new
        tot[b] = tot[b] * shrink + jnp.sum(lifted, 0, keepdims=True)
        acc[b] = acc[b] * shrink + dot(kv[1, rows, :], lifted.astype(bf16), TN)

    acc[...] = jnp.zeros_like(acc)
    mx[...] = jnp.full_like(mx, NEG)
    tot[...] = jnp.zeros_like(tot)
    own_q.wait()
    own_p.wait()

    @pl.loop(1, N)
    def _(d):
        t = (s + d) % N
        remote(p64.at[hs], p_rows(t), pps.at[t], ppr.at[t], seq=t).wait_recv()

    @pl.loop(0, 2)
    def _(b):
        @pl.when(b == 1)
        def _():
            q_out.wait_recv()

        forward_tile(b, 0, PRM, False)

    def wait_tile(tile):
        @pl.loop(0, 4)
        def _(i):
            j = tile * 4 + i

            @pl.when(j == s)
            def _():
                own_kv.wait()

            @pl.when((j != s) & (j <= need))
            def _():
                remote(kv_in.at[hs], kv_rows(j), kvs.at[j], kvr.at[j], seq=j).wait_recv()

    @pl.loop(0, 2)
    def _(b):
        blk = block_of(b)
        last = blk // 4

        @pl.loop(0, last)
        def _(tile):
            @pl.when((b == 0) | (tile > s // 4))
            def _():
                wait_tile(tile)

            forward_tile(b, PRM + tile * TILE, TILE, False)

        @pl.when((b == 0) | (last > s // 4))
        def _():
            wait_tile(last)

        @pl.loop(0, 1 + (blk % 4) // 2)
        def _(half):
            forward_tile(b, PRM + last * TILE + half * HALF, HALF, True)

    own_do.wait()
    do_out.wait_recv()

    @pl.loop(0, 2)
    def _(b):
        total = tot[b]
        normal = acc[b] / total
        lse[b] = mx[b] + jnp.log2(total)
        off[b] = jnp.sum(normal * do2[b].astype(f32).T, 0, keepdims=True)
        o16[b] = normal.T.astype(bf16)

    own_out = pltpu.make_async_copy(o16.at[0], out.at[hs], lsem.at[4])
    own_out.start()
    out_out = remote(o16.at[1], out.at[hs], osem.at[0], osem.at[1], seq=partner)
    out_out.start()

    acc[...] = jnp.zeros_like(acc)
    dk[...] = jnp.zeros_like(dk)
    dv[...] = jnp.zeros_like(dv)

    def backward_tile(b, k0, size, masked):
        rows = pl.ds(pl.multiple_of(k0, 64), size)

        for c in range(RB // RC):
            part = pl.ds(c * RC, RC)
            keys, values = kv[0, rows, :], kv[1, rows, :]
            queries, cot = q2[b, part, :], do2[b, part, :]
            scores = dot(keys, queries, NT) * SCALE2
            if masked:
                scores = masked_scores(scores, k0, block_of(b) * BLK + c * (RC // PG))
            weights = jnp.exp2(scores - lse[b, :, part])
            grads = (weights * (dot(values, cot, NT) - off[b, :, part])).astype(bf16)
            dv[rows, :] += dot(weights.astype(bf16), cot)
            dk[rows, :] += dot(grads, queries)
            acc[b, :, part] += dot(keys, grads, TN)

    def finish_rows(k0, size):
        rows = pl.ds(pl.multiple_of(k0, 64), size)
        g16[0, rows, :] = (dk[rows, :] * SCALE).astype(bf16)
        g16[1, rows, :] = dv[rows, :].astype(bf16)

    def grad_rows(j):
        return g16.at[:, pl.ds(pl.multiple_of(PRM + j * BLK, 64), BLK), :]

    def grad_copy(j):
        return remote(grad_rows(j), recv.at[s], gs.at[j], gr.at[s], seq=j)

    own_g = pltpu.make_async_copy(grad_rows(s), recv.at[s], lsem.at[5])

    def send_tile(tile):
        finish_rows(PRM + tile * TILE, TILE)

        @pl.loop(0, 4)
        def _(i):
            j = tile * 4 + i

            @pl.when(j == s)
            def _():
                own_g.start()

            @pl.when((j != s) & (j <= high))
            def _():
                grad_copy(j).start()

    def gp_rows(t):
        return g16.at[:, pl.ds(pl.multiple_of(t * PB, PB), PB), :]

    def gp_copy(t):
        return remote(gp_rows(t), recvp.at[s], gps.at[t], gpr.at[s], seq=t)

    own_gp = pltpu.make_async_copy(gp_rows(s), recvp.at[s], lsem.at[6])
    dq_out = remote(o16.at[3], dq.at[hs], osem.at[2], osem.at[3], seq=partner)

    @pl.loop(0, 2)
    def _(i):
        b = 1 - i
        blk = block_of(b)
        last = blk // 4
        backward_tile(b, 0, PRM, False)

        @pl.when(b == 0)
        def _():
            finish_rows(0, PRM)
            own_gp.start()

            @pl.loop(1, N)
            def _(d):
                gp_copy((s + d) % N).start()

        @pl.loop(0, last)
        def _(tile):
            backward_tile(b, PRM + tile * TILE, TILE, False)

            @pl.when(b == 0)
            def _():
                send_tile(tile)

        @pl.loop(0, 1 + (blk % 4) // 2)
        def _(half):
            backward_tile(b, PRM + last * TILE + half * HALF, HALF, True)

        o16[2 + b] = (acc[b] * SCALE).T.astype(bf16)

        @pl.when(b == 0)
        def _():
            send_tile(last)

        @pl.when(b == 1)
        def _():
            dq_out.start()

            @pl.loop(s // 4 + 1, partner // 4 + 1)
            def _(tile):
                send_tile(tile)

    own_dq = pltpu.make_async_copy(o16.at[2], dq.at[hs], lsem.at[7])
    own_dq.start()

    own_gp.wait()

    @pl.loop(1, N)
    def _(d):
        t = (s + d) % N
        remote(gp_rows(t), recvp.at[t], gps.at[t], gpr.at[t], seq=t).wait_recv()

    for h in range(2):
        total = recvp[8 * h].astype(f32)
        for i in range(1, 8):
            total = total + recvp[8 * h + i].astype(f32)
        psum[h] = total
    theirs = pl.ds(pl.multiple_of((1 - r) * 32, 32), 32)
    f_out = remote(psum.at[:, :, theirs, :], prem, fsem.at[0], fsem.at[1], roll=1 - r)
    f_out.start()

    own_g.wait()

    @pl.loop(1, N)
    def _(d):
        t = (s + d) % N

        @pl.when(s <= jnp.maximum(t, N - 1 - t))
        def _():
            remote(grad_rows(s), recv.at[t], gs.at[t], gr.at[t], seq=t).wait_recv()

    total0 = jnp.zeros(recv.shape[1:], f32)
    total1 = jnp.zeros(recv.shape[1:], f32)
    for i in range(8):
        total0 = total0 + jnp.where(s <= N - 1 - i, recv[i].astype(f32), 0.0)
        total1 = total1 + jnp.where(s <= 8 + i, recv[8 + i].astype(f32), 0.0)
    dkv_out[0] = total0.astype(bf16)
    dkv_out[1] = total1.astype(bf16)
    f_out.wait_recv()
    dp_out[...] = (psum[:, :, rows32, :] + prem[...]).astype(bf16)

    p_out.wait_send()
    q_out.wait_send()
    do_out.wait_send()
    out_out.wait()
    dq_out.wait()
    f_out.wait_send()
    own_out.wait()
    own_dq.wait()

    @pl.loop(1, N)
    def _(d):
        t = (s + d) % N
        p_copy(t).wait_send()
        gp_copy(t).wait_send()

        @pl.when(kv_wanted(t))
        def _():
            kv_copy(t).wait_send()

        @pl.when(t <= high)
        def _():
            grad_copy(t).wait_send()


def attention(q_rows, do_rows, kv_rows, prompt_rows):
    any_spec = pl.BlockSpec(memory_space=pl.ANY)
    vmem = pl.BlockSpec(memory_space=pltpu.VMEM)
    dma = pltpu.SemaphoreType.DMA
    return pl.pallas_call(
        kernel,
        out_shape=[
            jax.ShapeDtypeStruct((2, RB, HD), bf16),
            jax.ShapeDtypeStruct((2, RB, HD), bf16),
            jax.ShapeDtypeStruct((2, 2, BLK, HD), bf16),
            jax.ShapeDtypeStruct((2, 2, 32, HD), bf16),
        ],
        in_specs=[any_spec] * 4,
        out_specs=[any_spec, any_spec, vmem, vmem],
        scratch_shapes=[
            pltpu.VMEM((2, RB, HD), bf16),
            pltpu.VMEM((2, RB, HD), bf16),
            pltpu.VMEM((2, PRM + N * BLK, HD), bf16),
            pltpu.VMEM((2, 2, PB, HD), bf16),
            pltpu.VMEM((2, HD, RB), f32),
            pltpu.VMEM((2, 1, RB), f32),
            pltpu.VMEM((2, 1, RB), f32),
            pltpu.VMEM((2, 1, RB), f32),
            pltpu.VMEM((2, 1, RB), f32),
            pltpu.VMEM((4, RB, HD), bf16),
            pltpu.VMEM((PRM + N * BLK, HD), f32),
            pltpu.VMEM((PRM + N * BLK, HD), f32),
            pltpu.VMEM((2, PRM + N * BLK, HD), bf16),
            pltpu.VMEM((N, 2, BLK, HD), bf16),
            pltpu.VMEM((N, 2, PB, HD), bf16),
            pltpu.VMEM((2, 2, PB, HD), f32),
            pltpu.VMEM((2, 2, 32, HD), f32),
            dma((8,)),
            dma((3,)),
            dma((N,)),
            dma((N,)),
            dma((N,)),
            dma((N,)),
            dma((4,)),
            dma((4,)),
            dma((N,)),
            dma((N,)),
            dma((N,)),
            dma((N,)),
            dma((2,)),
        ],
        compiler_params=pltpu.CompilerParams(
            collective_id=0, has_side_effects=True, vmem_limit_bytes=58 * 2**20
        ),
    )(q_rows, do_rows, kv_rows, prompt_rows)


def local(queries, rollout_keys, rollout_values, prompt_keys, prompt_values, grad_out, lengths):
    first_row = lax.axis_index("seq") * BLK
    valid = ((first_row + jnp.arange(BLK, dtype=jnp.int32)) < lengths[0])[None, :, None, None]

    def by_group(rows):
        return rows.reshape(BLK, 2, PG, HD).transpose(1, 0, 2, 3)

    def merged(rows):
        return rows.transpose(1, 0, 2, 3).reshape(1, BLK, 2 * PG, HD)

    q_rows = by_group(queries[0]).reshape(2, RB, HD)
    cot = by_group(grad_out[0])
    do_rows = jnp.where(valid, cot, jnp.zeros_like(cot)).reshape(2, RB, HD)
    kv_rows = jnp.stack([rollout_keys[0], rollout_values[0]]).transpose(2, 0, 1, 3)
    prompt_rows = jnp.stack([prompt_keys, prompt_values]).transpose(2, 0, 1, 3)
    out, dq, dkv, dprompt = attention(q_rows, do_rows, kv_rows, prompt_rows)
    out = out.reshape(2, BLK, PG, HD)
    out = jnp.where(valid, out, jnp.zeros_like(out))
    dkv = dkv.transpose(1, 2, 0, 3)
    dprompt = dprompt.transpose(1, 2, 0, 3)
    return (
        merged(out),
        merged(dq.reshape(2, BLK, PG, HD)),
        dkv[0][None],
        dkv[1][None],
        dprompt[0],
        dprompt[1],
    )


def solution(mesh):
    rows = P("roll", "seq", "head", None)
    prompt = P(("seq", "roll"), "head", None)
    return jax.shard_map(
        local,
        mesh=mesh,
        in_specs=(rows, rows, rows, prompt, prompt, rows, P("roll")),
        out_specs=(rows, rows, rows, rows, prompt, prompt),
        check_vma=False,
    )
```

```python
import math

import jax
import jax.numpy as jnp
from jax import lax
from jax.experimental import pallas as pl
from jax.experimental.pallas import tpu as pltpu
from jax.sharding import PartitionSpec as P

f32, bf16 = jnp.float32, jnp.bfloat16
N = 16
BLK = 192
PRM = 1024
PB = 64
HD = 128
PG = 8
RB = BLK * PG
TILE = 4 * BLK
HALF = 2 * BLK
RC = RB // 2
SCALE = HD**-0.5
SCALE2 = SCALE * math.log2(math.e)
NEG = -1e30
MESH = pl.DeviceIdType.MESH

NN = (((1,), (0,)), ((), ()))
NT = (((1,), (1,)), ((), ()))
TN = (((0,), (0,)), ((), ()))


def dot(a, b, dims=NN):
    return lax.dot_general(a, b, dims, preferred_element_type=f32)


def kernel(
    q_in, do_in, kv_in, pk_in,
    out, dq, dkv_out, dp_out,
    q2, do2, kv, p64, acc, mx, tot, lse, off, o16, dk, dv, g16,
    zr, zrp, gx, gxp, xr, xrp, psum, prem,
    lsem, psem, kvxs, kvxr, kvzs, kvzr, ppxs, ppxr, ppzs, ppzr, qsem, osem,
    gzs, gzr, gpzs, gpzr, gxs, gxr, gpxs, gpxr, fsem,
):
    s = lax.axis_index("seq")
    r = lax.axis_index("roll")
    x, z = s // 4, s % 4
    hs = x // 2
    top = jnp.maximum(x, 3 - x)
    partner = 4 * (3 - x) + z

    barrier = pltpu.get_barrier_semaphore()
    for d in range(1, 4):
        pl.semaphore_signal(barrier, inc=1, device_id={"seq": (x + d) % 4 * 4 + z}, device_id_type=MESH)
        pl.semaphore_signal(barrier, inc=1, device_id={"seq": 4 * x + (z + d) % 4}, device_id_type=MESH)
    pl.semaphore_signal(barrier, inc=1, device_id={"roll": 1 - r}, device_id_type=MESH)

    def remote(src, dst, ssem, rsem, **where):
        return pltpu.make_async_remote_copy(
            src_ref=src, dst_ref=dst, send_sem=ssem, recv_sem=rsem,
            device_id=where, device_id_type=MESH,
        )

    def kv_rows(j):
        return kv.at[:, pl.ds(pl.multiple_of(PRM + j * BLK, 64), BLK), :]

    def p_rows(zz, xx):
        return kv.at[:, pl.ds(pl.multiple_of((zz * 4 + xx) * PB, PB), PB), :]

    def p_column(zz):
        return kv.at[:, pl.ds(pl.multiple_of(zz * 4 * PB, 4 * PB), 4 * PB), :]

    rows32 = pl.ds(pl.multiple_of(r * 32, 32), 32)
    p_own = pltpu.make_async_copy(pk_in, p64.at[:, :, rows32, :], psem.at[2])
    p_own.start()
    own_kv = pltpu.make_async_copy(kv_in.at[hs], kv_rows(s), lsem.at[2])
    own_kv.start()
    own_q = pltpu.make_async_copy(q_in.at[hs], q2.at[0], lsem.at[0])
    own_q.start()
    own_do = pltpu.make_async_copy(do_in.at[hs], do2.at[0], lsem.at[1])
    own_do.start()
    pl.semaphore_wait(barrier, 7)
    p_out = remote(pk_in, p64.at[:, :, rows32, :], psem.at[0], psem.at[1], roll=1 - r)
    p_out.start()

    def kvx_copy(xx):
        return remote(kv_in.at[xx // 2], kv_rows(s), kvxs.at[xx], kvxr.at[x], seq=4 * xx + z)

    def px_copy(xx):
        return remote(p64.at[xx // 2], p_rows(z, x), ppxs.at[xx], ppxr.at[x], seq=4 * xx + z)

    def pz_copy(zz):
        return remote(p_column(z), p_column(z), ppzs.at[zz], ppzr.at[z], seq=4 * x + zz)

    def kvz_copy(zz, tile):
        rows = kv_rows(4 * tile + z)
        return remote(rows, rows, kvzs.at[zz, tile], kvzr.at[z, tile], seq=4 * x + zz)

    def sees(xx):
        return x <= jnp.maximum(xx, 3 - xx)

    @pl.loop(1, 4)
    def _(d):
        xx = (x + d) % 4

        @pl.when(sees(xx))
        def _():
            kvx_copy(xx).start()

    p_own.wait()
    p_out.wait_recv()
    own_p = pltpu.make_async_copy(p64.at[hs], p_rows(z, x), lsem.at[3])
    own_p.start()

    @pl.loop(1, 4)
    def _(d):
        px_copy((x + d) % 4).start()

    q_out = remote(q_in.at[1 - hs], q2.at[1], qsem.at[0], qsem.at[1], seq=partner)
    q_out.start()
    acc[...] = jnp.zeros_like(acc)
    mx[...] = jnp.full_like(mx, NEG)
    tot[...] = jnp.zeros_like(tot)
    own_p.wait()

    @pl.loop(1, 4)
    def _(d):
        xx = (x + d) % 4
        remote(p64.at[hs], p_rows(z, xx), ppxs.at[xx], ppxr.at[xx], seq=4 * xx + z).wait_recv()

    @pl.loop(1, 4)
    def _(d):
        pz_copy((z + d) % 4).start()

    own_kv.wait()

    @pl.loop(0, top + 1)
    def _(tile):
        @pl.when(tile != x)
        def _():
            remote(kv_in.at[hs], kv_rows(4 * tile + z), kvxs.at[tile], kvxr.at[tile], seq=4 * tile + z).wait_recv()

        @pl.loop(1, 4)
        def _(d):
            kvz_copy((z + d) % 4, tile).start()

    do_out = remote(do_in.at[1 - hs], do2.at[1], qsem.at[2], qsem.at[3], seq=partner)
    do_out.start()

    def block_of(b):
        return jnp.where(b == 0, s, partner)

    def masked_scores(scores, k0, q0):
        key_pos = k0 - PRM + lax.broadcasted_iota(jnp.int32, scores.shape, 0)
        query_pos = q0 + lax.broadcasted_iota(jnp.int32, scores.shape, 1) // PG
        return jnp.where(key_pos <= query_pos, scores, NEG)

    def forward_tile(b, k0, size, masked):
        rows = pl.ds(pl.multiple_of(k0, 64), size)
        scores = dot(kv[0, rows, :], q2[b], NT) * SCALE2
        if masked:
            scores = masked_scores(scores, k0, block_of(b) * BLK)
        old = mx[b]
        new = jnp.maximum(old, jnp.max(scores, 0, keepdims=True))
        lifted = jnp.exp2(scores - new)
        shrink = jnp.exp2(old - new)
        mx[b] = new
        tot[b] = tot[b] * shrink + jnp.sum(lifted, 0, keepdims=True)
        acc[b] = acc[b] * shrink + dot(kv[1, rows, :], lifted.astype(bf16), TN)

    own_q.wait()

    @pl.loop(1, 4)
    def _(d):
        zz = (z + d) % 4
        remote(p_column(zz), p_column(zz), ppzs.at[zz], ppzr.at[zz], seq=4 * x + zz).wait_recv()

    def wait_tile(tile):
        @pl.loop(1, 4)
        def _(d):
            zz = (z + d) % 4
            rows = kv_rows(4 * tile + zz)
            remote(rows, rows, kvzs.at[zz, tile], kvzr.at[zz, tile], seq=4 * x + zz).wait_recv()

    @pl.loop(0, 2)
    def _(b):
        blk = block_of(b)
        last = blk // 4

        @pl.when(b == 1)
        def _():
            q_out.wait_recv()

        forward_tile(b, 0, PRM, False)

        @pl.loop(0, last)
        def _(tile):
            @pl.when((b == 0) | (tile > x))
            def _():
                wait_tile(tile)

            forward_tile(b, PRM + tile * TILE, TILE, False)

        @pl.when((b == 0) | (last > x))
        def _():
            wait_tile(last)

        @pl.loop(0, 1 + z // 2)
        def _(half):
            forward_tile(b, PRM + last * TILE + half * HALF, HALF, True)

    own_do.wait()
    do_out.wait_recv()

    @pl.loop(0, 2)
    def _(b):
        total = tot[b]
        normal = acc[b] / total
        lse[b] = mx[b] + jnp.log2(total)
        off[b] = jnp.sum(normal * do2[b].astype(f32).T, 0, keepdims=True)
        o16[b] = normal.T.astype(bf16)

    own_out = pltpu.make_async_copy(o16.at[0], out.at[hs], lsem.at[4])
    own_out.start()
    out_out = remote(o16.at[1], out.at[hs], osem.at[0], osem.at[1], seq=partner)
    out_out.start()

    acc[...] = jnp.zeros_like(acc)
    dk[...] = jnp.zeros_like(dk)
    dv[...] = jnp.zeros_like(dv)

    def backward_tile(b, k0, size, masked):
        rows = pl.ds(pl.multiple_of(k0, 64), size)

        for c in range(RB // RC):
            part = pl.ds(c * RC, RC)
            keys, values = kv[0, rows, :], kv[1, rows, :]
            queries, cot = q2[b, part, :], do2[b, part, :]
            scores = dot(keys, queries, NT) * SCALE2
            if masked:
                scores = masked_scores(scores, k0, block_of(b) * BLK + c * (RC // PG))
            weights = jnp.exp2(scores - lse[b, :, part])
            grads = (weights * (dot(values, cot, NT) - off[b, :, part])).astype(bf16)
            dv[rows, :] += dot(weights.astype(bf16), cot)
            dk[rows, :] += dot(grads, queries)
            acc[b, :, part] += dot(keys, grads, TN)

    def finish_rows(k0, size):
        rows = pl.ds(pl.multiple_of(k0, 64), size)
        g16[0, rows, :] = (dk[rows, :] * SCALE).astype(bf16)
        g16[1, rows, :] = dv[rows, :].astype(bf16)

    def grad_rows(j):
        return pl.ds(pl.multiple_of(PRM + j * BLK, 64), BLK)

    def gz_copy(zz, tile):
        rows = grad_rows(4 * tile + zz)
        return remote(g16.at[:, rows, :], zr.at[z, tile], gzs.at[zz, tile], gzr.at[z, tile], seq=4 * x + zz)

    def gx_copy(tile):
        return remote(gx.at[tile], xr.at[x], gxs.at[tile], gxr.at[x], seq=4 * tile + z)

    def send_tile(tile):
        finish_rows(PRM + tile * TILE, TILE)

        @pl.loop(1, 4)
        def _(d):
            gz_copy((z + d) % 4, tile).start()

    def pass_tile(tile):
        rows = grad_rows(4 * tile + z)
        total = g16[:, rows, :].astype(f32)
        for d in range(1, 4):
            zz = (z + d) % 4
            remote(g16.at[:, rows, :], zr.at[zz, tile], gzs.at[zz, tile], gzr.at[zz, tile], seq=4 * x + zz).wait_recv()
            total = total + zr[zz, tile].astype(f32)

        @pl.when(tile == x)
        def _():
            xr[x] = total.astype(bf16)

        @pl.when(tile != x)
        def _():
            gx[tile] = total.astype(bf16)
            gx_copy(tile).start()

    def column(zz):
        return pl.ds(pl.multiple_of(zz * 4 * PB, 4 * PB), 4 * PB)

    def gpz_copy(zz):
        return remote(g16.at[:, column(zz), :], zrp.at[z], gpzs.at[zz], gpzr.at[z], seq=4 * x + zz)

    def gpx_copy(xx):
        rows = pl.ds(pl.multiple_of(xx * PB, PB), PB)
        return remote(gxp.at[:, rows, :], xrp.at[x], gpxs.at[xx], gpxr.at[x], seq=4 * xx + z)

    def send_prompt():
        finish_rows(0, PRM)

        @pl.loop(1, 4)
        def _(d):
            gpz_copy((z + d) % 4).start()

    def pass_prompt():
        total = g16[:, column(z), :].astype(f32)
        for d in range(1, 4):
            zz = (z + d) % 4
            remote(g16.at[:, column(z), :], zrp.at[zz], gpzs.at[zz], gpzr.at[zz], seq=4 * x + zz).wait_recv()
            total = total + zrp[zz].astype(f32)
        gxp[...] = total.astype(bf16)

        @pl.loop(1, 4)
        def _(d):
            gpx_copy((x + d) % 4).start()

        xrp[x] = gxp[:, pl.ds(pl.multiple_of(x * PB, PB), PB), :]

    dq_out = remote(o16.at[3], dq.at[hs], osem.at[2], osem.at[3], seq=partner)

    @pl.loop(0, 2)
    def _(i):
        b = 1 - i
        last = jnp.where(b == 0, x, 3 - x)
        backward_tile(b, 0, PRM, False)

        @pl.when(b == 0)
        def _():
            send_prompt()

            @pl.loop(x + 1, 4 - x)
            def _(tile):
                pass_tile(tile)

        @pl.loop(0, last)
        def _(tile):
            backward_tile(b, PRM + tile * TILE, TILE, False)

            @pl.when(b == 0)
            def _():
                send_tile(tile)

                @pl.when(tile == 0)
                def _():
                    pass_prompt()

                @pl.when(tile > 0)
                def _():
                    pass_tile(tile - 1)

        @pl.loop(0, 1 + z // 2)
        def _(half):
            backward_tile(b, PRM + last * TILE + half * HALF, HALF, True)

        @pl.when(b == 0)
        def _():
            send_tile(last)

        o16[2 + b] = (acc[b] * SCALE).T.astype(bf16)

        @pl.when(b == 1)
        def _():
            dq_out.start()

            @pl.loop(x + 1, 4 - x)
            def _(tile):
                send_tile(tile)

    own_dq = pltpu.make_async_copy(o16.at[2], dq.at[hs], lsem.at[7])
    own_dq.start()

    @pl.when(x == 0)
    def _():
        pass_prompt()

    @pl.when(x > 0)
    def _():
        pass_tile(x - 1)

    pass_tile(x)

    @pl.loop(1, 4)
    def _(d):
        xx = (x + d) % 4
        remote(gxp.at[:, pl.ds(0, PB), :], xrp.at[xx], gpxs.at[xx], gpxr.at[xx], seq=4 * xx + z).wait_recv()

    for h in range(2):
        psum[h] = xrp[2 * h].astype(f32) + xrp[2 * h + 1].astype(f32)
    theirs = pl.ds(pl.multiple_of((1 - r) * 32, 32), 32)
    f_out = remote(psum.at[:, :, theirs, :], prem, fsem.at[0], fsem.at[1], roll=1 - r)
    f_out.start()

    @pl.loop(1, 4)
    def _(d):
        xx = (x + d) % 4

        @pl.when(sees(xx))
        def _():
            remote(gx.at[xx], xr.at[xx], gxs.at[xx], gxr.at[xx], seq=4 * xx + z).wait_recv()

    for h in range(2):
        total = jnp.zeros(xr.shape[1:], f32)
        for xx in (2 * h, 2 * h + 1):
            total = total + jnp.where(x <= max(xx, 3 - xx), xr[xx].astype(f32), 0.0)
        dkv_out[h] = total.astype(bf16)
    f_out.wait_recv()
    dp_out[...] = (psum[:, :, rows32, :] + prem[...]).astype(bf16)

    p_out.wait_send()
    q_out.wait_send()
    do_out.wait_send()
    out_out.wait()
    dq_out.wait()
    f_out.wait_send()
    own_out.wait()
    own_dq.wait()

    @pl.loop(1, 4)
    def _(d):
        xx = (x + d) % 4
        zz = (z + d) % 4
        px_copy(xx).wait_send()
        pz_copy(zz).wait_send()
        gpz_copy(zz).wait_send()
        gpx_copy(xx).wait_send()

        @pl.when(sees(xx))
        def _():
            kvx_copy(xx).wait_send()

        @pl.when(xx <= top)
        def _():
            gx_copy(xx).wait_send()

        @pl.loop(0, top + 1)
        def _(tile):
            kvz_copy(zz, tile).wait_send()
            gz_copy(zz, tile).wait_send()


def attention(q_rows, do_rows, kv_rows, prompt_rows):
    any_spec = pl.BlockSpec(memory_space=pl.ANY)
    vmem = pl.BlockSpec(memory_space=pltpu.VMEM)
    dma = pltpu.SemaphoreType.DMA
    return pl.pallas_call(
        kernel,
        out_shape=[
            jax.ShapeDtypeStruct((2, RB, HD), bf16),
            jax.ShapeDtypeStruct((2, RB, HD), bf16),
            jax.ShapeDtypeStruct((2, 2, BLK, HD), bf16),
            jax.ShapeDtypeStruct((2, 2, 32, HD), bf16),
        ],
        in_specs=[any_spec] * 4,
        out_specs=[any_spec, any_spec, vmem, vmem],
        scratch_shapes=[
            pltpu.VMEM((2, RB, HD), bf16),
            pltpu.VMEM((2, RB, HD), bf16),
            pltpu.VMEM((2, PRM + N * BLK, HD), bf16),
            pltpu.VMEM((2, 2, PB, HD), bf16),
            pltpu.VMEM((2, HD, RB), f32),
            pltpu.VMEM((2, 1, RB), f32),
            pltpu.VMEM((2, 1, RB), f32),
            pltpu.VMEM((2, 1, RB), f32),
            pltpu.VMEM((2, 1, RB), f32),
            pltpu.VMEM((4, RB, HD), bf16),
            pltpu.VMEM((PRM + N * BLK, HD), f32),
            pltpu.VMEM((PRM + N * BLK, HD), f32),
            pltpu.VMEM((2, PRM + N * BLK, HD), bf16),
            pltpu.VMEM((4, 4, 2, BLK, HD), bf16),
            pltpu.VMEM((4, 2, 4 * PB, HD), bf16),
            pltpu.VMEM((4, 2, BLK, HD), bf16),
            pltpu.VMEM((2, 4 * PB, HD), bf16),
            pltpu.VMEM((4, 2, BLK, HD), bf16),
            pltpu.VMEM((4, 2, PB, HD), bf16),
            pltpu.VMEM((2, 2, PB, HD), f32),
            pltpu.VMEM((2, 2, 32, HD), f32),
            dma((8,)),
            dma((3,)),
            dma((4,)),
            dma((4,)),
            dma((4, 4)),
            dma((4, 4)),
            dma((4,)),
            dma((4,)),
            dma((4,)),
            dma((4,)),
            dma((4,)),
            dma((4,)),
            dma((4, 4)),
            dma((4, 4)),
            dma((4,)),
            dma((4,)),
            dma((4,)),
            dma((4,)),
            dma((4,)),
            dma((4,)),
            dma((2,)),
        ],
        compiler_params=pltpu.CompilerParams(
            collective_id=0, has_side_effects=True, vmem_limit_bytes=58 * 2**20
        ),
    )(q_rows, do_rows, kv_rows, prompt_rows)


def local(queries, rollout_keys, rollout_values, prompt_keys, prompt_values, grad_out, lengths):
    first_row = lax.axis_index("seq") * BLK
    valid = ((first_row + jnp.arange(BLK, dtype=jnp.int32)) < lengths[0])[None, :, None, None]

    def by_group(rows):
        return rows.reshape(BLK, 2, PG, HD).transpose(1, 0, 2, 3)

    def merged(rows):
        return rows.transpose(1, 0, 2, 3).reshape(1, BLK, 2 * PG, HD)

    q_rows = by_group(queries[0]).reshape(2, RB, HD)
    cot = by_group(grad_out[0])
    do_rows = jnp.where(valid, cot, jnp.zeros_like(cot)).reshape(2, RB, HD)
    kv_rows = jnp.stack([rollout_keys[0], rollout_values[0]]).transpose(2, 0, 1, 3)
    prompt_rows = jnp.stack([prompt_keys, prompt_values]).transpose(2, 0, 1, 3)
    out, dq, dkv, dprompt = attention(q_rows, do_rows, kv_rows, prompt_rows)
    out = out.reshape(2, BLK, PG, HD)
    out = jnp.where(valid, out, jnp.zeros_like(out))
    dkv = dkv.transpose(1, 2, 0, 3)
    dprompt = dprompt.transpose(1, 2, 0, 3)
    return (
        merged(out),
        merged(dq.reshape(2, BLK, PG, HD)),
        dkv[0][None],
        dkv[1][None],
        dprompt[0],
        dprompt[1],
    )


def solution(mesh):
    rows = P("roll", "seq", "head", None)
    prompt = P(("seq", "roll"), "head", None)
    return jax.shard_map(
        local,
        mesh=mesh,
        in_specs=(rows, rows, rows, prompt, prompt, rows, P("roll")),
        out_specs=(rows, rows, rows, rows, prompt, prompt),
        check_vma=False,
    )
```

```python
import math

import jax
import jax.numpy as jnp
from jax import lax
from jax.experimental import pallas as pl
from jax.experimental.pallas import tpu as pltpu
from jax.sharding import PartitionSpec as P

f32, bf16 = jnp.float32, jnp.bfloat16
N = 16
BLK = 192
PRM = 1024
HD = 128
PG = 8
RB = BLK * PG
TILE = 4 * BLK
HALF = 2 * BLK
RC = RB // 2
SCALE = HD**-0.5
SCALE2 = SCALE * math.log2(math.e)
NEG = -1e30
MESH = pl.DeviceIdType.MESH

NN = (((1,), (0,)), ((), ()))
NT = (((1,), (1,)), ((), ()))
TN = (((0,), (0,)), ((), ()))


def dot(a, b, dims=NN):
    return lax.dot_general(a, b, dims, preferred_element_type=f32)


def kernel(
    q_in, do_in, kv_in, pk_in,
    out, dq, dkv_out, dp_out,
    q2, do2, kv, acc, mx, tot, lse, off, o16, dk, dv, g16,
    zr, yrp, gyp, zrp, gx, gxp, xr, xrp,
    lsem, kvxs, kvxr, kvzs, kvzr, ppxs, ppxr, ppzs, ppzr, ppys, ppyr, qsem, osem,
    gzs, gzr, gpys, gpzs, gpzr, gxs, gxr, gpxs, gpxr,
):
    s = lax.axis_index("seq")
    r = lax.axis_index("roll")
    x, z = s // 4, s % 4
    hs = x // 2
    top = jnp.maximum(x, 3 - x)
    partner = 4 * (3 - x) + z

    barrier = pltpu.get_barrier_semaphore()
    for d in range(1, 4):
        pl.semaphore_signal(barrier, inc=1, device_id={"seq": (x + d) % 4 * 4 + z}, device_id_type=MESH)
        pl.semaphore_signal(barrier, inc=1, device_id={"seq": 4 * x + (z + d) % 4}, device_id_type=MESH)
    pl.semaphore_signal(barrier, inc=1, device_id={"roll": 1 - r}, device_id_type=MESH)

    def remote(src, dst, ssem, rsem, **where):
        return pltpu.make_async_remote_copy(
            src_ref=src, dst_ref=dst, send_sem=ssem, recv_sem=rsem,
            device_id=where, device_id_type=MESH,
        )

    def kv_rows(j):
        return kv.at[:, pl.ds(pl.multiple_of(PRM + j * BLK, 64), BLK), :]

    def p_rows(xx):
        return kv.at[:, pl.ds(pl.multiple_of(r * 512 + z * 128 + xx * 32, 32), 32), :]

    def p_column(rr, zz):
        return kv.at[:, pl.ds(pl.multiple_of(rr * 512 + zz * 128, 128), 128), :]

    own_p = pltpu.make_async_copy(pk_in.at[hs], p_rows(x), lsem.at[3])
    own_p.start()
    own_kv = pltpu.make_async_copy(kv_in.at[hs], kv_rows(s), lsem.at[2])
    own_kv.start()
    own_q = pltpu.make_async_copy(q_in.at[hs], q2.at[0], lsem.at[0])
    own_q.start()
    own_do = pltpu.make_async_copy(do_in.at[hs], do2.at[0], lsem.at[1])
    own_do.start()
    pl.semaphore_wait(barrier, 7)

    def kvx_copy(xx):
        return remote(kv_in.at[xx // 2], kv_rows(s), kvxs.at[xx], kvxr.at[x], seq=4 * xx + z)

    def px_copy(xx):
        return remote(pk_in.at[xx // 2], p_rows(x), ppxs.at[xx], ppxr.at[x], seq=4 * xx + z)

    def pz_copy(zz):
        return remote(p_column(r, z), p_column(r, z), ppzs.at[zz], ppzr.at[z], seq=4 * x + zz)

    def py_copy(zz):
        return remote(p_column(r, zz), p_column(r, zz), ppys.at[zz], ppyr.at[zz], roll=1 - r)

    def kvz_copy(zz, tile):
        rows = kv_rows(4 * tile + z)
        return remote(rows, rows, kvzs.at[zz, tile], kvzr.at[z, tile], seq=4 * x + zz)

    def sees(xx):
        return x <= jnp.maximum(xx, 3 - xx)

    @pl.loop(1, 4)
    def _(d):
        px_copy((x + d) % 4).start()

    @pl.loop(1, 4)
    def _(d):
        xx = (x + d) % 4

        @pl.when(sees(xx))
        def _():
            kvx_copy(xx).start()

    q_out = remote(q_in.at[1 - hs], q2.at[1], qsem.at[0], qsem.at[1], seq=partner)
    q_out.start()
    acc[...] = jnp.zeros_like(acc)
    mx[...] = jnp.full_like(mx, NEG)
    tot[...] = jnp.zeros_like(tot)
    own_p.wait()

    @pl.loop(1, 4)
    def _(d):
        xx = (x + d) % 4
        remote(pk_in.at[hs], p_rows(xx), ppxs.at[xx], ppxr.at[xx], seq=4 * xx + z).wait_recv()

    @pl.loop(1, 4)
    def _(d):
        pz_copy((z + d) % 4).start()

    py_copy(z).start()
    own_kv.wait()

    @pl.loop(0, top + 1)
    def _(tile):
        @pl.when(tile != x)
        def _():
            remote(kv_in.at[hs], kv_rows(4 * tile + z), kvxs.at[tile], kvxr.at[tile], seq=4 * tile + z).wait_recv()

        @pl.loop(1, 4)
        def _(d):
            kvz_copy((z + d) % 4, tile).start()

    @pl.loop(1, 4)
    def _(d):
        zz = (z + d) % 4
        remote(p_column(r, zz), p_column(r, zz), ppzs.at[zz], ppzr.at[zz], seq=4 * x + zz).wait_recv()
        py_copy(zz).start()

    do_out = remote(do_in.at[1 - hs], do2.at[1], qsem.at[2], qsem.at[3], seq=partner)
    do_out.start()

    def block_of(b):
        return jnp.where(b == 0, s, partner)

    def masked_scores(scores, k0, q0):
        key_pos = k0 - PRM + lax.broadcasted_iota(jnp.int32, scores.shape, 0)
        query_pos = q0 + lax.broadcasted_iota(jnp.int32, scores.shape, 1) // PG
        return jnp.where(key_pos <= query_pos, scores, NEG)

    def forward_tile(b, k0, size, masked):
        rows = pl.ds(pl.multiple_of(k0, 64), size)
        scores = dot(kv[0, rows, :], q2[b], NT) * SCALE2
        if masked:
            scores = masked_scores(scores, k0, block_of(b) * BLK)
        old = mx[b]
        new = jnp.maximum(old, jnp.max(scores, 0, keepdims=True))
        lifted = jnp.exp2(scores - new)
        shrink = jnp.exp2(old - new)
        mx[b] = new
        tot[b] = tot[b] * shrink + jnp.sum(lifted, 0, keepdims=True)
        acc[b] = acc[b] * shrink + dot(kv[1, rows, :], lifted.astype(bf16), TN)

    own_q.wait()

    def wait_tile(tile):
        @pl.loop(1, 4)
        def _(d):
            zz = (z + d) % 4
            rows = kv_rows(4 * tile + zz)
            remote(rows, rows, kvzs.at[zz, tile], kvzr.at[zz, tile], seq=4 * x + zz).wait_recv()

    @pl.loop(0, 2)
    def _(b):
        blk = block_of(b)
        last = blk // 4

        @pl.when(b == 1)
        def _():
            q_out.wait_recv()

        @pl.loop(0, 2)
        def _(i):
            half = (r + i) % 2

            @pl.when((b == 0) & (i == 1))
            def _():
                @pl.loop(0, 4)
                def _(zz):
                    remote(p_column(half, zz), p_column(half, zz), ppys.at[zz], ppyr.at[zz], roll=half).wait_recv()

            forward_tile(b, half * 512, 512, False)

        @pl.loop(0, last)
        def _(tile):
            @pl.when((b == 0) | (tile > x))
            def _():
                wait_tile(tile)

            forward_tile(b, PRM + tile * TILE, TILE, False)

        @pl.when((b == 0) | (last > x))
        def _():
            wait_tile(last)

        @pl.loop(0, 1 + z // 2)
        def _(half):
            forward_tile(b, PRM + last * TILE + half * HALF, HALF, True)

    own_do.wait()
    do_out.wait_recv()

    @pl.loop(0, 2)
    def _(b):
        total = tot[b]
        normal = acc[b] / total
        lse[b] = mx[b] + jnp.log2(total)
        off[b] = jnp.sum(normal * do2[b].astype(f32).T, 0, keepdims=True)
        o16[b] = normal.T.astype(bf16)

    own_out = pltpu.make_async_copy(o16.at[0], out.at[hs], lsem.at[4])
    own_out.start()
    out_out = remote(o16.at[1], out.at[hs], osem.at[0], osem.at[1], seq=partner)
    out_out.start()

    acc[...] = jnp.zeros_like(acc)
    dk[...] = jnp.zeros_like(dk)
    dv[...] = jnp.zeros_like(dv)

    def backward_tile(b, k0, size, masked):
        rows = pl.ds(pl.multiple_of(k0, 64), size)

        for c in range(RB // RC):
            part = pl.ds(c * RC, RC)
            keys, values = kv[0, rows, :], kv[1, rows, :]
            queries, cot = q2[b, part, :], do2[b, part, :]
            scores = dot(keys, queries, NT) * SCALE2
            if masked:
                scores = masked_scores(scores, k0, block_of(b) * BLK + c * (RC // PG))
            weights = jnp.exp2(scores - lse[b, :, part])
            grads = (weights * (dot(values, cot, NT) - off[b, :, part])).astype(bf16)
            dv[rows, :] += dot(weights.astype(bf16), cot)
            dk[rows, :] += dot(grads, queries)
            acc[b, :, part] += dot(keys, grads, TN)

    def finish_rows(k0, size):
        rows = pl.ds(pl.multiple_of(k0, 64), size)
        g16[0, rows, :] = (dk[rows, :] * SCALE).astype(bf16)
        g16[1, rows, :] = dv[rows, :].astype(bf16)

    def grad_rows(j):
        return pl.ds(pl.multiple_of(PRM + j * BLK, 64), BLK)

    def gz_copy(zz, tile):
        rows = grad_rows(4 * tile + zz)
        return remote(g16.at[:, rows, :], zr.at[z, tile], gzs.at[zz, tile], gzr.at[z, tile], seq=4 * x + zz)

    def gx_copy(tile):
        return remote(gx.at[tile], xr.at[x], gxs.at[tile], gxr.at[x], seq=4 * tile + z)

    def send_tile(tile):
        finish_rows(PRM + tile * TILE, TILE)

        @pl.loop(1, 4)
        def _(d):
            gz_copy((z + d) % 4, tile).start()

    def pass_tile(tile):
        rows = grad_rows(4 * tile + z)
        total = g16[:, rows, :].astype(f32)
        for d in range(1, 4):
            zz = (z + d) % 4
            remote(g16.at[:, rows, :], zr.at[zz, tile], gzs.at[zz, tile], gzr.at[zz, tile], seq=4 * x + zz).wait_recv()
            total = total + zr[zz, tile].astype(f32)

        @pl.when(tile == x)
        def _():
            xr[x] = total.astype(bf16)

        @pl.when(tile != x)
        def _():
            gx[tile] = total.astype(bf16)
            gx_copy(tile).start()

    mine = pl.ds(pl.multiple_of(r * 512, 512), 512)
    theirs = pl.ds(pl.multiple_of((1 - r) * 512, 512), 512)
    gpy_out = remote(g16.at[:, theirs, :], yrp, gpys.at[0], gpys.at[1], roll=1 - r)

    def gpz_copy(zz):
        rows = pl.ds(pl.multiple_of(zz * 128, 128), 128)
        return remote(gyp.at[:, rows, :], zrp.at[z], gpzs.at[zz], gpzr.at[z], seq=4 * x + zz)

    def gpx_copy(xx):
        rows = pl.ds(pl.multiple_of(xx * 32, 32), 32)
        return remote(gxp.at[:, rows, :], xrp.at[x], gpxs.at[xx], gpxr.at[x], seq=4 * xx + z)

    def pass_rolls():
        gpy_out.wait_recv()
        gyp[0] = (dk[mine, :] * SCALE + yrp[0].astype(f32)).astype(bf16)
        gyp[1] = (dv[mine, :] + yrp[1].astype(f32)).astype(bf16)

        @pl.loop(1, 4)
        def _(d):
            gpz_copy((z + d) % 4).start()

    def pass_prompt():
        rows = pl.ds(pl.multiple_of(z * 128, 128), 128)
        total = gyp[:, rows, :].astype(f32)
        for d in range(1, 4):
            zz = (z + d) % 4
            remote(gyp.at[:, rows, :], zrp.at[zz], gpzs.at[zz], gpzr.at[zz], seq=4 * x + zz).wait_recv()
            total = total + zrp[zz].astype(f32)
        gxp[...] = total.astype(bf16)

        @pl.loop(1, 4)
        def _(d):
            gpx_copy((x + d) % 4).start()

        xrp[x] = gxp[:, pl.ds(pl.multiple_of(x * 32, 32), 32), :]

    dq_out = remote(o16.at[3], dq.at[hs], osem.at[2], osem.at[3], seq=partner)

    low = jnp.minimum(x, 3 - x)
    early = 3 - 2 * low
    later = jnp.where(x < 2, 1, 0)

    @pl.loop(0, 7)
    def _(i):
        k = i - early - 2
        rest = k >= 0
        first = i < early
        prompt = (i >= early) & (k < 0)
        second = k > low
        b = jnp.where(first, later, jnp.where(prompt, early + 1 - i, jnp.where(second, 0, 1)))
        tile = jnp.where(first, 3 - low - i, jnp.where(second, k - low - 1, jnp.maximum(k, 0)))
        diagonal = (i == 0) | (rest & (b != later) & (tile == low))

        @pl.when(prompt)
        def _():
            backward_tile(b, 0, PRM, False)

        @pl.when((first | rest) & jnp.logical_not(diagonal))
        def _():
            backward_tile(b, PRM + tile * TILE, TILE, False)

        @pl.when(diagonal)
        def _():
            @pl.loop(0, 1 + z // 2)
            def _(half):
                backward_tile(b, PRM + tile * TILE + half * HALF, HALF, True)

        @pl.when(first | (rest & second))
        def _():
            send_tile(tile)

        @pl.when((i > 0) & (i <= early))
        def _():
            pass_tile(4 - low - i)

        @pl.when(i == early + 1)
        def _():
            finish_rows(0, PRM)
            gpy_out.start()

        @pl.when(k == 0)
        def _():
            pass_rolls()

        @pl.when(k == 1)
        def _():
            pass_prompt()

        @pl.when(k == low)
        def _():
            o16[3] = (acc[1] * SCALE).T.astype(bf16)
            dq_out.start()

        @pl.when(k == 2 * low + 1)
        def _():
            o16[2] = (acc[0] * SCALE).T.astype(bf16)

            @pl.when(low == 1)
            def _():
                pass_tile(0)

    own_dq = pltpu.make_async_copy(o16.at[2], dq.at[hs], lsem.at[7])
    own_dq.start()
    pass_tile(low)

    @pl.loop(1, 4)
    def _(d):
        xx = (x + d) % 4
        remote(gxp.at[:, pl.ds(0, 32), :], xrp.at[xx], gpxs.at[xx], gpxr.at[xx], seq=4 * xx + z).wait_recv()

    for h in range(2):
        dp_out[h] = (xrp[2 * h].astype(f32) + xrp[2 * h + 1].astype(f32)).astype(bf16)

    @pl.loop(1, 4)
    def _(d):
        xx = (x + d) % 4

        @pl.when(sees(xx))
        def _():
            remote(gx.at[xx], xr.at[xx], gxs.at[xx], gxr.at[xx], seq=4 * xx + z).wait_recv()

    for h in range(2):
        total = jnp.zeros(xr.shape[1:], f32)
        for xx in (2 * h, 2 * h + 1):
            total = total + jnp.where(x <= max(xx, 3 - xx), xr[xx].astype(f32), 0.0)
        dkv_out[h] = total.astype(bf16)

    py_copy(z).wait_send()
    gpy_out.wait_send()
    q_out.wait_send()
    do_out.wait_send()
    out_out.wait()
    dq_out.wait()
    own_out.wait()
    own_dq.wait()

    @pl.loop(1, 4)
    def _(d):
        xx = (x + d) % 4
        zz = (z + d) % 4
        px_copy(xx).wait_send()
        pz_copy(zz).wait_send()
        py_copy(zz).wait_send()
        gpz_copy(zz).wait_send()
        gpx_copy(xx).wait_send()

        @pl.when(sees(xx))
        def _():
            kvx_copy(xx).wait_send()

        @pl.when(xx <= top)
        def _():
            gx_copy(xx).wait_send()

        @pl.loop(0, top + 1)
        def _(tile):
            kvz_copy(zz, tile).wait_send()
            gz_copy(zz, tile).wait_send()


def attention(q_rows, do_rows, kv_rows, prompt_rows):
    any_spec = pl.BlockSpec(memory_space=pl.ANY)
    vmem = pl.BlockSpec(memory_space=pltpu.VMEM)
    dma = pltpu.SemaphoreType.DMA
    return pl.pallas_call(
        kernel,
        out_shape=[
            jax.ShapeDtypeStruct((2, RB, HD), bf16),
            jax.ShapeDtypeStruct((2, RB, HD), bf16),
            jax.ShapeDtypeStruct((2, 2, BLK, HD), bf16),
            jax.ShapeDtypeStruct((2, 2, 32, HD), bf16),
        ],
        in_specs=[any_spec] * 4,
        out_specs=[any_spec, any_spec, vmem, vmem],
        scratch_shapes=[
            pltpu.VMEM((2, RB, HD), bf16),
            pltpu.VMEM((2, RB, HD), bf16),
            pltpu.VMEM((2, PRM + N * BLK, HD), bf16),
            pltpu.VMEM((2, HD, RB), f32),
            pltpu.VMEM((2, 1, RB), f32),
            pltpu.VMEM((2, 1, RB), f32),
            pltpu.VMEM((2, 1, RB), f32),
            pltpu.VMEM((2, 1, RB), f32),
            pltpu.VMEM((4, RB, HD), bf16),
            pltpu.VMEM((PRM + N * BLK, HD), f32),
            pltpu.VMEM((PRM + N * BLK, HD), f32),
            pltpu.VMEM((2, PRM + N * BLK, HD), bf16),
            pltpu.VMEM((4, 4, 2, BLK, HD), bf16),
            pltpu.VMEM((2, 512, HD), bf16),
            pltpu.VMEM((2, 512, HD), bf16),
            pltpu.VMEM((4, 2, 128, HD), bf16),
            pltpu.VMEM((4, 2, BLK, HD), bf16),
            pltpu.VMEM((2, 128, HD), bf16),
            pltpu.VMEM((4, 2, BLK, HD), bf16),
            pltpu.VMEM((4, 2, 32, HD), bf16),
            dma((8,)),
            dma((4,)),
            dma((4,)),
            dma((4, 4)),
            dma((4, 4)),
            dma((4,)),
            dma((4,)),
            dma((4,)),
            dma((4,)),
            dma((4,)),
            dma((4,)),
            dma((4,)),
            dma((4,)),
            dma((4, 4)),
            dma((4, 4)),
            dma((2,)),
            dma((4,)),
            dma((4,)),
            dma((4,)),
            dma((4,)),
            dma((4,)),
            dma((4,)),
        ],
        compiler_params=pltpu.CompilerParams(
            collective_id=0, has_side_effects=True, vmem_limit_bytes=58 * 2**20
        ),
    )(q_rows, do_rows, kv_rows, prompt_rows)


def local(queries, rollout_keys, rollout_values, prompt_keys, prompt_values, grad_out, lengths):
    first_row = lax.axis_index("seq") * BLK
    valid = ((first_row + jnp.arange(BLK, dtype=jnp.int32)) < lengths[0])[None, :, None, None]

    def by_group(rows):
        return rows.reshape(BLK, 2, PG, HD).transpose(1, 0, 2, 3)

    def merged(rows):
        return rows.transpose(1, 0, 2, 3).reshape(1, BLK, 2 * PG, HD)

    q_rows = by_group(queries[0]).reshape(2, RB, HD)
    cot = by_group(grad_out[0])
    do_rows = jnp.where(valid, cot, jnp.zeros_like(cot)).reshape(2, RB, HD)
    kv_rows = jnp.stack([rollout_keys[0], rollout_values[0]]).transpose(2, 0, 1, 3)
    prompt_rows = jnp.stack([prompt_keys, prompt_values]).transpose(2, 0, 1, 3)
    out, dq, dkv, dprompt = attention(q_rows, do_rows, kv_rows, prompt_rows)
    out = out.reshape(2, BLK, PG, HD)
    out = jnp.where(valid, out, jnp.zeros_like(out))
    dkv = dkv.transpose(1, 2, 0, 3)
    dprompt = dprompt.transpose(1, 2, 0, 3)
    return (
        merged(out),
        merged(dq.reshape(2, BLK, PG, HD)),
        dkv[0][None],
        dkv[1][None],
        dprompt[0],
        dprompt[1],
    )


def solution(mesh):
    rows = P("roll", "seq", "head", None)
    prompt = P(("seq", "roll"), "head", None)
    return jax.shard_map(
        local,
        mesh=mesh,
        in_specs=(rows, rows, rows, prompt, prompt, rows, P("roll")),
        out_specs=(rows, rows, rows, rows, prompt, prompt),
        check_vma=False,
    )
```

```python
import math

import jax
import jax.numpy as jnp
from jax import lax
from jax.experimental import pallas as pl
from jax.experimental.pallas import tpu as pltpu
from jax.sharding import PartitionSpec as P

f32, bf16 = jnp.float32, jnp.bfloat16
N = 16
BLK = 192
PRM = 1024
HD = 128
PG = 8
RB = BLK * PG
TILE = 4 * BLK
HALF = 2 * BLK
RC = RB // 2
SCALE = HD**-0.5
SCALE2 = SCALE * math.log2(math.e)
NEG = -1e30
MESH = pl.DeviceIdType.MESH

NN = (((1,), (0,)), ((), ()))
NT = (((1,), (1,)), ((), ()))
TN = (((0,), (0,)), ((), ()))


F_PROMPT, F_FULL, F_DIAG, F_END, B_PROMPT, B_FULL, B_DIAG = range(7)
W_ROLL, W_Q, W_DO, W_TILE, SEND, PASS, ROLLS, PROMPT, DQ, GPY = (1 << i for i in range(10))


def schedule(x):
    low, top = min(x, 3 - x), max(x, 3 - x)
    late = 1 if x < 2 else 0
    steps = []

    def forward(b, tiles, waits):
        for t in tiles:
            last = top if b == late else low
            steps.append((F_DIAG if t == last else F_FULL, b, t, W_TILE if t in waits else 0))

    def prompt(b):
        steps.append((F_PROMPT, b, 0, W_Q if b else 0))
        steps.append((F_PROMPT, b, 1, 0 if b else W_ROLL))

    def backward_low(b):
        steps.append((B_PROMPT, b, 0, 0))
        for t in range(low + 1):
            last = t == low
            steps.append((B_DIAG if last else B_FULL, b, t, DQ if last else 0))

    prompt(0)
    if late:
        forward(0, range(low + 1), range(low + 1))
        steps.append((F_END, 0, 0, 0))
        backward_low(0)
        prompt(1)
        forward(1, range(top + 1), range(low + 1, top + 1))
        steps.append((F_END, 1, 0, W_DO))
    else:
        forward(0, (0, 1), (0, 1))
        prompt(1)
        forward(0, range(2, top + 1), range(2, top + 1))
        steps.append((F_END, 0, 0, 0))
        forward(1, range(low + 1), ())
        steps.append((F_END, 1, 0, W_DO))
        backward_low(1)
    steps.append((B_PROMPT, late, 0, GPY))
    for i, t in enumerate(range(top, -1, -1)):
        flags = SEND | (ROLLS if i == 0 else PASS) | (PROMPT if i == 1 else 0) | (DQ if t == 0 else 0)
        steps.append((B_DIAG if t == top else B_FULL, late, t, flags))
    return [kind + 8 * b + 16 * t + 64 * flags for kind, b, t, flags in steps]


def dot(a, b, dims=NN):
    return lax.dot_general(a, b, dims, preferred_element_type=f32)


def kernel(
    length, q_in, do_in, kvp_in,
    out, dq, dkv_out, dp_out,
    q2, do2, kv, acc, mx, tot, lse, off, o16, dk, dv, g16,
    zr, yrp, gyp, zrp, gx, gxp, xr, xrp,
    lsem, kvxs, kvxr, kvzs, kvzr, ppxs, ppxr, ppzs, ppzr, ppys, ppyr, qsem, osem,
    gzs, gzr, gpys, gpzs, gpzr, gxs, gxr, gpxs, gpxr,
):
    s = lax.axis_index("seq")
    r = lax.axis_index("roll")
    x, z = s // 4, s % 4
    kv_in = kvp_in.at[:, :, pl.ds(0, BLK), :]
    pk_in = kvp_in.at[:, :, pl.ds(BLK, 32), :]
    hs = x // 2
    top = jnp.maximum(x, 3 - x)
    partner = 4 * (3 - x) + z

    barrier = pltpu.get_barrier_semaphore()
    for d in range(1, 4):
        pl.semaphore_signal(barrier, inc=1, device_id={"seq": (x + d) % 4 * 4 + z}, device_id_type=MESH)
        pl.semaphore_signal(barrier, inc=1, device_id={"seq": 4 * x + (z + d) % 4}, device_id_type=MESH)
    pl.semaphore_signal(barrier, inc=1, device_id={"roll": 1 - r}, device_id_type=MESH)

    def remote(src, dst, ssem, rsem, **where):
        return pltpu.make_async_remote_copy(
            src_ref=src, dst_ref=dst, send_sem=ssem, recv_sem=rsem,
            device_id=where, device_id_type=MESH,
        )

    def kv_rows(j):
        return kv.at[:, pl.ds(pl.multiple_of(PRM + j * BLK, 64), BLK), :]

    def p_rows(xx):
        return kv.at[:, pl.ds(pl.multiple_of(r * 512 + z * 128 + xx * 32, 32), 32), :]

    def p_column(rr, zz):
        return kv.at[:, pl.ds(pl.multiple_of(rr * 512 + zz * 128, 128), 128), :]

    own_p = pltpu.make_async_copy(pk_in.at[hs], p_rows(x), lsem.at[3])
    own_p.start()
    own_kv = pltpu.make_async_copy(kv_in.at[hs], kv_rows(s), lsem.at[2])
    own_kv.start()
    own_q = pltpu.make_async_copy(q_in.at[hs], q2.at[0], lsem.at[0])
    own_q.start()
    own_do = pltpu.make_async_copy(do_in.at[hs], do2.at[0], lsem.at[1])
    own_do.start()
    pl.semaphore_wait(barrier, 7)

    def kvx_copy(xx):
        return remote(kv_in.at[xx // 2], kv_rows(s), kvxs.at[xx], kvxr.at[x], seq=4 * xx + z)

    def px_copy(xx):
        return remote(pk_in.at[xx // 2], p_rows(x), ppxs.at[xx], ppxr.at[x], seq=4 * xx + z)

    def pz_copy(zz):
        return remote(p_column(r, z), p_column(r, z), ppzs.at[zz], ppzr.at[z], seq=4 * x + zz)

    def py_copy(zz):
        return remote(p_column(r, zz), p_column(r, zz), ppys.at[zz], ppyr.at[zz], roll=1 - r)

    def kvz_copy(zz, tile):
        rows = kv_rows(4 * tile + z)
        return remote(rows, rows, kvzs.at[zz, tile], kvzr.at[z, tile], seq=4 * x + zz)

    def sees(xx):
        return x <= jnp.maximum(xx, 3 - xx)

    @pl.loop(1, 4)
    def _(d):
        px_copy((x + d) % 4).start()

    @pl.loop(1, 4)
    def _(d):
        xx = (x + d) % 4

        @pl.when(sees(xx))
        def _():
            kvx_copy(xx).start()

    q_out = remote(q_in.at[1 - hs], q2.at[1], qsem.at[0], qsem.at[1], seq=partner)
    q_out.start()
    acc[...] = jnp.zeros_like(acc)
    mx[...] = jnp.full_like(mx, NEG)
    tot[...] = jnp.zeros_like(tot)
    dk[...] = jnp.zeros_like(dk)
    dv[...] = jnp.zeros_like(dv)
    own_p.wait()

    @pl.loop(1, 4)
    def _(d):
        xx = (x + d) % 4
        remote(pk_in.at[hs], p_rows(xx), ppxs.at[xx], ppxr.at[xx], seq=4 * xx + z).wait_recv()

    @pl.loop(1, 4)
    def _(d):
        pz_copy((z + d) % 4).start()

    py_copy(z).start()
    own_kv.wait()

    @pl.loop(0, top + 1)
    def _(tile):
        @pl.when(tile != x)
        def _():
            remote(kv_in.at[hs], kv_rows(4 * tile + z), kvxs.at[tile], kvxr.at[tile], seq=4 * tile + z).wait_recv()

        @pl.loop(1, 4)
        def _(d):
            kvz_copy((z + d) % 4, tile).start()

    @pl.loop(1, 4)
    def _(d):
        zz = (z + d) % 4
        remote(p_column(r, zz), p_column(r, zz), ppzs.at[zz], ppzr.at[zz], seq=4 * x + zz).wait_recv()
        py_copy(zz).start()

    do_out = remote(do_in.at[1 - hs], do2.at[1], qsem.at[2], qsem.at[3], seq=partner)
    do_out.start()

    def block_of(b):
        return jnp.where(b == 0, s, partner)

    def masked_scores(scores, k0, q0):
        key_pos = k0 - PRM + lax.broadcasted_iota(jnp.int32, scores.shape, 0)
        query_pos = q0 + lax.broadcasted_iota(jnp.int32, scores.shape, 1) // PG
        return jnp.where(key_pos <= query_pos, scores, NEG)

    def forward_tile(b, k0, size, masked):
        rows = pl.ds(pl.multiple_of(k0, 64), size)
        scores = dot(kv[0, rows, :], q2[b], NT) * SCALE2
        if masked:
            scores = masked_scores(scores, k0, block_of(b) * BLK)
        old = mx[b]
        new = jnp.maximum(old, jnp.max(scores, 0, keepdims=True))
        lifted = jnp.exp2(scores - new)
        shrink = jnp.exp2(old - new)
        mx[b] = new
        tot[b] = tot[b] * shrink + jnp.sum(lifted, 0, keepdims=True)
        acc[b] = acc[b] * shrink + dot(kv[1, rows, :], lifted.astype(bf16), TN)

    own_q.wait()
    own_do.wait()

    def wait_tile(tile):
        @pl.loop(1, 4)
        def _(d):
            zz = (z + d) % 4
            rows = kv_rows(4 * tile + zz)
            remote(rows, rows, kvzs.at[zz, tile], kvzr.at[zz, tile], seq=4 * x + zz).wait_recv()

    def backward_tile(b, k0, size, masked):
        rows = pl.ds(pl.multiple_of(k0, 64), size)

        for c in range(RB // RC):
            part = pl.ds(c * RC, RC)
            keys, values = kv[0, rows, :], kv[1, rows, :]
            queries, cot = q2[b, part, :], do2[b, part, :]
            scores = dot(keys, queries, NT) * SCALE2
            if masked:
                scores = masked_scores(scores, k0, block_of(b) * BLK + c * (RC // PG))
            weights = jnp.exp2(scores - lse[b, :, part])
            grads = (weights * (dot(values, cot, NT) - off[b, :, part])).astype(bf16)
            dv[rows, :] += dot(weights.astype(bf16), cot)
            dk[rows, :] += dot(grads, queries)
            acc[b, :, part] += dot(keys, grads, TN)

    def finish_rows(k0, size):
        rows = pl.ds(pl.multiple_of(k0, 64), size)
        g16[0, rows, :] = (dk[rows, :] * SCALE).astype(bf16)
        g16[1, rows, :] = dv[rows, :].astype(bf16)

    def grad_rows(j):
        return pl.ds(pl.multiple_of(PRM + j * BLK, 64), BLK)

    def gz_copy(zz, tile):
        rows = grad_rows(4 * tile + zz)
        return remote(g16.at[:, rows, :], zr.at[z, tile], gzs.at[zz, tile], gzr.at[z, tile], seq=4 * x + zz)

    def gx_copy(tile):
        return remote(gx.at[tile], xr.at[x], gxs.at[tile], gxr.at[x], seq=4 * tile + z)

    def send_tile(tile):
        finish_rows(PRM + tile * TILE, TILE)

        @pl.loop(1, 4)
        def _(d):
            gz_copy((z + d) % 4, tile).start()

    def pass_tile(tile):
        rows = grad_rows(4 * tile + z)
        total = g16[:, rows, :].astype(f32)
        for d in range(1, 4):
            zz = (z + d) % 4
            remote(g16.at[:, rows, :], zr.at[zz, tile], gzs.at[zz, tile], gzr.at[zz, tile], seq=4 * x + zz).wait_recv()
            total = total + zr[zz, tile].astype(f32)

        @pl.when(tile == x)
        def _():
            xr[x] = total.astype(bf16)

        @pl.when(tile != x)
        def _():
            gx[tile] = total.astype(bf16)
            gx_copy(tile).start()

    mine = pl.ds(pl.multiple_of(r * 512, 512), 512)
    theirs = pl.ds(pl.multiple_of((1 - r) * 512, 512), 512)
    gpy_out = remote(g16.at[:, theirs, :], yrp, gpys.at[0], gpys.at[1], roll=1 - r)

    def gpz_copy(zz):
        rows = pl.ds(pl.multiple_of(zz * 128, 128), 128)
        return remote(gyp.at[:, rows, :], zrp.at[z], gpzs.at[zz], gpzr.at[z], seq=4 * x + zz)

    def gpx_copy(xx):
        rows = pl.ds(pl.multiple_of(xx * 32, 32), 32)
        return remote(gxp.at[:, rows, :], xrp.at[x], gpxs.at[xx], gpxr.at[x], seq=4 * xx + z)

    def pass_rolls():
        gpy_out.wait_recv()
        gyp[0] = (dk[mine, :] * SCALE + yrp[0].astype(f32)).astype(bf16)
        gyp[1] = (dv[mine, :] + yrp[1].astype(f32)).astype(bf16)

        @pl.loop(1, 4)
        def _(d):
            gpz_copy((z + d) % 4).start()

    def pass_prompt():
        rows = pl.ds(pl.multiple_of(z * 128, 128), 128)
        total = gyp[:, rows, :].astype(f32)
        for d in range(1, 4):
            zz = (z + d) % 4
            remote(gyp.at[:, rows, :], zrp.at[zz], gpzs.at[zz], gpzr.at[zz], seq=4 * x + zz).wait_recv()
            total = total + zrp[zz].astype(f32)
        gxp[...] = total.astype(bf16)

        @pl.loop(1, 4)
        def _(d):
            gpx_copy((x + d) % 4).start()

        xrp[x] = gxp[:, pl.ds(pl.multiple_of(x * 32, 32), 32), :]

    dq_out = remote(o16.at[3], dq.at[hs], osem.at[2], osem.at[3], seq=partner)

    own_out = pltpu.make_async_copy(o16.at[0], out.at[hs], lsem.at[4])
    out_out = remote(o16.at[1], out.at[hs], osem.at[0], osem.at[1], seq=partner)
    own_dq = pltpu.make_async_copy(o16.at[2], dq.at[hs], lsem.at[7])
    plans = [schedule(xx) for xx in range(4)]

    @pl.loop(0, len(plans[0]))
    def _(i):
        code = jnp.int32(0)
        for n, column in enumerate(zip(*plans)):
            here = jnp.where(x == 0, column[0], jnp.where(x == 1, column[1], jnp.where(x == 2, column[2], column[3])))
            code = jnp.where(i == n, here, code)
        kind = code % 8
        b = code // 8 % 2
        tile = code // 16 % 4
        flags = code // 64

        def has(flag):
            return flags // flag % 2 == 1

        @pl.when(has(W_Q))
        def _():
            q_out.wait_recv()

        @pl.when(has(W_ROLL))
        def _():
            @pl.loop(0, 4)
            def _(zz):
                rows = p_column(1 - r, zz)
                remote(rows, rows, ppys.at[zz], ppyr.at[zz], roll=1 - r).wait_recv()

        @pl.when(has(W_TILE))
        def _():
            wait_tile(tile)

        @pl.when(has(W_DO))
        def _():
            do_out.wait_recv()

        @pl.when(kind == F_PROMPT)
        def _():
            forward_tile(b, (r + tile) % 2 * 512, 512, False)

        @pl.when(kind == F_FULL)
        def _():
            forward_tile(b, PRM + tile * TILE, TILE, False)

        @pl.when(kind == F_DIAG)
        def _():
            @pl.loop(0, 1 + z // 2)
            def _(half):
                forward_tile(b, PRM + tile * TILE + half * HALF, HALF, True)

        @pl.when(kind == F_END)
        def _():
            total = tot[b]
            normal = acc[b] / total
            lse[b] = mx[b] + jnp.log2(total)
            off[b] = jnp.sum(normal * do2[b].astype(f32).T, 0, keepdims=True)
            row_pos = block_of(b) * BLK + lax.broadcasted_iota(jnp.int32, (1, RB), 1) // PG
            o16[b] = jnp.where(row_pos < length[0], normal, 0.0).T.astype(bf16)
            acc[b] = jnp.zeros(acc.shape[1:], f32)

            @pl.when(b == 0)
            def _():
                own_out.start()

            @pl.when(b == 1)
            def _():
                out_out.start()

        @pl.when(kind == B_PROMPT)
        def _():
            backward_tile(b, 0, PRM, False)

        @pl.when(kind == B_FULL)
        def _():
            backward_tile(b, PRM + tile * TILE, TILE, False)

        @pl.when(kind == B_DIAG)
        def _():
            @pl.loop(0, 1 + z // 2)
            def _(half):
                backward_tile(b, PRM + tile * TILE + half * HALF, HALF, True)

        @pl.when(has(SEND))
        def _():
            send_tile(tile)

        @pl.when(has(GPY))
        def _():
            finish_rows(0, PRM)
            gpy_out.start()

        @pl.when(has(DQ))
        def _():
            o16[2 + b] = (acc[b] * SCALE).T.astype(bf16)

            @pl.when(b == 0)
            def _():
                own_dq.start()

            @pl.when(b == 1)
            def _():
                dq_out.start()

        @pl.when(has(ROLLS))
        def _():
            pass_rolls()

        @pl.when(has(PASS))
        def _():
            pass_tile(tile + 1)

        @pl.when(has(PROMPT))
        def _():
            pass_prompt()

    pass_tile(0)

    @pl.loop(1, 4)
    def _(d):
        xx = (x + d) % 4
        remote(gxp.at[:, pl.ds(0, 32), :], xrp.at[xx], gpxs.at[xx], gpxr.at[xx], seq=4 * xx + z).wait_recv()

    for h in range(2):
        dp_out[h] = (xrp[2 * h].astype(f32) + xrp[2 * h + 1].astype(f32)).astype(bf16)

    @pl.loop(1, 4)
    def _(d):
        xx = (x + d) % 4

        @pl.when(sees(xx))
        def _():
            remote(gx.at[xx], xr.at[xx], gxs.at[xx], gxr.at[xx], seq=4 * xx + z).wait_recv()

    for h in range(2):
        total = jnp.zeros(xr.shape[1:], f32)
        for xx in (2 * h, 2 * h + 1):
            total = total + jnp.where(x <= max(xx, 3 - xx), xr[xx].astype(f32), 0.0)
        dkv_out[h] = total.astype(bf16)

    py_copy(z).wait_send()
    gpy_out.wait_send()
    q_out.wait_send()
    do_out.wait_send()
    out_out.wait()
    dq_out.wait()
    own_out.wait()
    own_dq.wait()

    @pl.loop(1, 4)
    def _(d):
        xx = (x + d) % 4
        zz = (z + d) % 4
        px_copy(xx).wait_send()
        pz_copy(zz).wait_send()
        py_copy(zz).wait_send()
        gpz_copy(zz).wait_send()
        gpx_copy(xx).wait_send()

        @pl.when(sees(xx))
        def _():
            kvx_copy(xx).wait_send()

        @pl.when(xx <= top)
        def _():
            gx_copy(xx).wait_send()

        @pl.loop(0, top + 1)
        def _(tile):
            kvz_copy(zz, tile).wait_send()
            gz_copy(zz, tile).wait_send()


def attention(lengths, q_rows, do_rows, kvp_rows):
    any_spec = pl.BlockSpec(memory_space=pl.ANY)
    vmem = pl.BlockSpec(memory_space=pltpu.VMEM)
    dma = pltpu.SemaphoreType.DMA
    return pl.pallas_call(
        kernel,
        out_shape=[
            jax.ShapeDtypeStruct((2, RB, HD), bf16),
            jax.ShapeDtypeStruct((2, RB, HD), bf16),
            jax.ShapeDtypeStruct((2, 2, BLK, HD), bf16),
            jax.ShapeDtypeStruct((2, 2, 32, HD), bf16),
        ],
        in_specs=[pl.BlockSpec(memory_space=pltpu.SMEM)] + [any_spec] * 3,
        out_specs=[any_spec, any_spec, vmem, vmem],
        scratch_shapes=[
            pltpu.VMEM((2, RB, HD), bf16),
            pltpu.VMEM((2, RB, HD), bf16),
            pltpu.VMEM((2, PRM + N * BLK, HD), bf16),
            pltpu.VMEM((2, HD, RB), f32),
            pltpu.VMEM((2, 1, RB), f32),
            pltpu.VMEM((2, 1, RB), f32),
            pltpu.VMEM((2, 1, RB), f32),
            pltpu.VMEM((2, 1, RB), f32),
            pltpu.VMEM((4, RB, HD), bf16),
            pltpu.VMEM((PRM + N * BLK, HD), f32),
            pltpu.VMEM((PRM + N * BLK, HD), f32),
            pltpu.VMEM((2, PRM + N * BLK, HD), bf16),
            pltpu.VMEM((4, 4, 2, BLK, HD), bf16),
            pltpu.VMEM((2, 512, HD), bf16),
            pltpu.VMEM((2, 512, HD), bf16),
            pltpu.VMEM((4, 2, 128, HD), bf16),
            pltpu.VMEM((4, 2, BLK, HD), bf16),
            pltpu.VMEM((2, 128, HD), bf16),
            pltpu.VMEM((4, 2, BLK, HD), bf16),
            pltpu.VMEM((4, 2, 32, HD), bf16),
            dma((8,)),
            dma((4,)),
            dma((4,)),
            dma((4, 4)),
            dma((4, 4)),
            dma((4,)),
            dma((4,)),
            dma((4,)),
            dma((4,)),
            dma((4,)),
            dma((4,)),
            dma((4,)),
            dma((4,)),
            dma((4, 4)),
            dma((4, 4)),
            dma((2,)),
            dma((4,)),
            dma((4,)),
            dma((4,)),
            dma((4,)),
            dma((4,)),
            dma((4,)),
        ],
        compiler_params=pltpu.CompilerParams(
            collective_id=0, has_side_effects=True, vmem_limit_bytes=58 * 2**20
        ),
    )(lengths, q_rows, do_rows, kvp_rows)


def local(queries, rollout_keys, rollout_values, prompt_keys, prompt_values, grad_out, lengths):
    first_row = lax.axis_index("seq") * BLK
    valid = ((first_row + jnp.arange(BLK, dtype=jnp.int32)) < lengths[0])[None, :, None, None]

    def by_group(rows):
        return rows.reshape(BLK, 2, PG, HD).transpose(1, 0, 2, 3)

    def merged(rows):
        return rows.transpose(1, 0, 2, 3).reshape(1, BLK, 2 * PG, HD)

    q_rows = by_group(queries[0]).reshape(2, RB, HD)
    cot = by_group(grad_out[0])
    do_rows = jnp.where(valid, cot, jnp.zeros_like(cot)).reshape(2, RB, HD)
    joined = jnp.concatenate([rollout_keys[0], prompt_keys, rollout_values[0], prompt_values])
    joined = lax.optimization_barrier(joined).reshape(2, BLK + 32, 2, HD)
    out, dq, dkv, dprompt = attention(lengths, q_rows, do_rows, joined.transpose(2, 0, 1, 3))
    out = out.reshape(2, BLK, PG, HD)
    dkv = dkv.transpose(1, 2, 0, 3)
    dprompt = dprompt.transpose(1, 2, 0, 3)
    return (
        merged(out),
        merged(dq.reshape(2, BLK, PG, HD)),
        dkv[0][None],
        dkv[1][None],
        dprompt[0],
        dprompt[1],
    )


def solution(mesh):
    rows = P("roll", "seq", "head", None)
    prompt = P(("seq", "roll"), "head", None)
    return jax.shard_map(
        local,
        mesh=mesh,
        in_specs=(rows, rows, rows, prompt, prompt, rows, P("roll")),
        out_specs=(rows, rows, rows, rows, prompt, prompt),
        check_vma=False,
    )
```

```python
import math

import jax
import jax.numpy as jnp
from jax import lax
from jax.experimental import pallas as pl
from jax.experimental.pallas import tpu as pltpu
from jax.sharding import PartitionSpec as P

f32, bf16 = jnp.float32, jnp.bfloat16
N = 16
BLK = 192
PRM = 1024
HD = 128
PG = 8
RB = BLK * PG
TILE = 4 * BLK
HALF = 2 * BLK
RC = RB // 2
SCALE = HD**-0.5
SCALE2 = SCALE * math.log2(math.e)
NEG = -1e30
MESH = pl.DeviceIdType.MESH

NN = (((1,), (0,)), ((), ()))
NT = (((1,), (1,)), ((), ()))
TN = (((0,), (0,)), ((), ()))


F_PROMPT, F_FULL, F_DIAG, F_END, B_PROMPT, B_FULL, B_DIAG = range(7)
W_ROLL, W_Q, W_DO, W_TILE, SEND, PASS, DQ, GPY = (1 << i for i in range(8))


def schedule(x):
    low, top = min(x, 3 - x), max(x, 3 - x)
    late = 1 if x < 2 else 0
    steps = []

    def forward(b, tiles, waits):
        for t in tiles:
            last = top if b == late else low
            steps.append((F_DIAG if t == last else F_FULL, b, t, W_TILE if t in waits else 0))

    def prompt(b):
        steps.append((F_PROMPT, b, 0, W_Q if b else 0))
        steps.append((F_PROMPT, b, 1, 0 if b else W_ROLL))

    def backward_low(b):
        steps.append((B_PROMPT, b, 0, 0))
        for t in range(low + 1):
            last = t == low
            steps.append((B_DIAG if last else B_FULL, b, t, DQ if last else 0))

    prompt(0)
    if late:
        forward(0, range(low + 1), range(low + 1))
        steps.append((F_END, 0, 0, 0))
        backward_low(0)
        prompt(1)
        forward(1, range(top + 1), range(low + 1, top + 1))
        steps.append((F_END, 1, 0, W_DO))
    else:
        forward(0, (0, 1), (0, 1))
        prompt(1)
        forward(0, range(2, top + 1), range(2, top + 1))
        steps.append((F_END, 0, 0, 0))
        forward(1, range(low + 1), ())
        steps.append((F_END, 1, 0, W_DO))
        backward_low(1)
    for t in range(top, -1, -1):
        if t == 0:
            steps.append((B_PROMPT, late, 0, GPY | PASS))
        flags = SEND | (PASS if 0 < t < top else 0) | (DQ if t == 0 else 0)
        steps.append((B_DIAG if t == top else B_FULL, late, t, flags))
    return [kind + 8 * b + 16 * t + 64 * flags for kind, b, t, flags in steps]


def dot(a, b, dims=NN):
    return lax.dot_general(a, b, dims, preferred_element_type=f32)


def kernel(
    length, q_in, do_in, kvp_in,
    out, dq, dkv_out, dp_out,
    q2, do2, kv, acc, mx, tot, lse, off, o16, dk, dv, g16,
    zr, yrp, gyp, zrp, gx, gxp, xr, xrp,
    lsem, kvxs, kvxr, kvzs, kvzr, ppxs, ppxr, ppzs, ppzr, ppys, ppyr, qsem, osem,
    dsem, gzs, gzr, gpys, gpzs, gpzr, gxs, gxr, gpxs, gpxr,
):
    s = lax.axis_index("seq")
    r = lax.axis_index("roll")
    x, z = s // 4, s % 4
    kv_in = kvp_in.at[:, :, pl.ds(0, BLK), :]
    pk_in = kvp_in.at[:, :, pl.ds(BLK, 32), :]
    hs = x // 2
    top = jnp.maximum(x, 3 - x)
    partner = 4 * (3 - x) + z

    barrier = pltpu.get_barrier_semaphore()
    for d in range(1, 4):
        pl.semaphore_signal(barrier, inc=1, device_id={"seq": (x + d) % 4 * 4 + z}, device_id_type=MESH)
        pl.semaphore_signal(barrier, inc=1, device_id={"seq": 4 * x + (z + d) % 4}, device_id_type=MESH)
    pl.semaphore_signal(barrier, inc=1, device_id={"roll": 1 - r}, device_id_type=MESH)

    def remote(src, dst, ssem, rsem, **where):
        return pltpu.make_async_remote_copy(
            src_ref=src, dst_ref=dst, send_sem=ssem, recv_sem=rsem,
            device_id=where, device_id_type=MESH,
        )

    def kv_rows(j):
        return kv.at[:, pl.ds(pl.multiple_of(PRM + j * BLK, 64), BLK), :]

    def p_rows(xx):
        return kv.at[:, pl.ds(pl.multiple_of(r * 512 + z * 128 + xx * 32, 32), 32), :]

    def p_column(rr, zz):
        return kv.at[:, pl.ds(pl.multiple_of(rr * 512 + zz * 128, 128), 128), :]

    own_p = pltpu.make_async_copy(pk_in.at[hs], p_rows(x), lsem.at[3])
    own_p.start()
    own_kv = pltpu.make_async_copy(kv_in.at[hs], kv_rows(s), lsem.at[2])
    own_kv.start()
    own_q = pltpu.make_async_copy(q_in.at[hs], q2.at[0], lsem.at[0])
    own_q.start()
    own_do = pltpu.make_async_copy(do_in.at[hs], do2.at[0], lsem.at[1])
    own_do.start()
    pl.semaphore_wait(barrier, 7)

    def kvx_copy(xx):
        return remote(kv_in.at[xx // 2], kv_rows(s), kvxs.at[xx], kvxr.at[x], seq=4 * xx + z)

    def px_copy(xx):
        return remote(pk_in.at[xx // 2], p_rows(x), ppxs.at[xx], ppxr.at[x], seq=4 * xx + z)

    def pz_copy(zz):
        return remote(p_column(r, z), p_column(r, z), ppzs.at[zz], ppzr.at[z], seq=4 * x + zz)

    def py_copy(zz):
        return remote(p_column(r, zz), p_column(r, zz), ppys.at[zz], ppyr.at[zz], roll=1 - r)

    def kvz_copy(zz, tile):
        rows = kv_rows(4 * tile + z)
        return remote(rows, rows, kvzs.at[zz, tile], kvzr.at[z, tile], seq=4 * x + zz)

    def sees(xx):
        return x <= jnp.maximum(xx, 3 - xx)

    @pl.loop(1, 4)
    def _(d):
        px_copy((x + d) % 4).start()

    @pl.loop(1, 4)
    def _(d):
        xx = (x + d) % 4

        @pl.when(sees(xx))
        def _():
            kvx_copy(xx).start()

    q_out = remote(q_in.at[1 - hs], q2.at[1], qsem.at[0], qsem.at[1], seq=partner)
    q_out.start()
    acc[...] = jnp.zeros_like(acc)
    mx[...] = jnp.full_like(mx, NEG)
    tot[...] = jnp.zeros_like(tot)
    dk[...] = jnp.zeros_like(dk)
    dv[...] = jnp.zeros_like(dv)
    own_p.wait()

    @pl.loop(1, 4)
    def _(d):
        xx = (x + d) % 4
        remote(pk_in.at[hs], p_rows(xx), ppxs.at[xx], ppxr.at[xx], seq=4 * xx + z).wait_recv()

    @pl.loop(1, 4)
    def _(d):
        pz_copy((z + d) % 4).start()

    py_copy(z).start()
    own_kv.wait()

    @pl.loop(0, top + 1)
    def _(tile):
        @pl.when(tile != x)
        def _():
            remote(kv_in.at[hs], kv_rows(4 * tile + z), kvxs.at[tile], kvxr.at[tile], seq=4 * tile + z).wait_recv()

        @pl.loop(1, 4)
        def _(d):
            kvz_copy((z + d) % 4, tile).start()

    @pl.loop(1, 4)
    def _(d):
        zz = (z + d) % 4
        remote(p_column(r, zz), p_column(r, zz), ppzs.at[zz], ppzr.at[zz], seq=4 * x + zz).wait_recv()
        py_copy(zz).start()

    do_out = remote(do_in.at[1 - hs], do2.at[1], qsem.at[2], qsem.at[3], seq=partner)
    do_out.start()

    def block_of(b):
        return jnp.where(b == 0, s, partner)

    def masked_scores(scores, k0, q0):
        key_pos = k0 - PRM + lax.broadcasted_iota(jnp.int32, scores.shape, 0)
        query_pos = q0 + lax.broadcasted_iota(jnp.int32, scores.shape, 1) // PG
        return jnp.where(key_pos <= query_pos, scores, NEG)

    def forward_tile(b, k0, size, masked):
        rows = pl.ds(pl.multiple_of(k0, 64), size)
        scores = dot(kv[0, rows, :], q2[b], NT) * SCALE2
        if masked:
            scores = masked_scores(scores, k0, block_of(b) * BLK)
        old = mx[b]
        new = jnp.maximum(old, jnp.max(scores, 0, keepdims=True))
        lifted = jnp.exp2(scores - new)
        shrink = jnp.exp2(old - new)
        mx[b] = new
        tot[b] = tot[b] * shrink + jnp.sum(lifted, 0, keepdims=True)
        acc[b] = acc[b] * shrink + dot(kv[1, rows, :], lifted.astype(bf16), TN)

    own_q.wait()
    own_do.wait()

    def wait_tile(tile):
        @pl.loop(1, 4)
        def _(d):
            zz = (z + d) % 4
            rows = kv_rows(4 * tile + zz)
            remote(rows, rows, kvzs.at[zz, tile], kvzr.at[zz, tile], seq=4 * x + zz).wait_recv()

    def backward_tile(b, k0, size, masked, after=lambda c: None):
        rows = pl.ds(pl.multiple_of(k0, 64), size)

        for c in range(RB // RC):
            part = pl.ds(c * RC, RC)
            keys, values = kv[0, rows, :], kv[1, rows, :]
            queries, cot = q2[b, part, :], do2[b, part, :]
            scores = dot(keys, queries, NT) * SCALE2
            if masked:
                scores = masked_scores(scores, k0, block_of(b) * BLK + c * (RC // PG))
            weights = jnp.exp2(scores - lse[b, :, part])
            grads = (weights * (dot(values, cot, NT) - off[b, :, part])).astype(bf16)
            dv[rows, :] += dot(weights.astype(bf16), cot)
            dk[rows, :] += dot(grads, queries)
            acc[b, :, part] += dot(keys, grads, TN)
            after(c)

    def finish_rows(k0, size):
        rows = pl.ds(pl.multiple_of(k0, 64), size)
        g16[0, rows, :] = (dk[rows, :] * SCALE).astype(bf16)
        g16[1, rows, :] = dv[rows, :].astype(bf16)

    def grad_rows(j):
        return pl.ds(pl.multiple_of(PRM + j * BLK, 64), BLK)

    def gz_copy(zz, tile):
        rows = grad_rows(4 * tile + zz)
        return remote(g16.at[:, rows, :], zr.at[z, tile], gzs.at[zz, tile], gzr.at[z, tile], seq=4 * x + zz)

    def gx_copy(tile):
        return remote(gx.at[tile], xr.at[x], gxs.at[tile], gxr.at[x], seq=4 * tile + z)

    def send_tile(tile):
        finish_rows(PRM + tile * TILE, TILE)

        @pl.loop(1, 4)
        def _(d):
            gz_copy((z + d) % 4, tile).start()

    def pass_tile(tile):
        rows = grad_rows(4 * tile + z)
        total = g16[:, rows, :].astype(f32)
        for d in range(1, 4):
            zz = (z + d) % 4
            remote(g16.at[:, rows, :], zr.at[zz, tile], gzs.at[zz, tile], gzr.at[zz, tile], seq=4 * x + zz).wait_recv()
            total = total + zr[zz, tile].astype(f32)

        @pl.when(tile == x)
        def _():
            xr[x] = total.astype(bf16)

        @pl.when(tile != x)
        def _():
            gx[tile] = total.astype(bf16)
            gx_copy(tile).start()

    mine = pl.ds(pl.multiple_of(r * 512, 512), 512)
    theirs = pl.ds(pl.multiple_of((1 - r) * 512, 512), 512)
    gpy_out = remote(g16.at[:, theirs, :], yrp, gpys.at[0], gpys.at[1], roll=1 - r)

    def gpz_copy(zz):
        rows = pl.ds(pl.multiple_of(zz * 128, 128), 128)
        return remote(gyp.at[:, rows, :], zrp.at[z], gpzs.at[zz], gpzr.at[z], seq=4 * x + zz)

    def gpx_copy(xx):
        rows = pl.ds(pl.multiple_of(xx * 32, 32), 32)
        return remote(gxp.at[:, rows, :], xrp.at[x], gpxs.at[xx], gpxr.at[x], seq=4 * xx + z)

    def pass_rolls():
        gpy_out.wait_recv()
        gyp[0] = (dk[mine, :] * SCALE + yrp[0].astype(f32)).astype(bf16)
        gyp[1] = (dv[mine, :] + yrp[1].astype(f32)).astype(bf16)

        @pl.loop(1, 4)
        def _(d):
            gpz_copy((z + d) % 4).start()

    def pass_prompt():
        rows = pl.ds(pl.multiple_of(z * 128, 128), 128)
        total = gyp[:, rows, :].astype(f32)
        for d in range(1, 4):
            zz = (z + d) % 4
            remote(gyp.at[:, rows, :], zrp.at[zz], gpzs.at[zz], gpzr.at[zz], seq=4 * x + zz).wait_recv()
            total = total + zrp[zz].astype(f32)
        gxp[...] = total.astype(bf16)

        @pl.loop(1, 4)
        def _(d):
            gpx_copy((x + d) % 4).start()

        xrp[x] = gxp[:, pl.ds(pl.multiple_of(x * 32, 32), 32), :]

    def dq_copies(c):
        rows = pl.ds(c * RC, RC)
        return (
            pltpu.make_async_copy(o16.at[2, rows, :], dq.at[hs, rows, :], dsem.at[c]),
            remote(o16.at[3, rows, :], dq.at[hs, rows, :], dsem.at[2 + c], dsem.at[4 + c], seq=partner),
        )

    def send_dq(b, c):
        rows = pl.ds(c * RC, RC)
        o16[2 + b, rows, :] = (acc[b, :, rows] * SCALE).T.astype(bf16)

        @pl.when(b == 0)
        def _():
            dq_copies(c)[0].start()

        @pl.when(b == 1)
        def _():
            dq_copies(c)[1].start()

    own_out = pltpu.make_async_copy(o16.at[0], out.at[hs], lsem.at[4])
    out_out = remote(o16.at[1], out.at[hs], osem.at[0], osem.at[1], seq=partner)
    plans = [schedule(xx) for xx in range(4)]

    @pl.loop(0, len(plans[0]))
    def _(i):
        code = jnp.int32(0)
        for n, column in enumerate(zip(*plans)):
            here = jnp.where(x == 0, column[0], jnp.where(x == 1, column[1], jnp.where(x == 2, column[2], column[3])))
            code = jnp.where(i == n, here, code)
        kind = code % 8
        b = code // 8 % 2
        tile = code // 16 % 4
        flags = code // 64

        def has(flag):
            return flags // flag % 2 == 1

        @pl.when(has(W_Q))
        def _():
            q_out.wait_recv()

        @pl.when(has(W_ROLL))
        def _():
            @pl.loop(0, 4)
            def _(zz):
                rows = p_column(1 - r, zz)
                remote(rows, rows, ppys.at[zz], ppyr.at[zz], roll=1 - r).wait_recv()

        @pl.when(has(W_TILE))
        def _():
            wait_tile(tile)

        @pl.when(has(W_DO))
        def _():
            do_out.wait_recv()

        @pl.when(kind == F_PROMPT)
        def _():
            forward_tile(b, (r + tile) % 2 * 512, 512, False)

        @pl.when(kind == F_FULL)
        def _():
            forward_tile(b, PRM + tile * TILE, TILE, False)

        @pl.when(kind == F_DIAG)
        def _():
            @pl.loop(0, 1 + z // 2)
            def _(half):
                forward_tile(b, PRM + tile * TILE + half * HALF, HALF, True)

        @pl.when(kind == F_END)
        def _():
            total = tot[b]
            normal = acc[b] / total
            lse[b] = mx[b] + jnp.log2(total)
            off[b] = jnp.sum(normal * do2[b].astype(f32).T, 0, keepdims=True)
            row_pos = block_of(b) * BLK + lax.broadcasted_iota(jnp.int32, (1, RB), 1) // PG
            o16[b] = jnp.where(row_pos < length[0], normal, 0.0).T.astype(bf16)
            acc[b] = jnp.zeros(acc.shape[1:], f32)

            @pl.when(b == 0)
            def _():
                own_out.start()

            @pl.when(b == 1)
            def _():
                out_out.start()

        @pl.when(kind == B_PROMPT)
        def _():
            backward_tile(b, 0, PRM, False)

        @pl.when(kind == B_FULL)
        def _():
            def after(c):
                @pl.when(has(DQ))
                def _():
                    send_dq(b, c)

            backward_tile(b, PRM + tile * TILE, TILE, False, after)

        @pl.when(kind == B_DIAG)
        def _():
            @pl.loop(0, 1 + z // 2)
            def _(half):
                backward_tile(b, PRM + tile * TILE + half * HALF, HALF, True)

            @pl.when(has(DQ))
            def _():
                for c in range(RB // RC):
                    send_dq(b, c)

        @pl.when(has(SEND))
        def _():
            send_tile(tile)

        @pl.when(has(GPY))
        def _():
            finish_rows(0, PRM)
            gpy_out.start()

        @pl.when(has(PASS))
        def _():
            pass_tile(tile + 1)

    pass_rolls()
    pass_tile(0)
    pass_prompt()

    @pl.loop(1, 4)
    def _(d):
        xx = (x + d) % 4
        remote(gxp.at[:, pl.ds(0, 32), :], xrp.at[xx], gpxs.at[xx], gpxr.at[xx], seq=4 * xx + z).wait_recv()

    for h in range(2):
        dp_out[h] = (xrp[2 * h].astype(f32) + xrp[2 * h + 1].astype(f32)).astype(bf16)

    @pl.loop(1, 4)
    def _(d):
        xx = (x + d) % 4

        @pl.when(sees(xx))
        def _():
            remote(gx.at[xx], xr.at[xx], gxs.at[xx], gxr.at[xx], seq=4 * xx + z).wait_recv()

    for h in range(2):
        total = jnp.zeros(xr.shape[1:], f32)
        for xx in (2 * h, 2 * h + 1):
            total = total + jnp.where(x <= max(xx, 3 - xx), xr[xx].astype(f32), 0.0)
        dkv_out[h] = total.astype(bf16)

    py_copy(z).wait_send()
    gpy_out.wait_send()
    q_out.wait_send()
    do_out.wait_send()
    out_out.wait()
    own_out.wait()
    for c in range(RB // RC):
        for copy in dq_copies(c):
            copy.wait()

    @pl.loop(1, 4)
    def _(d):
        xx = (x + d) % 4
        zz = (z + d) % 4
        px_copy(xx).wait_send()
        pz_copy(zz).wait_send()
        py_copy(zz).wait_send()
        gpz_copy(zz).wait_send()
        gpx_copy(xx).wait_send()

        @pl.when(sees(xx))
        def _():
            kvx_copy(xx).wait_send()

        @pl.when(xx <= top)
        def _():
            gx_copy(xx).wait_send()

        @pl.loop(0, top + 1)
        def _(tile):
            kvz_copy(zz, tile).wait_send()
            gz_copy(zz, tile).wait_send()


def attention(lengths, q_rows, do_rows, kvp_rows):
    any_spec = pl.BlockSpec(memory_space=pl.ANY)
    vmem = pl.BlockSpec(memory_space=pltpu.VMEM)
    dma = pltpu.SemaphoreType.DMA
    return pl.pallas_call(
        kernel,
        out_shape=[
            jax.ShapeDtypeStruct((2, RB, HD), bf16),
            jax.ShapeDtypeStruct((2, RB, HD), bf16),
            jax.ShapeDtypeStruct((2, 2, BLK, HD), bf16),
            jax.ShapeDtypeStruct((2, 2, 32, HD), bf16),
        ],
        in_specs=[pl.BlockSpec(memory_space=pltpu.SMEM)] + [any_spec] * 3,
        out_specs=[any_spec, any_spec, vmem, vmem],
        scratch_shapes=[
            pltpu.VMEM((2, RB, HD), bf16),
            pltpu.VMEM((2, RB, HD), bf16),
            pltpu.VMEM((2, PRM + N * BLK, HD), bf16),
            pltpu.VMEM((2, HD, RB), f32),
            pltpu.VMEM((2, 1, RB), f32),
            pltpu.VMEM((2, 1, RB), f32),
            pltpu.VMEM((2, 1, RB), f32),
            pltpu.VMEM((2, 1, RB), f32),
            pltpu.VMEM((4, RB, HD), bf16),
            pltpu.VMEM((PRM + N * BLK, HD), f32),
            pltpu.VMEM((PRM + N * BLK, HD), f32),
            pltpu.VMEM((2, PRM + N * BLK, HD), bf16),
            pltpu.VMEM((4, 4, 2, BLK, HD), bf16),
            pltpu.VMEM((2, 512, HD), bf16),
            pltpu.VMEM((2, 512, HD), bf16),
            pltpu.VMEM((4, 2, 128, HD), bf16),
            pltpu.VMEM((4, 2, BLK, HD), bf16),
            pltpu.VMEM((2, 128, HD), bf16),
            pltpu.VMEM((4, 2, BLK, HD), bf16),
            pltpu.VMEM((4, 2, 32, HD), bf16),
            dma((8,)),
            dma((4,)),
            dma((4,)),
            dma((4, 4)),
            dma((4, 4)),
            dma((4,)),
            dma((4,)),
            dma((4,)),
            dma((4,)),
            dma((4,)),
            dma((4,)),
            dma((4,)),
            dma((2,)),
            dma((6,)),
            dma((4, 4)),
            dma((4, 4)),
            dma((2,)),
            dma((4,)),
            dma((4,)),
            dma((4,)),
            dma((4,)),
            dma((4,)),
            dma((4,)),
        ],
        compiler_params=pltpu.CompilerParams(
            collective_id=0, has_side_effects=True, vmem_limit_bytes=58 * 2**20
        ),
    )(lengths, q_rows, do_rows, kvp_rows)


def local(queries, rollout_keys, rollout_values, prompt_keys, prompt_values, grad_out, lengths):
    first_row = lax.axis_index("seq") * BLK
    valid = ((first_row + jnp.arange(BLK, dtype=jnp.int32)) < lengths[0])[None, :, None, None]

    def by_group(rows):
        return rows.reshape(BLK, 2, PG, HD).transpose(1, 0, 2, 3)

    def merged(rows):
        return rows.transpose(1, 0, 2, 3).reshape(1, BLK, 2 * PG, HD)

    q_rows = by_group(queries[0]).reshape(2, RB, HD)
    cot = by_group(grad_out[0])
    do_rows = jnp.where(valid, cot, jnp.zeros_like(cot)).reshape(2, RB, HD)
    joined = jnp.concatenate([rollout_keys[0], prompt_keys, rollout_values[0], prompt_values])
    joined = lax.optimization_barrier(joined).reshape(2, BLK + 32, 2, HD)
    out, dq, dkv, dprompt = attention(lengths, q_rows, do_rows, joined.transpose(2, 0, 1, 3))
    out = out.reshape(2, BLK, PG, HD)
    dkv = dkv.transpose(1, 2, 0, 3)
    dprompt = dprompt.transpose(1, 2, 0, 3)
    return (
        merged(out),
        merged(dq.reshape(2, BLK, PG, HD)),
        dkv[0][None],
        dkv[1][None],
        dprompt[0],
        dprompt[1],
    )


def solution(mesh):
    rows = P("roll", "seq", "head", None)
    prompt = P(("seq", "roll"), "head", None)
    return jax.shard_map(
        local,
        mesh=mesh,
        in_specs=(rows, rows, rows, prompt, prompt, rows, P("roll")),
        out_specs=(rows, rows, rows, rows, prompt, prompt),
        check_vma=False,
    )
```

```python
import math

import jax
import jax.numpy as jnp
from jax import lax
from jax.experimental import pallas as pl
from jax.experimental.pallas import tpu as pltpu
from jax.sharding import PartitionSpec as P

f32, bf16 = jnp.float32, jnp.bfloat16
N = 16
BLK = 192
PRM = 1024
HD = 128
PG = 8
RB = BLK * PG
TILE = 4 * BLK
HALF = 2 * BLK
RC = RB // 2
SCALE = HD**-0.5
SCALE2 = SCALE * math.log2(math.e)
NEG = -1e30
MESH = pl.DeviceIdType.MESH

NN = (((1,), (0,)), ((), ()))
NT = (((1,), (1,)), ((), ()))
TN = (((0,), (0,)), ((), ()))


F_PROMPT, F_FULL, F_DIAG, F_END, B_PROMPT, B_FULL, B_DIAG = range(7)
W_ROLL, W_Q, W_DO, W_TILE, SEND, DQ, GPY, PASS = (1 << i for i in range(8))


def schedule(x):
    low, top = min(x, 3 - x), max(x, 3 - x)
    late = 1 if x < 2 else 0
    steps = []

    def forward(b, tiles, waits):
        for t in tiles:
            last = top if b == late else low
            steps.append((F_DIAG if t == last else F_FULL, b, t, W_TILE if t in waits else 0))

    def prompt(b):
        steps.append((F_PROMPT, b, 0, W_Q if b else 0))
        steps.append((F_PROMPT, b, 1, 0 if b else W_ROLL))

    def backward_low(b):
        steps.append((B_PROMPT, b, 0, 0))
        for t in range(low + 1):
            last = t == low
            steps.append((B_DIAG if last else B_FULL, b, t, DQ if last else 0))

    prompt(0)
    if late:
        forward(0, range(low + 1), range(low + 1))
        steps.append((F_END, 0, 0, 0))
        backward_low(0)
        prompt(1)
        forward(1, range(top + 1), range(low + 1, top + 1))
        steps.append((F_END, 1, 0, W_DO))
    else:
        forward(0, (0, 1), (0, 1))
        prompt(1)
        forward(0, range(2, top + 1), range(2, top + 1))
        steps.append((F_END, 0, 0, 0))
        forward(1, range(low + 1), ())
        steps.append((F_END, 1, 0, W_DO))
        backward_low(1)
    order = [t for t in range(top, -1, -1) if t != x] + [x]
    prompt_at = len(order) - (1 if x < 2 else 2)
    sent = None
    for i, t in enumerate(order):
        if i == prompt_at:
            steps.append((B_PROMPT, late, 0, GPY | PASS * (1 + sent)))
            sent = None
        flags = SEND | (0 if sent is None else PASS * (1 + sent)) | (DQ if i == len(order) - 1 else 0)
        steps.append((B_DIAG if t == top else B_FULL, late, t, flags))
        sent = t
    return [kind + 8 * b + 16 * t + 64 * flags for kind, b, t, flags in steps]


def dot(a, b, dims=NN):
    return lax.dot_general(a, b, dims, preferred_element_type=f32)


def kernel(
    length, q_in, do_in, kvp_in,
    out, dq, dkv_out, dp_out,
    q2, do2, kv, acc, mx, tot, lse, off, o16, dk, dv, g16,
    zr, yrp, gyp, zrp, gx, gxp, xr, xrp,
    lsem, kvxs, kvxr, kvzs, kvzr, ppxs, ppxr, ppzs, ppzr, ppys, ppyr, qsem, osem,
    dsem, gzs, gzr, gpys, gpzs, gpzr, gxs, gxr, gpxs, gpxr,
):
    s = lax.axis_index("seq")
    r = lax.axis_index("roll")
    x, z = s // 4, s % 4
    kv_in = kvp_in.at[:, :, pl.ds(0, BLK), :]
    pk_in = kvp_in.at[:, :, pl.ds(BLK, 32), :]
    hs = x // 2
    top = jnp.maximum(x, 3 - x)
    partner = 4 * (3 - x) + z

    barrier = pltpu.get_barrier_semaphore()
    for d in range(1, 4):
        pl.semaphore_signal(barrier, inc=1, device_id={"seq": (x + d) % 4 * 4 + z}, device_id_type=MESH)
        pl.semaphore_signal(barrier, inc=1, device_id={"seq": 4 * x + (z + d) % 4}, device_id_type=MESH)
    pl.semaphore_signal(barrier, inc=1, device_id={"roll": 1 - r}, device_id_type=MESH)

    def remote(src, dst, ssem, rsem, **where):
        return pltpu.make_async_remote_copy(
            src_ref=src, dst_ref=dst, send_sem=ssem, recv_sem=rsem,
            device_id=where, device_id_type=MESH,
        )

    def kv_rows(j):
        return kv.at[:, pl.ds(pl.multiple_of(PRM + j * BLK, 64), BLK), :]

    def p_rows(xx):
        return kv.at[:, pl.ds(pl.multiple_of(r * 512 + z * 128 + xx * 32, 32), 32), :]

    def p_column(rr, zz):
        return kv.at[:, pl.ds(pl.multiple_of(rr * 512 + zz * 128, 128), 128), :]

    own_p = pltpu.make_async_copy(pk_in.at[hs], p_rows(x), lsem.at[3])
    own_p.start()
    own_kv = pltpu.make_async_copy(kv_in.at[hs], kv_rows(s), lsem.at[2])
    own_kv.start()
    own_q = pltpu.make_async_copy(q_in.at[hs], q2.at[0], lsem.at[0])
    own_q.start()
    own_do = pltpu.make_async_copy(do_in.at[hs], do2.at[0], lsem.at[1])
    own_do.start()
    pl.semaphore_wait(barrier, 7)

    def kvx_copy(xx):
        return remote(kv_in.at[xx // 2], kv_rows(s), kvxs.at[xx], kvxr.at[x], seq=4 * xx + z)

    def px_copy(xx):
        return remote(pk_in.at[xx // 2], p_rows(x), ppxs.at[xx], ppxr.at[x], seq=4 * xx + z)

    def pz_copy(zz):
        return remote(p_column(r, z), p_column(r, z), ppzs.at[zz], ppzr.at[z], seq=4 * x + zz)

    def py_copy(zz):
        return remote(p_column(r, zz), p_column(r, zz), ppys.at[zz], ppyr.at[zz], roll=1 - r)

    def kvz_copy(zz, tile):
        rows = kv_rows(4 * tile + z)
        return remote(rows, rows, kvzs.at[zz, tile], kvzr.at[z, tile], seq=4 * x + zz)

    def uses(zz, tile, other):
        return (tile != top) | (other <= zz // 2 * 2 + 1)

    def gives(zz, tile, other):
        return (tile != top) | (other < zz)

    def sees(xx):
        return x <= jnp.maximum(xx, 3 - xx)

    @pl.loop(1, 4)
    def _(d):
        px_copy((x + d) % 4).start()

    @pl.loop(1, 4)
    def _(d):
        xx = (x + d) % 4

        @pl.when(sees(xx))
        def _():
            kvx_copy(xx).start()

    q_out = remote(q_in.at[1 - hs], q2.at[1], qsem.at[0], qsem.at[1], seq=partner)
    q_out.start()
    acc[...] = jnp.zeros_like(acc)
    mx[...] = jnp.full_like(mx, NEG)
    tot[...] = jnp.zeros_like(tot)
    dk[...] = jnp.zeros_like(dk)
    dv[...] = jnp.zeros_like(dv)
    own_p.wait()

    @pl.loop(1, 4)
    def _(d):
        xx = (x + d) % 4
        remote(pk_in.at[hs], p_rows(xx), ppxs.at[xx], ppxr.at[xx], seq=4 * xx + z).wait_recv()

    @pl.loop(1, 4)
    def _(d):
        pz_copy((z + d) % 4).start()

    py_copy(z).start()
    own_kv.wait()

    @pl.loop(0, top + 1)
    def _(tile):
        @pl.when(tile != x)
        def _():
            remote(kv_in.at[hs], kv_rows(4 * tile + z), kvxs.at[tile], kvxr.at[tile], seq=4 * tile + z).wait_recv()

        @pl.loop(1, 4)
        def _(d):
            @pl.when(uses((z + d) % 4, tile, z))
            def _():
                kvz_copy((z + d) % 4, tile).start()

    @pl.loop(1, 4)
    def _(d):
        zz = (z + d) % 4
        remote(p_column(r, zz), p_column(r, zz), ppzs.at[zz], ppzr.at[zz], seq=4 * x + zz).wait_recv()
        py_copy(zz).start()

    do_out = remote(do_in.at[1 - hs], do2.at[1], qsem.at[2], qsem.at[3], seq=partner)
    do_out.start()

    def block_of(b):
        return jnp.where(b == 0, s, partner)

    def masked_scores(scores, k0, q0):
        key_pos = k0 - PRM + lax.broadcasted_iota(jnp.int32, scores.shape, 0)
        query_pos = q0 + lax.broadcasted_iota(jnp.int32, scores.shape, 1) // PG
        return jnp.where(key_pos <= query_pos, scores, NEG)

    def forward_tile(b, k0, size, masked):
        rows = pl.ds(pl.multiple_of(k0, 64), size)
        scores = dot(kv[0, rows, :], q2[b], NT) * SCALE2
        if masked:
            scores = masked_scores(scores, k0, block_of(b) * BLK)
        old = mx[b]
        new = jnp.maximum(old, jnp.max(scores, 0, keepdims=True))
        lifted = jnp.exp2(scores - new)
        shrink = jnp.exp2(old - new)
        mx[b] = new
        tot[b] = tot[b] * shrink + jnp.sum(lifted, 0, keepdims=True)
        acc[b] = acc[b] * shrink + dot(kv[1, rows, :], lifted.astype(bf16), TN)

    own_q.wait()
    own_do.wait()

    def wait_tile(tile):
        @pl.loop(1, 4)
        def _(d):
            zz = (z + d) % 4
            rows = kv_rows(4 * tile + zz)

            @pl.when(uses(z, tile, zz))
            def _():
                remote(rows, rows, kvzs.at[zz, tile], kvzr.at[zz, tile], seq=4 * x + zz).wait_recv()

    def backward_tile(b, k0, size, masked, after=lambda c: None):
        rows = pl.ds(pl.multiple_of(k0, 64), size)

        for c in range(RB // RC):
            part = pl.ds(c * RC, RC)
            keys, values = kv[0, rows, :], kv[1, rows, :]
            queries, cot = q2[b, part, :], do2[b, part, :]
            scores = dot(keys, queries, NT) * SCALE2
            if masked:
                scores = masked_scores(scores, k0, block_of(b) * BLK + c * (RC // PG))
            weights = jnp.exp2(scores - lse[b, :, part])
            grads = (weights * (dot(values, cot, NT) - off[b, :, part])).astype(bf16)
            dv[rows, :] += dot(weights.astype(bf16), cot)
            dk[rows, :] += dot(grads, queries)
            acc[b, :, part] += dot(keys, grads, TN)
            after(c)

    def finish_rows(k0, size):
        rows = pl.ds(pl.multiple_of(k0, 64), size)
        g16[0, rows, :] = (dk[rows, :] * SCALE).astype(bf16)
        g16[1, rows, :] = dv[rows, :].astype(bf16)

    def grad_rows(j):
        return pl.ds(pl.multiple_of(PRM + j * BLK, 64), BLK)

    def gz_copy(zz, tile):
        rows = grad_rows(4 * tile + zz)
        return remote(g16.at[:, rows, :], zr.at[z, tile], gzs.at[zz, tile], gzr.at[z, tile], seq=4 * x + zz)

    def gx_copy(tile):
        return remote(gx.at[tile], xr.at[x], gxs.at[tile], gxr.at[x], seq=4 * tile + z)

    def send_tile(tile):
        finish_rows(PRM + tile * TILE, TILE)

        @pl.loop(1, 4)
        def _(d):
            @pl.when(gives(z, tile, (z + d) % 4))
            def _():
                gz_copy((z + d) % 4, tile).start()

    def pass_tile(tile):
        rows = grad_rows(4 * tile + z)
        total = g16[:, rows, :].astype(f32)
        for d in range(1, 4):
            zz = (z + d) % 4
            given = gives(zz, tile, z)

            @pl.when(given)
            def _():
                remote(g16.at[:, rows, :], zr.at[zz, tile], gzs.at[zz, tile], gzr.at[zz, tile], seq=4 * x + zz).wait_recv()

            total = total + jnp.where(given, zr[zz, tile].astype(f32), 0.0)

        @pl.when(tile == x)
        def _():
            xr[x] = total.astype(bf16)

        @pl.when(tile != x)
        def _():
            gx[tile] = total.astype(bf16)
            gx_copy(tile).start()

    mine = pl.ds(pl.multiple_of(r * 512, 512), 512)
    theirs = pl.ds(pl.multiple_of((1 - r) * 512, 512), 512)
    gpy_out = remote(g16.at[:, theirs, :], yrp, gpys.at[0], gpys.at[1], roll=1 - r)

    def gpz_copy(zz):
        rows = pl.ds(pl.multiple_of(zz * 128, 128), 128)
        return remote(gyp.at[:, rows, :], zrp.at[z], gpzs.at[zz], gpzr.at[z], seq=4 * x + zz)

    def gpx_copy(xx):
        rows = pl.ds(pl.multiple_of(xx * 32, 32), 32)
        return remote(gxp.at[:, rows, :], xrp.at[x], gpxs.at[xx], gpxr.at[x], seq=4 * xx + z)

    def pass_rolls():
        gpy_out.wait_recv()
        gyp[0] = (dk[mine, :] * SCALE + yrp[0].astype(f32)).astype(bf16)
        gyp[1] = (dv[mine, :] + yrp[1].astype(f32)).astype(bf16)

        @pl.loop(1, 4)
        def _(d):
            gpz_copy((z + d) % 4).start()

    def pass_prompt():
        rows = pl.ds(pl.multiple_of(z * 128, 128), 128)
        total = gyp[:, rows, :].astype(f32)
        for d in range(1, 4):
            zz = (z + d) % 4
            remote(gyp.at[:, rows, :], zrp.at[zz], gpzs.at[zz], gpzr.at[zz], seq=4 * x + zz).wait_recv()
            total = total + zrp[zz].astype(f32)
        gxp[...] = total.astype(bf16)

        @pl.loop(1, 4)
        def _(d):
            gpx_copy((x + d) % 4).start()

        xrp[x] = gxp[:, pl.ds(pl.multiple_of(x * 32, 32), 32), :]

    def dq_copies(c):
        rows = pl.ds(c * RC, RC)
        return (
            pltpu.make_async_copy(o16.at[2, rows, :], dq.at[hs, rows, :], dsem.at[c]),
            remote(o16.at[3, rows, :], dq.at[hs, rows, :], dsem.at[2 + c], dsem.at[4 + c], seq=partner),
        )

    def send_dq(b, c):
        rows = pl.ds(c * RC, RC)
        o16[2 + b, rows, :] = (acc[b, :, rows] * SCALE).T.astype(bf16)

        @pl.when(b == 0)
        def _():
            dq_copies(c)[0].start()

        @pl.when(b == 1)
        def _():
            dq_copies(c)[1].start()

    own_out = pltpu.make_async_copy(o16.at[0], out.at[hs], lsem.at[4])
    out_out = remote(o16.at[1], out.at[hs], osem.at[0], osem.at[1], seq=partner)
    plans = [schedule(xx) for xx in range(4)]

    @pl.loop(0, len(plans[0]))
    def _(i):
        code = jnp.int32(0)
        for n, column in enumerate(zip(*plans)):
            here = jnp.where(x == 0, column[0], jnp.where(x == 1, column[1], jnp.where(x == 2, column[2], column[3])))
            code = jnp.where(i == n, here, code)
        kind = code % 8
        b = code // 8 % 2
        tile = code // 16 % 4
        flags = code // 64

        def has(flag):
            return flags // flag % 2 == 1

        @pl.when(has(W_Q))
        def _():
            q_out.wait_recv()

        @pl.when(has(W_ROLL))
        def _():
            @pl.loop(0, 4)
            def _(zz):
                rows = p_column(1 - r, zz)
                remote(rows, rows, ppys.at[zz], ppyr.at[zz], roll=1 - r).wait_recv()

        @pl.when(has(W_TILE))
        def _():
            wait_tile(tile)

        @pl.when(has(W_DO))
        def _():
            do_out.wait_recv()

        @pl.when(kind == F_PROMPT)
        def _():
            forward_tile(b, (r + tile) % 2 * 512, 512, False)

        @pl.when(kind == F_FULL)
        def _():
            forward_tile(b, PRM + tile * TILE, TILE, False)

        @pl.when(kind == F_DIAG)
        def _():
            @pl.loop(0, 1 + z // 2)
            def _(half):
                forward_tile(b, PRM + tile * TILE + half * HALF, HALF, True)

        @pl.when(kind == F_END)
        def _():
            total = tot[b]
            normal = acc[b] / total
            lse[b] = mx[b] + jnp.log2(total)
            off[b] = jnp.sum(normal * do2[b].astype(f32).T, 0, keepdims=True)
            row_pos = block_of(b) * BLK + lax.broadcasted_iota(jnp.int32, (1, RB), 1) // PG
            o16[b] = jnp.where(row_pos < length[0], normal, 0.0).T.astype(bf16)
            acc[b] = jnp.zeros(acc.shape[1:], f32)

            @pl.when(b == 0)
            def _():
                own_out.start()

            @pl.when(b == 1)
            def _():
                out_out.start()

        @pl.when(kind == B_PROMPT)
        def _():
            backward_tile(b, 0, PRM, False)

        @pl.when(kind == B_FULL)
        def _():
            def after(c):
                @pl.when(has(DQ))
                def _():
                    send_dq(b, c)

            backward_tile(b, PRM + tile * TILE, TILE, False, after)

        @pl.when(kind == B_DIAG)
        def _():
            @pl.loop(0, 1 + z // 2)
            def _(half):
                backward_tile(b, PRM + tile * TILE + half * HALF, HALF, True)

            @pl.when(has(DQ))
            def _():
                for c in range(RB // RC):
                    send_dq(b, c)

        @pl.when(has(SEND))
        def _():
            send_tile(tile)

        @pl.when(has(GPY))
        def _():
            finish_rows(0, PRM)
            gpy_out.start()

        @pl.when(flags >= PASS)
        def _():
            pass_tile(flags // PASS - 1)

    pass_rolls()
    pass_tile(x)
    pass_prompt()

    @pl.loop(1, 4)
    def _(d):
        xx = (x + d) % 4
        remote(gxp.at[:, pl.ds(0, 32), :], xrp.at[xx], gpxs.at[xx], gpxr.at[xx], seq=4 * xx + z).wait_recv()

    for h in range(2):
        dp_out[h] = (xrp[2 * h].astype(f32) + xrp[2 * h + 1].astype(f32)).astype(bf16)

    @pl.loop(1, 4)
    def _(d):
        xx = (x + d) % 4

        @pl.when(sees(xx))
        def _():
            remote(gx.at[xx], xr.at[xx], gxs.at[xx], gxr.at[xx], seq=4 * xx + z).wait_recv()

    for h in range(2):
        total = jnp.zeros(xr.shape[1:], f32)
        for xx in (2 * h, 2 * h + 1):
            total = total + jnp.where(x <= max(xx, 3 - xx), xr[xx].astype(f32), 0.0)
        dkv_out[h] = total.astype(bf16)

    py_copy(z).wait_send()
    gpy_out.wait_send()
    q_out.wait_send()
    do_out.wait_send()
    out_out.wait()
    own_out.wait()
    for c in range(RB // RC):
        for copy in dq_copies(c):
            copy.wait()

    @pl.loop(1, 4)
    def _(d):
        xx = (x + d) % 4
        zz = (z + d) % 4
        px_copy(xx).wait_send()
        pz_copy(zz).wait_send()
        py_copy(zz).wait_send()
        gpz_copy(zz).wait_send()
        gpx_copy(xx).wait_send()

        @pl.when(sees(xx))
        def _():
            kvx_copy(xx).wait_send()

        @pl.when(xx <= top)
        def _():
            gx_copy(xx).wait_send()

        @pl.loop(0, top + 1)
        def _(tile):
            @pl.when(uses(zz, tile, z))
            def _():
                kvz_copy(zz, tile).wait_send()

            @pl.when(gives(z, tile, zz))
            def _():
                gz_copy(zz, tile).wait_send()


def attention(lengths, q_rows, do_rows, kvp_rows):
    any_spec = pl.BlockSpec(memory_space=pl.ANY)
    vmem = pl.BlockSpec(memory_space=pltpu.VMEM)
    dma = pltpu.SemaphoreType.DMA
    return pl.pallas_call(
        kernel,
        out_shape=[
            jax.ShapeDtypeStruct((2, RB, HD), bf16),
            jax.ShapeDtypeStruct((2, RB, HD), bf16),
            jax.ShapeDtypeStruct((2, 2, BLK, HD), bf16),
            jax.ShapeDtypeStruct((2, 2, 32, HD), bf16),
        ],
        in_specs=[pl.BlockSpec(memory_space=pltpu.SMEM)] + [any_spec] * 3,
        out_specs=[any_spec, any_spec, vmem, vmem],
        scratch_shapes=[
            pltpu.VMEM((2, RB, HD), bf16),
            pltpu.VMEM((2, RB, HD), bf16),
            pltpu.VMEM((2, PRM + N * BLK, HD), bf16),
            pltpu.VMEM((2, HD, RB), f32),
            pltpu.VMEM((2, 1, RB), f32),
            pltpu.VMEM((2, 1, RB), f32),
            pltpu.VMEM((2, 1, RB), f32),
            pltpu.VMEM((2, 1, RB), f32),
            pltpu.VMEM((4, RB, HD), bf16),
            pltpu.VMEM((PRM + N * BLK, HD), f32),
            pltpu.VMEM((PRM + N * BLK, HD), f32),
            pltpu.VMEM((2, PRM + N * BLK, HD), bf16),
            pltpu.VMEM((4, 4, 2, BLK, HD), bf16),
            pltpu.VMEM((2, 512, HD), bf16),
            pltpu.VMEM((2, 512, HD), bf16),
            pltpu.VMEM((4, 2, 128, HD), bf16),
            pltpu.VMEM((4, 2, BLK, HD), bf16),
            pltpu.VMEM((2, 128, HD), bf16),
            pltpu.VMEM((4, 2, BLK, HD), bf16),
            pltpu.VMEM((4, 2, 32, HD), bf16),
            dma((8,)),
            dma((4,)),
            dma((4,)),
            dma((4, 4)),
            dma((4, 4)),
            dma((4,)),
            dma((4,)),
            dma((4,)),
            dma((4,)),
            dma((4,)),
            dma((4,)),
            dma((4,)),
            dma((2,)),
            dma((6,)),
            dma((4, 4)),
            dma((4, 4)),
            dma((2,)),
            dma((4,)),
            dma((4,)),
            dma((4,)),
            dma((4,)),
            dma((4,)),
            dma((4,)),
        ],
        compiler_params=pltpu.CompilerParams(
            collective_id=0, has_side_effects=True, vmem_limit_bytes=58 * 2**20
        ),
    )(lengths, q_rows, do_rows, kvp_rows)


def local(queries, rollout_keys, rollout_values, prompt_keys, prompt_values, grad_out, lengths):
    first_row = lax.axis_index("seq") * BLK
    valid = ((first_row + jnp.arange(BLK, dtype=jnp.int32)) < lengths[0])[None, :, None, None]

    def by_group(rows):
        return rows.reshape(BLK, 2, PG, HD).transpose(1, 0, 2, 3)

    def merged(rows):
        return rows.transpose(1, 0, 2, 3).reshape(1, BLK, 2 * PG, HD)

    q_rows = by_group(queries[0]).reshape(2, RB, HD)
    cot = by_group(grad_out[0])
    do_rows = jnp.where(valid, cot, jnp.zeros_like(cot)).reshape(2, RB, HD)
    joined = jnp.concatenate([rollout_keys[0], prompt_keys, rollout_values[0], prompt_values])
    joined = lax.optimization_barrier(joined).reshape(2, BLK + 32, 2, HD)
    out, dq, dkv, dprompt = attention(lengths, q_rows, do_rows, joined.transpose(2, 0, 1, 3))
    out = out.reshape(2, BLK, PG, HD)
    dkv = dkv.transpose(1, 2, 0, 3)
    dprompt = dprompt.transpose(1, 2, 0, 3)
    return (
        merged(out),
        merged(dq.reshape(2, BLK, PG, HD)),
        dkv[0][None],
        dkv[1][None],
        dprompt[0],
        dprompt[1],
    )


def solution(mesh):
    rows = P("roll", "seq", "head", None)
    prompt = P(("seq", "roll"), "head", None)
    return jax.shard_map(
        local,
        mesh=mesh,
        in_specs=(rows, rows, rows, prompt, prompt, rows, P("roll")),
        out_specs=(rows, rows, rows, rows, prompt, prompt),
        check_vma=False,
    )
```

```python
import math

import jax
import jax.numpy as jnp
from jax import lax
from jax.experimental import pallas as pl
from jax.experimental.pallas import tpu as pltpu
from jax.sharding import PartitionSpec as P

f32, bf16 = jnp.float32, jnp.bfloat16
N = 16
BLK = 192
PRM = 1024
HD = 128
PG = 8
RB = BLK * PG
TILE = 4 * BLK
HALF = 2 * BLK
RC = RB // 2
SCALE = HD**-0.5
SCALE2 = SCALE * math.log2(math.e)
NEG = -1e30
MESH = pl.DeviceIdType.MESH

NN = (((1,), (0,)), ((), ()))
NT = (((1,), (1,)), ((), ()))
TN = (((0,), (0,)), ((), ()))


F_PROMPT, F_FULL, F_DIAG, F_END, B_PROMPT, B_FULL, B_DIAG = range(7)
W_ROLL, W_Q, W_DO, W_TILE, SEND, DQ, GPY, PASS = (1 << i for i in range(8))


def schedule(x):
    low, top = min(x, 3 - x), max(x, 3 - x)
    late = 1 if x < 2 else 0
    steps = []

    def forward(b, tiles, waits):
        for t in tiles:
            last = top if b == late else low
            steps.append((F_DIAG if t == last else F_FULL, b, t, W_TILE if t in waits else 0))

    def prompt(b):
        steps.append((F_PROMPT, b, 0, W_Q if b else 0))
        steps.append((F_PROMPT, b, 1, 0 if b else W_ROLL))

    def backward_low(b):
        steps.append((B_PROMPT, b, 0, 0))
        for t in range(low + 1):
            last = t == low
            steps.append((B_DIAG if last else B_FULL, b, t, DQ if last else 0))

    prompt(0)
    if late:
        forward(0, range(low + 1), range(low + 1))
        steps.append((F_END, 0, 0, 0))
        backward_low(0)
        prompt(1)
        forward(1, range(top + 1), range(low + 1, top + 1))
        steps.append((F_END, 1, 0, W_DO))
    else:
        forward(0, (0, 1), (0, 1))
        prompt(1)
        forward(0, range(2, top + 1), range(2, top + 1))
        steps.append((F_END, 0, 0, 0))
        forward(1, range(low + 1), ())
        steps.append((F_END, 1, 0, W_DO))
        backward_low(1)
    order = [t for t in range(top, -1, -1) if t != x] + [x]
    prompt_at = len(order) - (1 if x < 2 else 2)
    waiting = []
    for i, t in enumerate(order):
        if i == prompt_at:
            ready = waiting.pop(0) if waiting and waiting[0][1] <= len(steps) - 2 else None
            steps.append((B_PROMPT, late, 0, GPY + PASS * (0 if ready is None else 1 + ready[0])))
        final = i == len(order) - 1
        ready = waiting.pop(0) if waiting and (final or waiting[0][1] <= len(steps) - 2) else None
        flags = SEND + PASS * (0 if ready is None else 1 + ready[0]) + (DQ if final else 0)
        waiting.append((t, len(steps)))
        steps.append((B_DIAG if t == top else B_FULL, late, t, flags))
    assert [t for t, _ in waiting] == [x]
    return [kind + 8 * b + 16 * t + 64 * flags for kind, b, t, flags in steps]


def dot(a, b, dims=NN):
    return lax.dot_general(a, b, dims, preferred_element_type=f32)


def kernel(
    length, q_in, do_in, kvp_in,
    out, dq, dkv_out, dp_out,
    raw, q2, do2, kv, acc, mx, tot, lse, off, o16, dk, dv, g16,
    zr, yrp, gyp, zrp, gx, gxp, xr, xrp,
    lsem, kvxs, kvxr, kvzs, kvzr, ppxs, ppxr, ppzs, ppzr, ppys, ppyr, qsem, osem,
    dsem, gzs, gzr, gpys, gpzs, gpzr, gxs, gxr, gpxs, gpxr,
):
    s = lax.axis_index("seq")
    r = lax.axis_index("roll")
    x, z = s // 4, s % 4
    kv_in = kvp_in.at[:, :, pl.ds(0, BLK), :]
    pk_in = kvp_in.at[:, :, pl.ds(BLK, 32), :]
    hs = x // 2
    top = jnp.maximum(x, 3 - x)
    partner = 4 * (3 - x) + z

    barrier = pltpu.get_barrier_semaphore()
    for d in range(1, 4):
        pl.semaphore_signal(barrier, inc=1, device_id={"seq": (x + d) % 4 * 4 + z}, device_id_type=MESH)
        pl.semaphore_signal(barrier, inc=1, device_id={"seq": 4 * x + (z + d) % 4}, device_id_type=MESH)
    pl.semaphore_signal(barrier, inc=1, device_id={"roll": 1 - r}, device_id_type=MESH)

    def remote(src, dst, ssem, rsem, **where):
        return pltpu.make_async_remote_copy(
            src_ref=src, dst_ref=dst, send_sem=ssem, recv_sem=rsem,
            device_id=where, device_id_type=MESH,
        )

    def kv_rows(j):
        return kv.at[:, pl.ds(pl.multiple_of(PRM + j * BLK, 64), BLK), :]

    def p_rows(xx):
        return kv.at[:, pl.ds(pl.multiple_of(r * 512 + z * 128 + xx * 32, 32), 32), :]

    def p_column(rr, zz):
        return kv.at[:, pl.ds(pl.multiple_of(rr * 512 + zz * 128, 128), 128), :]

    own_p = pltpu.make_async_copy(pk_in.at[hs], p_rows(x), lsem.at[3])
    own_p.start()
    own_kv = pltpu.make_async_copy(kv_in.at[hs], kv_rows(s), lsem.at[2])
    own_kv.start()
    own_q = pltpu.make_async_copy(q_in.at[:, hs], raw.at[0, 0], lsem.at[0])
    own_q.start()
    own_do = pltpu.make_async_copy(do_in.at[:, hs], raw.at[1, 0], lsem.at[1])
    own_do.start()
    pl.semaphore_wait(barrier, 7)

    def kvx_copy(xx):
        return remote(kv_in.at[xx // 2], kv_rows(s), kvxs.at[xx], kvxr.at[x], seq=4 * xx + z)

    def px_copy(xx):
        return remote(pk_in.at[xx // 2], p_rows(x), ppxs.at[xx], ppxr.at[x], seq=4 * xx + z)

    def pz_copy(zz):
        return remote(p_column(r, z), p_column(r, z), ppzs.at[zz], ppzr.at[z], seq=4 * x + zz)

    def py_copy(zz):
        return remote(p_column(r, zz), p_column(r, zz), ppys.at[zz], ppyr.at[zz], roll=1 - r)

    def kvz_copy(zz, tile):
        rows = kv_rows(4 * tile + z)
        return remote(rows, rows, kvzs.at[zz, tile], kvzr.at[z, tile], seq=4 * x + zz)

    def uses(zz, tile, other):
        return (tile != top) | (other <= zz // 2 * 2 + 1)

    def gives(zz, tile, other):
        return (tile != top) | (other < zz)

    def sees(xx):
        return x <= jnp.maximum(xx, 3 - xx)

    @pl.loop(1, 4)
    def _(d):
        px_copy((x + d) % 4).start()

    @pl.loop(1, 4)
    def _(d):
        xx = (x + d) % 4

        @pl.when(sees(xx))
        def _():
            kvx_copy(xx).start()

    q_out = remote(q_in.at[:, 1 - hs], raw.at[0, 1], qsem.at[0], qsem.at[1], seq=partner)
    q_out.start()
    acc[...] = jnp.zeros_like(acc)
    mx[...] = jnp.full_like(mx, NEG)
    tot[...] = jnp.zeros_like(tot)
    dk[...] = jnp.zeros_like(dk)
    dv[...] = jnp.zeros_like(dv)
    own_p.wait()

    @pl.loop(1, 4)
    def _(d):
        xx = (x + d) % 4
        remote(pk_in.at[hs], p_rows(xx), ppxs.at[xx], ppxr.at[xx], seq=4 * xx + z).wait_recv()

    @pl.loop(1, 4)
    def _(d):
        pz_copy((z + d) % 4).start()

    py_copy(z).start()
    own_kv.wait()

    @pl.loop(0, top + 1)
    def _(tile):
        @pl.when(tile != x)
        def _():
            remote(kv_in.at[hs], kv_rows(4 * tile + z), kvxs.at[tile], kvxr.at[tile], seq=4 * tile + z).wait_recv()

        @pl.loop(1, 4)
        def _(d):
            @pl.when(uses((z + d) % 4, tile, z))
            def _():
                kvz_copy((z + d) % 4, tile).start()

    @pl.loop(1, 4)
    def _(d):
        zz = (z + d) % 4
        remote(p_column(r, zz), p_column(r, zz), ppzs.at[zz], ppzr.at[zz], seq=4 * x + zz).wait_recv()
        py_copy(zz).start()

    do_out = remote(do_in.at[:, 1 - hs], raw.at[1, 1], qsem.at[2], qsem.at[3], seq=partner)
    do_out.start()

    def block_of(b):
        return jnp.where(b == 0, s, partner)

    def masked_scores(scores, k0, q0):
        key_pos = k0 - PRM + lax.broadcasted_iota(jnp.int32, scores.shape, 0)
        query_pos = q0 + lax.broadcasted_iota(jnp.int32, scores.shape, 1) // PG
        return jnp.where(key_pos <= query_pos, scores, NEG)

    def forward_tile(b, k0, size, masked):
        rows = pl.ds(pl.multiple_of(k0, 64), size)
        scores = dot(kv[0, rows, :], q2[b], NT) * SCALE2
        if masked:
            scores = masked_scores(scores, k0, block_of(b) * BLK)
        old = mx[b]
        new = jnp.maximum(old, jnp.max(scores, 0, keepdims=True))
        lifted = jnp.exp2(scores - new)
        shrink = jnp.exp2(old - new)
        mx[b] = new
        tot[b] = tot[b] * shrink + jnp.sum(lifted, 0, keepdims=True)
        acc[b] = acc[b] * shrink + dot(kv[1, rows, :], lifted.astype(bf16), TN)

    def take_q(b):
        q2[b] = raw[0, b].reshape(RB, HD)

    def take_do(b):
        row_pos = block_of(b) * BLK + lax.broadcasted_iota(jnp.int32, (RB, HD), 0) // PG
        rows = raw[1, b].reshape(RB, HD).astype(f32)
        do2[b] = jnp.where(row_pos < length[0], rows, 0.0).astype(bf16)

    own_q.wait()
    take_q(0)
    own_do.wait()
    take_do(0)

    def wait_tile(tile):
        @pl.loop(1, 4)
        def _(d):
            zz = (z + d) % 4
            rows = kv_rows(4 * tile + zz)

            @pl.when(uses(z, tile, zz))
            def _():
                remote(rows, rows, kvzs.at[zz, tile], kvzr.at[zz, tile], seq=4 * x + zz).wait_recv()

    def backward_tile(b, k0, size, masked, after=lambda c: None):
        rows = pl.ds(pl.multiple_of(k0, 64), size)

        for c in range(RB // RC):
            part = pl.ds(c * RC, RC)
            keys, values = kv[0, rows, :], kv[1, rows, :]
            queries, cot = q2[b, part, :], do2[b, part, :]
            scores = dot(keys, queries, NT) * SCALE2
            if masked:
                scores = masked_scores(scores, k0, block_of(b) * BLK + c * (RC // PG))
            weights = jnp.exp2(scores - lse[b, :, part])
            grads = (weights * (dot(values, cot, NT) - off[b, :, part])).astype(bf16)
            dv[rows, :] += dot(weights.astype(bf16), cot)
            dk[rows, :] += dot(grads, queries)
            acc[b, :, part] += dot(keys, grads, TN)
            after(c)

    def finish_rows(k0, size):
        rows = pl.ds(pl.multiple_of(k0, 64), size)
        g16[0, rows, :] = (dk[rows, :] * SCALE).astype(bf16)
        g16[1, rows, :] = dv[rows, :].astype(bf16)

    def grad_rows(j):
        return pl.ds(pl.multiple_of(PRM + j * BLK, 64), BLK)

    def gz_copy(zz, tile):
        rows = grad_rows(4 * tile + zz)
        return remote(g16.at[:, rows, :], zr.at[z, tile], gzs.at[zz, tile], gzr.at[z, tile], seq=4 * x + zz)

    def gx_copy(tile):
        return remote(gx.at[tile], xr.at[x], gxs.at[tile], gxr.at[x], seq=4 * tile + z)

    def send_tile(tile):
        finish_rows(PRM + tile * TILE, TILE)

        @pl.loop(1, 4)
        def _(d):
            @pl.when(gives(z, tile, (z + d) % 4))
            def _():
                gz_copy((z + d) % 4, tile).start()

    def pass_tile(tile):
        rows = grad_rows(4 * tile + z)
        total = g16[:, rows, :].astype(f32)
        for d in range(1, 4):
            zz = (z + d) % 4
            given = gives(zz, tile, z)

            @pl.when(given)
            def _():
                remote(g16.at[:, rows, :], zr.at[zz, tile], gzs.at[zz, tile], gzr.at[zz, tile], seq=4 * x + zz).wait_recv()

            total = total + jnp.where(given, zr[zz, tile].astype(f32), 0.0)

        @pl.when(tile == x)
        def _():
            xr[x] = total.astype(bf16)

        @pl.when(tile != x)
        def _():
            gx[tile] = total.astype(bf16)
            gx_copy(tile).start()

    mine = pl.ds(pl.multiple_of(r * 512, 512), 512)
    theirs = pl.ds(pl.multiple_of((1 - r) * 512, 512), 512)
    gpy_out = remote(g16.at[:, theirs, :], yrp, gpys.at[0], gpys.at[1], roll=1 - r)

    def gpz_copy(zz):
        rows = pl.ds(pl.multiple_of(zz * 128, 128), 128)
        return remote(gyp.at[:, rows, :], zrp.at[z], gpzs.at[zz], gpzr.at[z], seq=4 * x + zz)

    def gpx_copy(xx):
        rows = pl.ds(pl.multiple_of(xx * 32, 32), 32)
        return remote(gxp.at[:, rows, :], xrp.at[x], gpxs.at[xx], gpxr.at[x], seq=4 * xx + z)

    def pass_rolls():
        gpy_out.wait_recv()
        gyp[0] = (dk[mine, :] * SCALE + yrp[0].astype(f32)).astype(bf16)
        gyp[1] = (dv[mine, :] + yrp[1].astype(f32)).astype(bf16)

        @pl.loop(1, 4)
        def _(d):
            gpz_copy((z + d) % 4).start()

    def pass_prompt():
        rows = pl.ds(pl.multiple_of(z * 128, 128), 128)
        total = gyp[:, rows, :].astype(f32)
        for d in range(1, 4):
            zz = (z + d) % 4
            remote(gyp.at[:, rows, :], zrp.at[zz], gpzs.at[zz], gpzr.at[zz], seq=4 * x + zz).wait_recv()
            total = total + zrp[zz].astype(f32)
        gxp[...] = total.astype(bf16)

        @pl.loop(1, 4)
        def _(d):
            gpx_copy((x + d) % 4).start()

        xrp[x] = gxp[:, pl.ds(pl.multiple_of(x * 32, 32), 32), :]

    def dq_copies(c):
        rows = pl.ds(c * (RC // PG), RC // PG)
        return (
            pltpu.make_async_copy(o16.at[2, rows], dq.at[rows, hs], dsem.at[c]),
            remote(o16.at[3, rows], dq.at[rows, hs], dsem.at[2 + c], dsem.at[4 + c], seq=partner),
        )

    def send_dq(b, c):
        part = (acc[b, :, pl.ds(c * RC, RC)] * SCALE).T.astype(bf16)
        o16[2 + b, pl.ds(c * (RC // PG), RC // PG)] = part.reshape(RC // PG, PG, HD)

        @pl.when(b == 0)
        def _():
            dq_copies(c)[0].start()

        @pl.when(b == 1)
        def _():
            dq_copies(c)[1].start()

    own_out = pltpu.make_async_copy(o16.at[0], out.at[:, hs], lsem.at[4])
    out_out = remote(o16.at[1], out.at[:, hs], osem.at[0], osem.at[1], seq=partner)
    plans = [schedule(xx) for xx in range(4)]

    @pl.loop(0, len(plans[0]))
    def _(i):
        code = jnp.int32(0)
        for n, column in enumerate(zip(*plans)):
            here = jnp.where(x == 0, column[0], jnp.where(x == 1, column[1], jnp.where(x == 2, column[2], column[3])))
            code = jnp.where(i == n, here, code)
        kind = code % 8
        b = code // 8 % 2
        tile = code // 16 % 4
        flags = code // 64

        def has(flag):
            return flags // flag % 2 == 1

        @pl.when(has(W_Q))
        def _():
            q_out.wait_recv()
            take_q(1)

        @pl.when(has(W_ROLL))
        def _():
            @pl.loop(0, 4)
            def _(zz):
                rows = p_column(1 - r, zz)
                remote(rows, rows, ppys.at[zz], ppyr.at[zz], roll=1 - r).wait_recv()

        @pl.when(has(W_TILE))
        def _():
            wait_tile(tile)

        @pl.when(has(W_DO))
        def _():
            do_out.wait_recv()
            take_do(1)

        @pl.when(kind == F_PROMPT)
        def _():
            forward_tile(b, (r + tile) % 2 * 512, 512, False)

        @pl.when(kind == F_FULL)
        def _():
            forward_tile(b, PRM + tile * TILE, TILE, False)

        @pl.when(kind == F_DIAG)
        def _():
            @pl.loop(0, 1 + z // 2)
            def _(half):
                forward_tile(b, PRM + tile * TILE + half * HALF, HALF, True)

        @pl.when(kind == F_END)
        def _():
            total = tot[b]
            normal = acc[b] / total
            lse[b] = mx[b] + jnp.log2(total)
            off[b] = jnp.sum(normal * do2[b].astype(f32).T, 0, keepdims=True)
            row_pos = block_of(b) * BLK + lax.broadcasted_iota(jnp.int32, (1, RB), 1) // PG
            o16[b] = jnp.where(row_pos < length[0], normal, 0.0).T.astype(bf16).reshape(BLK, PG, HD)
            acc[b] = jnp.zeros(acc.shape[1:], f32)

            @pl.when(b == 0)
            def _():
                own_out.start()

            @pl.when(b == 1)
            def _():
                out_out.start()

        @pl.when(kind == B_PROMPT)
        def _():
            backward_tile(b, 0, PRM, False)

        @pl.when(kind == B_FULL)
        def _():
            def after(c):
                @pl.when(has(DQ))
                def _():
                    send_dq(b, c)

            backward_tile(b, PRM + tile * TILE, TILE, False, after)

        @pl.when(kind == B_DIAG)
        def _():
            @pl.loop(0, 1 + z // 2)
            def _(half):
                backward_tile(b, PRM + tile * TILE + half * HALF, HALF, True)

            @pl.when(has(DQ))
            def _():
                for c in range(RB // RC):
                    send_dq(b, c)

        @pl.when(has(SEND))
        def _():
            send_tile(tile)

        @pl.when(has(GPY))
        def _():
            finish_rows(0, PRM)
            gpy_out.start()

        @pl.when(flags >= PASS)
        def _():
            pass_tile(flags // PASS - 1)

    pass_rolls()
    pass_tile(x)
    pass_prompt()

    @pl.loop(1, 4)
    def _(d):
        xx = (x + d) % 4
        remote(gxp.at[:, pl.ds(0, 32), :], xrp.at[xx], gpxs.at[xx], gpxr.at[xx], seq=4 * xx + z).wait_recv()

    for h in range(2):
        dp_out[h] = (xrp[2 * h].astype(f32) + xrp[2 * h + 1].astype(f32)).astype(bf16)

    @pl.loop(1, 4)
    def _(d):
        xx = (x + d) % 4

        @pl.when(sees(xx))
        def _():
            remote(gx.at[xx], xr.at[xx], gxs.at[xx], gxr.at[xx], seq=4 * xx + z).wait_recv()

    for h in range(2):
        total = jnp.zeros(xr.shape[1:], f32)
        for xx in (2 * h, 2 * h + 1):
            total = total + jnp.where(x <= max(xx, 3 - xx), xr[xx].astype(f32), 0.0)
        dkv_out[h] = total.astype(bf16)

    py_copy(z).wait_send()
    gpy_out.wait_send()
    q_out.wait_send()
    do_out.wait_send()
    out_out.wait()
    own_out.wait()
    for c in range(RB // RC):
        for copy in dq_copies(c):
            copy.wait()

    @pl.loop(1, 4)
    def _(d):
        xx = (x + d) % 4
        zz = (z + d) % 4
        px_copy(xx).wait_send()
        pz_copy(zz).wait_send()
        py_copy(zz).wait_send()
        gpz_copy(zz).wait_send()
        gpx_copy(xx).wait_send()

        @pl.when(sees(xx))
        def _():
            kvx_copy(xx).wait_send()

        @pl.when(xx <= top)
        def _():
            gx_copy(xx).wait_send()

        @pl.loop(0, top + 1)
        def _(tile):
            @pl.when(uses(zz, tile, z))
            def _():
                kvz_copy(zz, tile).wait_send()

            @pl.when(gives(z, tile, zz))
            def _():
                gz_copy(zz, tile).wait_send()


def attention(lengths, q_rows, do_rows, kvp_rows):
    any_spec = pl.BlockSpec(memory_space=pl.ANY)
    vmem = pl.BlockSpec(memory_space=pltpu.VMEM)
    dma = pltpu.SemaphoreType.DMA
    return pl.pallas_call(
        kernel,
        out_shape=[
            jax.ShapeDtypeStruct((BLK, 2, PG, HD), bf16),
            jax.ShapeDtypeStruct((BLK, 2, PG, HD), bf16),
            jax.ShapeDtypeStruct((2, 2, BLK, HD), bf16),
            jax.ShapeDtypeStruct((2, 2, 32, HD), bf16),
        ],
        in_specs=[pl.BlockSpec(memory_space=pltpu.SMEM)] + [any_spec] * 3,
        out_specs=[any_spec, any_spec, vmem, vmem],
        scratch_shapes=[
            pltpu.VMEM((2, 2, BLK, PG, HD), bf16),
            pltpu.VMEM((2, RB, HD), bf16),
            pltpu.VMEM((2, RB, HD), bf16),
            pltpu.VMEM((2, PRM + N * BLK, HD), bf16),
            pltpu.VMEM((2, HD, RB), f32),
            pltpu.VMEM((2, 1, RB), f32),
            pltpu.VMEM((2, 1, RB), f32),
            pltpu.VMEM((2, 1, RB), f32),
            pltpu.VMEM((2, 1, RB), f32),
            pltpu.VMEM((4, BLK, PG, HD), bf16),
            pltpu.VMEM((PRM + N * BLK, HD), f32),
            pltpu.VMEM((PRM + N * BLK, HD), f32),
            pltpu.VMEM((2, PRM + N * BLK, HD), bf16),
            pltpu.VMEM((4, 4, 2, BLK, HD), bf16),
            pltpu.VMEM((2, 512, HD), bf16),
            pltpu.VMEM((2, 512, HD), bf16),
            pltpu.VMEM((4, 2, 128, HD), bf16),
            pltpu.VMEM((4, 2, BLK, HD), bf16),
            pltpu.VMEM((2, 128, HD), bf16),
            pltpu.VMEM((4, 2, BLK, HD), bf16),
            pltpu.VMEM((4, 2, 32, HD), bf16),
            dma((8,)),
            dma((4,)),
            dma((4,)),
            dma((4, 4)),
            dma((4, 4)),
            dma((4,)),
            dma((4,)),
            dma((4,)),
            dma((4,)),
            dma((4,)),
            dma((4,)),
            dma((4,)),
            dma((2,)),
            dma((6,)),
            dma((4, 4)),
            dma((4, 4)),
            dma((2,)),
            dma((4,)),
            dma((4,)),
            dma((4,)),
            dma((4,)),
            dma((4,)),
            dma((4,)),
        ],
        compiler_params=pltpu.CompilerParams(
            collective_id=0, has_side_effects=True, vmem_limit_bytes=58 * 2**20
        ),
    )(lengths, q_rows, do_rows, kvp_rows)


def local(queries, rollout_keys, rollout_values, prompt_keys, prompt_values, grad_out, lengths):
    by_group = (BLK, 2, PG, HD)
    q_rows = queries.reshape(by_group)
    do_rows = grad_out.reshape(by_group)
    joined = jnp.concatenate([rollout_keys[0], prompt_keys, rollout_values[0], prompt_values])
    joined = lax.optimization_barrier(joined).reshape(2, BLK + 32, 2, HD)
    out, dq, dkv, dprompt = attention(lengths, q_rows, do_rows, joined.transpose(2, 0, 1, 3))
    dkv = dkv.transpose(1, 2, 0, 3)
    dprompt = dprompt.transpose(1, 2, 0, 3)
    return (
        out.reshape(queries.shape),
        dq.reshape(queries.shape),
        dkv[0][None],
        dkv[1][None],
        dprompt[0],
        dprompt[1],
    )


def solution(mesh):
    rows = P("roll", "seq", "head", None)
    prompt = P(("seq", "roll"), "head", None)
    return jax.shard_map(
        local,
        mesh=mesh,
        in_specs=(rows, rows, rows, prompt, prompt, rows, P("roll")),
        out_specs=(rows, rows, rows, rows, prompt, prompt),
        check_vma=False,
    )
```

```python
import math

import jax
import jax.numpy as jnp
from jax import lax
from jax.experimental import pallas as pl
from jax.experimental.pallas import tpu as pltpu
from jax.sharding import PartitionSpec as P

f32, bf16 = jnp.float32, jnp.bfloat16
N = 16
BLK = 192
PRM = 1024
HD = 128
PG = 8
RB = BLK * PG
TILE = 4 * BLK
HALF = 2 * BLK
RC = RB // 2
SCALE = HD**-0.5
SCALE2 = SCALE * math.log2(math.e)
NEG = -1e30
MESH = pl.DeviceIdType.MESH

NN = (((1,), (0,)), ((), ()))
NT = (((1,), (1,)), ((), ()))
TN = (((0,), (0,)), ((), ()))


F_PROMPT, F_FULL, F_DIAG, F_END, B_PROMPT, B_FULL, B_DIAG = range(7)
W_ROLL, W_Q, W_DO, W_TILE, SEND, DQ, GPY, PASS = (1 << i for i in range(8))


def schedule(x):
    low, top = min(x, 3 - x), max(x, 3 - x)
    late = 1 if x < 2 else 0
    steps = []

    def forward(b, tiles, waits):
        for t in tiles:
            last = top if b == late else low
            steps.append((F_DIAG if t == last else F_FULL, b, t, W_TILE if t in waits else 0))

    def prompt(b):
        steps.append((F_PROMPT, b, 0, W_Q if b else 0))
        steps.append((F_PROMPT, b, 1, 0 if b else W_ROLL))

    def backward_low(b):
        steps.append((B_PROMPT, b, 0, 0))
        for t in range(low + 1):
            last = t == low
            steps.append((B_DIAG if last else B_FULL, b, t, DQ if last else 0))

    prompt(0)
    if late:
        forward(0, range(low + 1), range(low + 1))
        steps.append((F_END, 0, 0, 0))
        backward_low(0)
        prompt(1)
        forward(1, range(top + 1), range(low + 1, top + 1))
        steps.append((F_END, 1, 0, W_DO))
    else:
        forward(0, (0, 1), (0, 1))
        prompt(1)
        forward(0, range(2, top + 1), range(2, top + 1))
        steps.append((F_END, 0, 0, 0))
        forward(1, range(low + 1), ())
        steps.append((F_END, 1, 0, W_DO))
        backward_low(1)
    order = [t for t in range(top, -1, -1) if t != x] + [x]
    prompt_at = len(order) - (1 if x < 2 else 2)
    waiting = []
    for i, t in enumerate(order):
        if i == prompt_at:
            ready = waiting.pop(0) if waiting and waiting[0][1] <= len(steps) - 2 else None
            steps.append((B_PROMPT, late, 0, GPY + PASS * (0 if ready is None else 1 + ready[0])))
        final = i == len(order) - 1
        ready = waiting.pop(0) if waiting and (final or waiting[0][1] <= len(steps) - 2) else None
        flags = SEND + PASS * (0 if ready is None else 1 + ready[0]) + (DQ if final else 0)
        waiting.append((t, len(steps)))
        steps.append((B_DIAG if t == top else B_FULL, late, t, flags))
    assert [t for t, _ in waiting] == [x]
    return [kind + 8 * b + 16 * t + 64 * flags for kind, b, t, flags in steps]


def dot(a, b, dims=NN):
    return lax.dot_general(a, b, dims, preferred_element_type=f32)


def kernel(
    length, q_in, do_in, kvp_in,
    out, dq, grads_out,
    raw, q2, do2, kv, acc, mx, tot, lse, off, o16, dk, dv, g16,
    zr, yrp, gyp, zrp, gx, gxp, xr, xrp,
    lsem, kvxs, kvxr, kvzs, kvzr, ppxs, ppxr, ppzs, ppzr, ppys, ppyr, qsem, osem,
    dsem, gzs, gzr, gpys, gpzs, gpzr, gxs, gxr, gpxs, gpxr,
):
    s = lax.axis_index("seq")
    r = lax.axis_index("roll")
    x, z = s // 4, s % 4
    kv_in = kvp_in.at[:, :, pl.ds(0, BLK), :]
    pk_in = kvp_in.at[:, :, pl.ds(BLK, 32), :]
    hs = x // 2
    top = jnp.maximum(x, 3 - x)
    partner = 4 * (3 - x) + z

    barrier = pltpu.get_barrier_semaphore()
    for d in range(1, 4):
        pl.semaphore_signal(barrier, inc=1, device_id={"seq": (x + d) % 4 * 4 + z}, device_id_type=MESH)
        pl.semaphore_signal(barrier, inc=1, device_id={"seq": 4 * x + (z + d) % 4}, device_id_type=MESH)
    pl.semaphore_signal(barrier, inc=1, device_id={"roll": 1 - r}, device_id_type=MESH)

    def remote(src, dst, ssem, rsem, **where):
        return pltpu.make_async_remote_copy(
            src_ref=src, dst_ref=dst, send_sem=ssem, recv_sem=rsem,
            device_id=where, device_id_type=MESH,
        )

    def kv_rows(j):
        return kv.at[:, pl.ds(pl.multiple_of(PRM + j * BLK, 64), BLK), :]

    def p_rows(xx):
        return kv.at[:, pl.ds(pl.multiple_of(r * 512 + z * 128 + xx * 32, 32), 32), :]

    def p_column(rr, zz):
        return kv.at[:, pl.ds(pl.multiple_of(rr * 512 + zz * 128, 128), 128), :]

    own_p = pltpu.make_async_copy(pk_in.at[hs], p_rows(x), lsem.at[3])
    own_p.start()
    own_kv = pltpu.make_async_copy(kv_in.at[hs], kv_rows(s), lsem.at[2])
    own_kv.start()
    own_q = pltpu.make_async_copy(q_in.at[:, hs], raw.at[0, 0], lsem.at[0])
    own_q.start()
    own_do = pltpu.make_async_copy(do_in.at[:, hs], raw.at[1, 0], lsem.at[1])
    own_do.start()
    pl.semaphore_wait(barrier, 7)

    def kvx_copy(xx):
        return remote(kv_in.at[xx // 2], kv_rows(s), kvxs.at[xx], kvxr.at[x], seq=4 * xx + z)

    def px_copy(xx):
        return remote(pk_in.at[xx // 2], p_rows(x), ppxs.at[xx], ppxr.at[x], seq=4 * xx + z)

    def pz_copy(zz):
        return remote(p_column(r, z), p_column(r, z), ppzs.at[zz], ppzr.at[z], seq=4 * x + zz)

    def py_copy(zz):
        return remote(p_column(r, zz), p_column(r, zz), ppys.at[zz], ppyr.at[zz], roll=1 - r)

    def kvz_copy(zz, tile):
        rows = kv_rows(4 * tile + z)
        return remote(rows, rows, kvzs.at[zz, tile], kvzr.at[z, tile], seq=4 * x + zz)

    def uses(zz, tile, other):
        return (tile != top) | (other <= zz // 2 * 2 + 1)

    def gives(zz, tile, other):
        return (tile != top) | (other < zz)

    def sees(xx):
        return x <= jnp.maximum(xx, 3 - xx)

    @pl.loop(1, 4)
    def _(d):
        px_copy((x + d) % 4).start()

    @pl.loop(1, 4)
    def _(d):
        xx = (x + d) % 4

        @pl.when(sees(xx))
        def _():
            kvx_copy(xx).start()

    q_out = remote(q_in.at[:, 1 - hs], raw.at[0, 1], qsem.at[0], qsem.at[1], seq=partner)
    q_out.start()
    acc[...] = jnp.zeros_like(acc)
    mx[...] = jnp.full_like(mx, NEG)
    tot[...] = jnp.zeros_like(tot)
    dk[...] = jnp.zeros_like(dk)
    dv[...] = jnp.zeros_like(dv)
    own_p.wait()

    @pl.loop(1, 4)
    def _(d):
        xx = (x + d) % 4
        remote(pk_in.at[hs], p_rows(xx), ppxs.at[xx], ppxr.at[xx], seq=4 * xx + z).wait_recv()

    @pl.loop(1, 4)
    def _(d):
        pz_copy((z + d) % 4).start()

    py_copy(z).start()
    @pl.loop(1, 4)
    def _(d):
        zz = (z + d) % 4
        remote(p_column(r, zz), p_column(r, zz), ppzs.at[zz], ppzr.at[zz], seq=4 * x + zz).wait_recv()
        py_copy(zz).start()

    own_kv.wait()

    @pl.loop(0, top + 1)
    def _(tile):
        @pl.when(tile != x)
        def _():
            remote(kv_in.at[hs], kv_rows(4 * tile + z), kvxs.at[tile], kvxr.at[tile], seq=4 * tile + z).wait_recv()

        @pl.loop(1, 4)
        def _(d):
            @pl.when(uses((z + d) % 4, tile, z))
            def _():
                kvz_copy((z + d) % 4, tile).start()

    do_out = remote(do_in.at[:, 1 - hs], raw.at[1, 1], qsem.at[2], qsem.at[3], seq=partner)
    do_out.start()

    def block_of(b):
        return jnp.where(b == 0, s, partner)

    def masked_scores(scores, k0, q0):
        key_pos = k0 - PRM + lax.broadcasted_iota(jnp.int32, scores.shape, 0)
        query_pos = q0 + lax.broadcasted_iota(jnp.int32, scores.shape, 1) // PG
        return jnp.where(key_pos <= query_pos, scores, NEG)

    def forward_tile(b, k0, size, masked):
        rows = pl.ds(pl.multiple_of(k0, 64), size)
        scores = dot(kv[0, rows, :], q2[b], NT) * SCALE2
        if masked:
            scores = masked_scores(scores, k0, block_of(b) * BLK)
        old = mx[b]
        new = jnp.maximum(old, jnp.max(scores, 0, keepdims=True))
        lifted = jnp.exp2(scores - new)
        shrink = jnp.exp2(old - new)
        mx[b] = new
        tot[b] = tot[b] * shrink + jnp.sum(lifted, 0, keepdims=True)
        acc[b] = acc[b] * shrink + dot(kv[1, rows, :], lifted.astype(bf16), TN)

    def take_q(b):
        q2[b] = raw[0, b].reshape(RB, HD)

    def take_do(b):
        row_pos = block_of(b) * BLK + lax.broadcasted_iota(jnp.int32, (RB, HD), 0) // PG
        rows = raw[1, b].reshape(RB, HD).astype(f32)
        do2[b] = jnp.where(row_pos < length[0], rows, 0.0).astype(bf16)

    own_q.wait()
    take_q(0)
    own_do.wait()
    take_do(0)

    def wait_tile(tile):
        @pl.loop(1, 4)
        def _(d):
            zz = (z + d) % 4
            rows = kv_rows(4 * tile + zz)

            @pl.when(uses(z, tile, zz))
            def _():
                remote(rows, rows, kvzs.at[zz, tile], kvzr.at[zz, tile], seq=4 * x + zz).wait_recv()

    def backward_tile(b, k0, size, masked, after=lambda c: None):
        rows = pl.ds(pl.multiple_of(k0, 64), size)

        for c in range(RB // RC):
            part = pl.ds(c * RC, RC)
            keys, values = kv[0, rows, :], kv[1, rows, :]
            queries, cot = q2[b, part, :], do2[b, part, :]
            scores = dot(keys, queries, NT) * SCALE2
            if masked:
                scores = masked_scores(scores, k0, block_of(b) * BLK + c * (RC // PG))
            weights = jnp.exp2(scores - lse[b, :, part])
            grads = (weights * (dot(values, cot, NT) - off[b, :, part])).astype(bf16)
            dv[rows, :] += dot(weights.astype(bf16), cot)
            dk[rows, :] += dot(grads, queries)
            acc[b, :, part] += dot(keys, grads, TN)
            after(c)

    def finish_rows(k0, size):
        rows = pl.ds(pl.multiple_of(k0, 64), size)
        g16[0, rows, :] = (dk[rows, :] * SCALE).astype(bf16)
        g16[1, rows, :] = dv[rows, :].astype(bf16)

    def grad_rows(j):
        return pl.ds(pl.multiple_of(PRM + j * BLK, 64), BLK)

    def gz_copy(zz, tile):
        rows = grad_rows(4 * tile + zz)
        return remote(g16.at[:, rows, :], zr.at[z, tile], gzs.at[zz, tile], gzr.at[z, tile], seq=4 * x + zz)

    def gx_copy(tile):
        return remote(gx.at[tile], xr.at[x], gxs.at[tile], gxr.at[x], seq=4 * tile + z)

    def send_tile(tile):
        finish_rows(PRM + tile * TILE, TILE)

        @pl.loop(1, 4)
        def _(d):
            @pl.when(gives(z, tile, (z + d) % 4))
            def _():
                gz_copy((z + d) % 4, tile).start()

    def send_half(tile, half):
        finish_rows(PRM + tile * TILE + half * HALF, HALF)

        @pl.loop(2 * half, 2 * half + 2)
        def _(zz):
            @pl.when((zz != z) & gives(z, tile, zz))
            def _():
                gz_copy(zz, tile).start()

    def pass_tile(tile):
        rows = grad_rows(4 * tile + z)
        total = g16[:, rows, :].astype(f32)
        for d in range(1, 4):
            zz = (z + d) % 4
            given = gives(zz, tile, z)

            @pl.when(given)
            def _():
                remote(g16.at[:, rows, :], zr.at[zz, tile], gzs.at[zz, tile], gzr.at[zz, tile], seq=4 * x + zz).wait_recv()

            total = total + jnp.where(given, zr[zz, tile].astype(f32), 0.0)

        @pl.when(tile == x)
        def _():
            xr[x] = total.astype(bf16)

        @pl.when(tile != x)
        def _():
            gx[tile] = total.astype(bf16)
            gx_copy(tile).start()

    mine = pl.ds(pl.multiple_of(r * 512, 512), 512)
    theirs = pl.ds(pl.multiple_of((1 - r) * 512, 512), 512)
    gpy_out = remote(g16.at[:, theirs, :], yrp, gpys.at[0], gpys.at[1], roll=1 - r)

    def gpz_copy(zz):
        rows = pl.ds(pl.multiple_of(zz * 128, 128), 128)
        return remote(gyp.at[:, rows, :], zrp.at[z], gpzs.at[zz], gpzr.at[z], seq=4 * x + zz)

    def gpx_copy(xx):
        rows = pl.ds(pl.multiple_of(xx * 32, 32), 32)
        return remote(gxp.at[:, rows, :], xrp.at[x], gpxs.at[xx], gpxr.at[x], seq=4 * xx + z)

    def pass_rolls():
        gpy_out.wait_recv()
        gyp[0] = (dk[mine, :] * SCALE + yrp[0].astype(f32)).astype(bf16)
        gyp[1] = (dv[mine, :] + yrp[1].astype(f32)).astype(bf16)

        @pl.loop(1, 4)
        def _(d):
            gpz_copy((z + d) % 4).start()

    def pass_prompt():
        rows = pl.ds(pl.multiple_of(z * 128, 128), 128)
        total = gyp[:, rows, :].astype(f32)
        for d in range(1, 4):
            zz = (z + d) % 4
            remote(gyp.at[:, rows, :], zrp.at[zz], gpzs.at[zz], gpzr.at[zz], seq=4 * x + zz).wait_recv()
            total = total + zrp[zz].astype(f32)
        gxp[...] = total.astype(bf16)

        @pl.loop(1, 4)
        def _(d):
            gpx_copy((x + d) % 4).start()

        xrp[x] = gxp[:, pl.ds(pl.multiple_of(x * 32, 32), 32), :]

    def dq_copies(c):
        rows = pl.ds(c * (RC // PG), RC // PG)
        return (
            pltpu.make_async_copy(o16.at[2, rows], dq.at[rows, hs], dsem.at[c]),
            remote(o16.at[3, rows], dq.at[rows, hs], dsem.at[2 + c], dsem.at[4 + c], seq=partner),
        )

    def send_dq(b, c):
        part = (acc[b, :, pl.ds(c * RC, RC)] * SCALE).T.astype(bf16)
        o16[2 + b, pl.ds(c * (RC // PG), RC // PG)] = part.reshape(RC // PG, PG, HD)

        @pl.when(b == 0)
        def _():
            dq_copies(c)[0].start()

        @pl.when(b == 1)
        def _():
            dq_copies(c)[1].start()

    own_out = pltpu.make_async_copy(o16.at[0], out.at[:, hs], lsem.at[4])
    out_out = remote(o16.at[1], out.at[:, hs], osem.at[0], osem.at[1], seq=partner)
    plans = [schedule(xx) for xx in range(4)]

    @pl.loop(0, len(plans[0]))
    def _(i):
        code = jnp.int32(0)
        for n, column in enumerate(zip(*plans)):
            here = jnp.where(x == 0, column[0], jnp.where(x == 1, column[1], jnp.where(x == 2, column[2], column[3])))
            code = jnp.where(i == n, here, code)
        kind = code % 8
        b = code // 8 % 2
        tile = code // 16 % 4
        flags = code // 64

        def has(flag):
            return flags // flag % 2 == 1

        @pl.when(has(W_Q))
        def _():
            q_out.wait_recv()
            take_q(1)

        @pl.when(has(W_ROLL))
        def _():
            @pl.loop(0, 4)
            def _(zz):
                rows = p_column(1 - r, zz)
                remote(rows, rows, ppys.at[zz], ppyr.at[zz], roll=1 - r).wait_recv()

        @pl.when(has(W_TILE))
        def _():
            wait_tile(tile)

        @pl.when(has(W_DO))
        def _():
            do_out.wait_recv()
            take_do(1)

        @pl.when(kind == F_PROMPT)
        def _():
            forward_tile(b, (r + tile) % 2 * 512, 512, False)

        @pl.when(kind == F_FULL)
        def _():
            forward_tile(b, PRM + tile * TILE, TILE, False)

        @pl.when(kind == F_DIAG)
        def _():
            @pl.loop(0, 1 + z // 2)
            def _(half):
                forward_tile(b, PRM + tile * TILE + half * HALF, HALF, True)

        @pl.when(kind == F_END)
        def _():
            total = tot[b]
            normal = acc[b] / total
            lse[b] = mx[b] + jnp.log2(total)
            off[b] = jnp.sum(normal * do2[b].astype(f32).T, 0, keepdims=True)
            row_pos = block_of(b) * BLK + lax.broadcasted_iota(jnp.int32, (1, RB), 1) // PG
            o16[b] = jnp.where(row_pos < length[0], normal, 0.0).T.astype(bf16).reshape(BLK, PG, HD)
            acc[b] = jnp.zeros(acc.shape[1:], f32)

            @pl.when(b == 0)
            def _():
                own_out.start()

            @pl.when(b == 1)
            def _():
                out_out.start()

        @pl.when(kind == B_PROMPT)
        def _():
            backward_tile(b, 0, PRM, False)

        @pl.when((kind == B_FULL) & jnp.logical_not(has(SEND) & has(DQ)))
        def _():
            backward_tile(b, PRM + tile * TILE, TILE, False)

        @pl.when((kind == B_FULL) & has(SEND) & has(DQ))
        def _():
            @pl.loop(0, 2)
            def _(half):
                def after(c):
                    @pl.when(half == 1)
                    def _():
                        send_dq(b, c)

                backward_tile(b, PRM + tile * TILE + half * HALF, HALF, False, after)
                send_half(tile, half)

        @pl.when(kind == B_DIAG)
        def _():
            @pl.loop(0, 1 + z // 2)
            def _(half):
                backward_tile(b, PRM + tile * TILE + half * HALF, HALF, True)

                @pl.when(has(SEND) & has(DQ))
                def _():
                    send_half(tile, half)

            @pl.when(has(DQ))
            def _():
                for c in range(RB // RC):
                    send_dq(b, c)

        @pl.when(has(SEND) & jnp.logical_not(has(DQ)))
        def _():
            send_tile(tile)

        @pl.when(has(GPY))
        def _():
            finish_rows(0, PRM)
            gpy_out.start()

        @pl.when(flags >= PASS)
        def _():
            pass_tile(flags // PASS - 1)

    pass_rolls()
    pass_tile(x)
    pass_prompt()

    @pl.loop(1, 4)
    def _(d):
        xx = (x + d) % 4
        remote(gxp.at[:, pl.ds(0, 32), :], xrp.at[xx], gpxs.at[xx], gpxr.at[xx], seq=4 * xx + z).wait_recv()

    for h in range(2):
        total = (xrp[2 * h].astype(f32) + xrp[2 * h + 1].astype(f32)).astype(bf16)
        grads_out[h, BLK : BLK + 32] = total[0]
        grads_out[h, 2 * BLK + 32 :] = total[1]

    @pl.loop(1, 4)
    def _(d):
        xx = (x + d) % 4

        @pl.when(sees(xx))
        def _():
            remote(gx.at[xx], xr.at[xx], gxs.at[xx], gxr.at[xx], seq=4 * xx + z).wait_recv()

    for h in range(2):
        total = jnp.zeros(xr.shape[1:], f32)
        for xx in (2 * h, 2 * h + 1):
            total = total + jnp.where(x <= max(xx, 3 - xx), xr[xx].astype(f32), 0.0)
        grads_out[h, :BLK] = total[0].astype(bf16)
        grads_out[h, BLK + 32 : 2 * BLK + 32] = total[1].astype(bf16)

    py_copy(z).wait_send()
    gpy_out.wait_send()
    q_out.wait_send()
    do_out.wait_send()
    out_out.wait()
    own_out.wait()
    for c in range(RB // RC):
        for copy in dq_copies(c):
            copy.wait()

    @pl.loop(1, 4)
    def _(d):
        xx = (x + d) % 4
        zz = (z + d) % 4
        px_copy(xx).wait_send()
        pz_copy(zz).wait_send()
        py_copy(zz).wait_send()
        gpz_copy(zz).wait_send()
        gpx_copy(xx).wait_send()

        @pl.when(sees(xx))
        def _():
            kvx_copy(xx).wait_send()

        @pl.when(xx <= top)
        def _():
            gx_copy(xx).wait_send()

        @pl.loop(0, top + 1)
        def _(tile):
            @pl.when(uses(zz, tile, z))
            def _():
                kvz_copy(zz, tile).wait_send()

            @pl.when(gives(z, tile, zz))
            def _():
                gz_copy(zz, tile).wait_send()


def attention(lengths, q_rows, do_rows, kvp_rows):
    any_spec = pl.BlockSpec(memory_space=pl.ANY)
    vmem = pl.BlockSpec(memory_space=pltpu.VMEM)
    dma = pltpu.SemaphoreType.DMA
    return pl.pallas_call(
        kernel,
        out_shape=[
            jax.ShapeDtypeStruct((BLK, 2, PG, HD), bf16),
            jax.ShapeDtypeStruct((BLK, 2, PG, HD), bf16),
            jax.ShapeDtypeStruct((2, 2 * (BLK + 32), HD), bf16),
        ],
        in_specs=[pl.BlockSpec(memory_space=pltpu.SMEM)] + [any_spec] * 3,
        out_specs=[any_spec, any_spec, vmem],
        scratch_shapes=[
            pltpu.VMEM((2, 2, BLK, PG, HD), bf16),
            pltpu.VMEM((2, RB, HD), bf16),
            pltpu.VMEM((2, RB, HD), bf16),
            pltpu.VMEM((2, PRM + N * BLK, HD), bf16),
            pltpu.VMEM((2, HD, RB), f32),
            pltpu.VMEM((2, 1, RB), f32),
            pltpu.VMEM((2, 1, RB), f32),
            pltpu.VMEM((2, 1, RB), f32),
            pltpu.VMEM((2, 1, RB), f32),
            pltpu.VMEM((4, BLK, PG, HD), bf16),
            pltpu.VMEM((PRM + N * BLK, HD), f32),
            pltpu.VMEM((PRM + N * BLK, HD), f32),
            pltpu.VMEM((2, PRM + N * BLK, HD), bf16),
            pltpu.VMEM((4, 4, 2, BLK, HD), bf16),
            pltpu.VMEM((2, 512, HD), bf16),
            pltpu.VMEM((2, 512, HD), bf16),
            pltpu.VMEM((4, 2, 128, HD), bf16),
            pltpu.VMEM((4, 2, BLK, HD), bf16),
            pltpu.VMEM((2, 128, HD), bf16),
            pltpu.VMEM((4, 2, BLK, HD), bf16),
            pltpu.VMEM((4, 2, 32, HD), bf16),
            dma((8,)),
            dma((4,)),
            dma((4,)),
            dma((4, 4)),
            dma((4, 4)),
            dma((4,)),
            dma((4,)),
            dma((4,)),
            dma((4,)),
            dma((4,)),
            dma((4,)),
            dma((4,)),
            dma((2,)),
            dma((6,)),
            dma((4, 4)),
            dma((4, 4)),
            dma((2,)),
            dma((4,)),
            dma((4,)),
            dma((4,)),
            dma((4,)),
            dma((4,)),
            dma((4,)),
        ],
        compiler_params=pltpu.CompilerParams(
            collective_id=0, has_side_effects=True, vmem_limit_bytes=58 * 2**20
        ),
    )(lengths, q_rows, do_rows, kvp_rows)


def output_kernel(out_in, dq_in, grads, out, dq, d_keys, d_values, d_prompt_keys, d_prompt_values, held, sem):
    pieces = [
        (source.at[rows], held.at[n, rows], target.at[rows])
        for rows in (pl.ds(0, BLK // 2), pl.ds(BLK // 2, BLK // 2))
        for n, (source, target) in enumerate(((out_in, out), (dq_in, dq)))
    ]
    loads = [pltpu.make_async_copy(a, b, sem.at[0, i]) for i, (a, b, _) in enumerate(pieces)]
    stores = [pltpu.make_async_copy(b, c, sem.at[1, i]) for i, (_, b, c) in enumerate(pieces)]
    for load in loads:
        load.start()
    for load, store in zip(loads, stores):
        load.wait()
        store.start()
    first = 0
    for target in (d_keys, d_prompt_keys, d_values, d_prompt_values):
        count = target.shape[0]
        for h in range(2):
            target[:, h, :] = grads[h, first : first + count, :]
        first += count
    for store in stores:
        store.wait()


def write_outputs(out, dq, grads):
    any_spec = pl.BlockSpec(memory_space=pl.ANY)
    vmem = pl.BlockSpec(memory_space=pltpu.VMEM)
    rows = jax.ShapeDtypeStruct((BLK, 2, PG, HD), bf16)
    keys = jax.ShapeDtypeStruct((BLK, 2, HD), bf16)
    prompt = jax.ShapeDtypeStruct((32, 2, HD), bf16)
    return pl.pallas_call(
        output_kernel,
        out_shape=[rows, rows, keys, keys, prompt, prompt],
        in_specs=[any_spec, any_spec, vmem],
        out_specs=[any_spec, any_spec, vmem, vmem, vmem, vmem],
        scratch_shapes=[
            pltpu.VMEM((2, BLK, 2, PG, HD), bf16),
            pltpu.SemaphoreType.DMA((2, 4)),
        ],
        compiler_params=pltpu.CompilerParams(vmem_limit_bytes=58 * 2**20),
    )(out, dq, grads)


def local(queries, rollout_keys, rollout_values, prompt_keys, prompt_values, grad_out, lengths):
    by_group = (BLK, 2, PG, HD)
    q_rows = queries.reshape(by_group)
    do_rows = grad_out.reshape(by_group)
    joined = jnp.concatenate([rollout_keys[0], prompt_keys, rollout_values[0], prompt_values])
    joined = lax.optimization_barrier(joined).reshape(2, BLK + 32, 2, HD)
    out, dq, grads = attention(lengths, q_rows, do_rows, joined.transpose(2, 0, 1, 3))
    out, dq, d_keys, d_values, d_prompt_keys, d_prompt_values = write_outputs(out, dq, grads)
    return (
        out.reshape(queries.shape),
        dq.reshape(queries.shape),
        d_keys[None],
        d_values[None],
        d_prompt_keys,
        d_prompt_values,
    )


def solution(mesh):
    rows = P("roll", "seq", "head", None)
    prompt = P(("seq", "roll"), "head", None)
    return jax.shard_map(
        local,
        mesh=mesh,
        in_specs=(rows, rows, rows, prompt, prompt, rows, P("roll")),
        out_specs=(rows, rows, rows, rows, prompt, prompt),
        check_vma=False,
    )
```

```python
import math

import jax
import jax.numpy as jnp
from jax import lax
from jax.experimental import pallas as pl
from jax.experimental.pallas import tpu as pltpu
from jax.sharding import PartitionSpec as P

f32, bf16 = jnp.float32, jnp.bfloat16
N = 16
BLK = 192
PRM = 1024
HD = 128
PG = 8
RB = BLK * PG
TILE = 4 * BLK
HALF = 2 * BLK
RC = RB // 2
SCALE = HD**-0.5
SCALE2 = SCALE * math.log2(math.e)
NEG = -1e30
MESH = pl.DeviceIdType.MESH

NN = (((1,), (0,)), ((), ()))
NT = (((1,), (1,)), ((), ()))
TN = (((0,), (0,)), ((), ()))


F_PROMPT, F_FULL, F_DIAG, F_END, B_PROMPT, B_FULL, B_DIAG = range(7)
W_ROLL, W_Q, W_DO, W_TILE, SEND, DQ, GPY, PASS = (1 << i for i in range(8))


def schedule(x):
    low, top = min(x, 3 - x), max(x, 3 - x)
    late = 1 if x < 2 else 0
    steps = []

    def forward(b, tiles, waits):
        for t in tiles:
            last = top if b == late else low
            steps.append((F_DIAG if t == last else F_FULL, b, t, W_TILE if t in waits else 0))

    def prompt(b):
        steps.append((F_PROMPT, b, 0, W_Q if b else 0))
        steps.append((F_PROMPT, b, 1, 0 if b else W_ROLL))

    def backward_low(b):
        steps.append((B_PROMPT, b, 0, 0))
        for t in range(low + 1):
            last = t == low
            steps.append((B_DIAG if last else B_FULL, b, t, DQ if last else 0))

    prompt(0)
    if late:
        forward(0, range(low + 1), range(low + 1))
        steps.append((F_END, 0, 0, 0))
        backward_low(0)
        prompt(1)
        forward(1, range(top + 1), range(low + 1, top + 1))
        steps.append((F_END, 1, 0, W_DO))
    else:
        forward(0, (0, 1), (0, 1))
        prompt(1)
        forward(0, range(2, top + 1), range(2, top + 1))
        steps.append((F_END, 0, 0, 0))
        forward(1, range(low + 1), ())
        steps.append((F_END, 1, 0, W_DO))
        backward_low(1)
    order = [t for t in range(top, -1, -1) if t != x] + [x]
    prompt_at = len(order) - (1 if x < 2 else 2)
    waiting = []
    for i, t in enumerate(order):
        if i == prompt_at:
            ready = waiting.pop(0) if waiting and waiting[0][1] <= len(steps) - 2 else None
            steps.append((B_PROMPT, late, 0, GPY + PASS * (0 if ready is None else 1 + ready[0])))
        final = i == len(order) - 1
        ready = waiting.pop(0) if waiting and (final or waiting[0][1] <= len(steps) - 2) else None
        flags = SEND + PASS * (0 if ready is None else 1 + ready[0]) + (DQ if final else 0)
        waiting.append((t, len(steps)))
        steps.append((B_DIAG if t == top else B_FULL, late, t, flags))
    assert [t for t, _ in waiting] == [x]
    return [kind + 8 * b + 16 * t + 64 * flags for kind, b, t, flags in steps]


def dot(a, b, dims=NN):
    return lax.dot_general(a, b, dims, preferred_element_type=f32)


def kernel(
    length, q_in, do_in, kvp_in,
    out, dq, grads_out,
    raw, q2, do2, kv, acc, mx, tot, lse, off, o16, dk, dv, g16,
    zr, yrp, gyp, zrp, gx, gxp, xr, xrp,
    lsem, kvxs, kvxr, kvzs, kvzr, ppxs, ppxr, ppzs, ppzr, ppys, ppyr, qsem, osem,
    dsem, gzs, gzr, gpys, gpzs, gpzr, gxs, gxr, gpxs, gpxr,
):
    s = lax.axis_index("seq")
    r = lax.axis_index("roll")
    x, z = s // 4, s % 4
    kv_in = kvp_in.at[:, :, pl.ds(0, BLK), :]
    pk_in = kvp_in.at[:, :, pl.ds(BLK, 32), :]
    hs = x // 2
    top = jnp.maximum(x, 3 - x)
    partner = 4 * (3 - x) + z

    barrier = pltpu.get_barrier_semaphore()
    for d in range(1, 4):
        pl.semaphore_signal(barrier, inc=1, device_id={"seq": (x + d) % 4 * 4 + z}, device_id_type=MESH)
        pl.semaphore_signal(barrier, inc=1, device_id={"seq": 4 * x + (z + d) % 4}, device_id_type=MESH)
    pl.semaphore_signal(barrier, inc=1, device_id={"roll": 1 - r}, device_id_type=MESH)

    def remote(src, dst, ssem, rsem, **where):
        return pltpu.make_async_remote_copy(
            src_ref=src, dst_ref=dst, send_sem=ssem, recv_sem=rsem,
            device_id=where, device_id_type=MESH,
        )

    def kv_rows(j):
        return kv.at[:, pl.ds(pl.multiple_of(PRM + j * BLK, 64), BLK), :]

    def p_rows(xx):
        return kv.at[:, pl.ds(pl.multiple_of(r * 512 + z * 128 + xx * 32, 32), 32), :]

    def p_column(rr, zz):
        return kv.at[:, pl.ds(pl.multiple_of(rr * 512 + zz * 128, 128), 128), :]

    own_p = pltpu.make_async_copy(pk_in.at[hs], p_rows(x), lsem.at[3])
    own_p.start()
    own_kv = pltpu.make_async_copy(kv_in.at[hs], kv_rows(s), lsem.at[2])
    own_kv.start()
    own_q = pltpu.make_async_copy(q_in.at[:, hs], raw.at[0, 0], lsem.at[0])
    own_q.start()
    own_do = pltpu.make_async_copy(do_in.at[:, hs], raw.at[1, 0], lsem.at[1])
    own_do.start()
    pl.semaphore_wait(barrier, 7)

    def kvx_copy(xx):
        return remote(kv_in.at[xx // 2], kv_rows(s), kvxs.at[xx], kvxr.at[x], seq=4 * xx + z)

    def px_copy(xx):
        return remote(pk_in.at[xx // 2], p_rows(x), ppxs.at[xx], ppxr.at[x], seq=4 * xx + z)

    def pz_copy(zz):
        return remote(p_column(r, z), p_column(r, z), ppzs.at[zz], ppzr.at[z], seq=4 * x + zz)

    def py_copy(zz):
        return remote(p_column(r, zz), p_column(r, zz), ppys.at[zz], ppyr.at[zz], roll=1 - r)

    def kvz_copy(zz, tile):
        rows = kv_rows(4 * tile + z)
        return remote(rows, rows, kvzs.at[zz, tile], kvzr.at[z, tile], seq=4 * x + zz)

    def uses(zz, tile, other):
        return (tile != top) | (other <= zz // 2 * 2 + 1)

    def gives(zz, tile, other):
        return (tile != top) | (other < zz)

    def sees(xx):
        return x <= jnp.maximum(xx, 3 - xx)

    @pl.loop(1, 4)
    def _(d):
        px_copy((x + d) % 4).start()

    @pl.loop(1, 4)
    def _(d):
        xx = (x + d) % 4

        @pl.when(sees(xx))
        def _():
            kvx_copy(xx).start()

    q_out = remote(q_in.at[:, 1 - hs], raw.at[0, 1], qsem.at[0], qsem.at[1], seq=partner)
    q_out.start()
    acc[...] = jnp.zeros_like(acc)
    mx[...] = jnp.full_like(mx, NEG)
    tot[...] = jnp.zeros_like(tot)
    dk[...] = jnp.zeros_like(dk)
    dv[...] = jnp.zeros_like(dv)
    own_p.wait()

    @pl.loop(1, 4)
    def _(d):
        xx = (x + d) % 4
        remote(pk_in.at[hs], p_rows(xx), ppxs.at[xx], ppxr.at[xx], seq=4 * xx + z).wait_recv()

    @pl.loop(1, 4)
    def _(d):
        pz_copy((z + d) % 4).start()

    py_copy(z).start()
    @pl.loop(1, 4)
    def _(d):
        zz = (z + d) % 4
        remote(p_column(r, zz), p_column(r, zz), ppzs.at[zz], ppzr.at[zz], seq=4 * x + zz).wait_recv()
        py_copy(zz).start()

    own_kv.wait()

    @pl.loop(0, top + 1)
    def _(tile):
        @pl.when(tile != x)
        def _():
            remote(kv_in.at[hs], kv_rows(4 * tile + z), kvxs.at[tile], kvxr.at[tile], seq=4 * tile + z).wait_recv()

        @pl.loop(1, 4)
        def _(d):
            @pl.when(uses((z + d) % 4, tile, z))
            def _():
                kvz_copy((z + d) % 4, tile).start()

    do_out = remote(do_in.at[:, 1 - hs], raw.at[1, 1], qsem.at[2], qsem.at[3], seq=partner)
    do_out.start()

    def block_of(b):
        return jnp.where(b == 0, s, partner)

    def masked_scores(scores, k0, q0):
        key_pos = k0 - PRM + lax.broadcasted_iota(jnp.int32, scores.shape, 0)
        query_pos = q0 + lax.broadcasted_iota(jnp.int32, scores.shape, 1) // PG
        return jnp.where(key_pos <= query_pos, scores, NEG)

    def forward_tile(b, k0, size, masked):
        rows = pl.ds(pl.multiple_of(k0, 64), size)
        scores = dot(kv[0, rows, :], q2[b], NT) * SCALE2
        if masked:
            scores = masked_scores(scores, k0, block_of(b) * BLK)
        old = mx[b]
        new = jnp.maximum(old, jnp.max(scores, 0, keepdims=True))
        lifted = jnp.exp2(scores - new)
        shrink = jnp.exp2(old - new)
        mx[b] = new
        tot[b] = tot[b] * shrink + jnp.sum(lifted, 0, keepdims=True)
        acc[b] = acc[b] * shrink + dot(kv[1, rows, :], lifted.astype(bf16), TN)

    def take_q(b):
        q2[b] = raw[0, b].reshape(RB, HD)

    def take_do(b):
        row_pos = block_of(b) * BLK + lax.broadcasted_iota(jnp.int32, (RB, HD), 0) // PG
        rows = raw[1, b].reshape(RB, HD).astype(f32)
        do2[b] = jnp.where(row_pos < length[0], rows, 0.0).astype(bf16)

    own_q.wait()
    take_q(0)
    own_do.wait()
    take_do(0)

    def wait_tile(tile):
        @pl.loop(1, 4)
        def _(d):
            zz = (z + d) % 4
            rows = kv_rows(4 * tile + zz)

            @pl.when(uses(z, tile, zz))
            def _():
                remote(rows, rows, kvzs.at[zz, tile], kvzr.at[zz, tile], seq=4 * x + zz).wait_recv()

    def backward_tile(b, k0, size, masked, after=lambda c: None):
        rows = pl.ds(pl.multiple_of(k0, 64), size)

        for c in range(RB // RC):
            part = pl.ds(c * RC, RC)
            keys, values = kv[0, rows, :], kv[1, rows, :]
            queries, cot = q2[b, part, :], do2[b, part, :]
            scores = dot(keys, queries, NT) * SCALE2
            if masked:
                scores = masked_scores(scores, k0, block_of(b) * BLK + c * (RC // PG))
            weights = jnp.exp2(scores - lse[b, :, part])
            grads = (weights * (dot(values, cot, NT) - off[b, :, part])).astype(bf16)
            dv[rows, :] += dot(weights.astype(bf16), cot)
            dk[rows, :] += dot(grads, queries)
            acc[b, :, part] += dot(keys, grads, TN)
            after(c)

    def finish_rows(k0, size):
        rows = pl.ds(pl.multiple_of(k0, 64), size)
        g16[0, rows, :] = (dk[rows, :] * SCALE).astype(bf16)
        g16[1, rows, :] = dv[rows, :].astype(bf16)

    def grad_rows(j):
        return pl.ds(pl.multiple_of(PRM + j * BLK, 64), BLK)

    def gz_copy(zz, tile):
        rows = grad_rows(4 * tile + zz)
        return remote(g16.at[:, rows, :], zr.at[z, tile], gzs.at[zz, tile], gzr.at[z, tile], seq=4 * x + zz)

    def gx_copy(tile):
        return remote(gx.at[tile], xr.at[x], gxs.at[tile], gxr.at[x], seq=4 * tile + z)

    def send_tile(tile):
        finish_rows(PRM + tile * TILE, TILE)

        @pl.loop(1, 4)
        def _(d):
            @pl.when(gives(z, tile, (z + d) % 4))
            def _():
                gz_copy((z + d) % 4, tile).start()

    def send_half(tile, half):
        finish_rows(PRM + tile * TILE + half * HALF, HALF)

        @pl.loop(2 * half, 2 * half + 2)
        def _(zz):
            @pl.when((zz != z) & gives(z, tile, zz))
            def _():
                gz_copy(zz, tile).start()

    def pass_tile(tile):
        rows = grad_rows(4 * tile + z)
        total = g16[:, rows, :].astype(f32)
        for d in range(1, 4):
            zz = (z + d) % 4
            given = gives(zz, tile, z)

            @pl.when(given)
            def _():
                remote(g16.at[:, rows, :], zr.at[zz, tile], gzs.at[zz, tile], gzr.at[zz, tile], seq=4 * x + zz).wait_recv()

            total = total + jnp.where(given, zr[zz, tile].astype(f32), 0.0)

        @pl.when(tile == x)
        def _():
            xr[x] = total.astype(bf16)

        @pl.when(tile != x)
        def _():
            gx[tile] = total.astype(bf16)
            gx_copy(tile).start()

    mine = pl.ds(pl.multiple_of(r * 512, 512), 512)
    theirs = pl.ds(pl.multiple_of((1 - r) * 512, 512), 512)
    gpy_out = remote(g16.at[:, theirs, :], yrp, gpys.at[0], gpys.at[1], roll=1 - r)

    def gpz_copy(zz):
        rows = pl.ds(pl.multiple_of(zz * 128, 128), 128)
        return remote(gyp.at[:, rows, :], zrp.at[z], gpzs.at[zz], gpzr.at[z], seq=4 * x + zz)

    def gpx_copy(xx):
        rows = pl.ds(pl.multiple_of(xx * 32, 32), 32)
        return remote(gxp.at[:, rows, :], xrp.at[x], gpxs.at[xx], gpxr.at[x], seq=4 * xx + z)

    def pass_rolls():
        gpy_out.wait_recv()
        gyp[0] = (dk[mine, :] * SCALE + yrp[0].astype(f32)).astype(bf16)
        gyp[1] = (dv[mine, :] + yrp[1].astype(f32)).astype(bf16)

        @pl.loop(1, 4)
        def _(d):
            gpz_copy((z + d) % 4).start()

    def pass_prompt():
        rows = pl.ds(pl.multiple_of(z * 128, 128), 128)
        total = gyp[:, rows, :].astype(f32)
        for d in range(1, 4):
            zz = (z + d) % 4
            remote(gyp.at[:, rows, :], zrp.at[zz], gpzs.at[zz], gpzr.at[zz], seq=4 * x + zz).wait_recv()
            total = total + zrp[zz].astype(f32)
        gxp[...] = total.astype(bf16)

        @pl.loop(1, 4)
        def _(d):
            gpx_copy((x + d) % 4).start()

        xrp[x] = gxp[:, pl.ds(pl.multiple_of(x * 32, 32), 32), :]

    def dq_copies(c):
        rows = pl.ds(c * (RC // PG), RC // PG)
        return (
            pltpu.make_async_copy(o16.at[2, rows], dq.at[rows, hs], dsem.at[c]),
            remote(o16.at[3, rows], dq.at[rows, hs], dsem.at[2 + c], dsem.at[4 + c], seq=partner),
        )

    def send_dq(b, c):
        part = (acc[b, :, pl.ds(c * RC, RC)] * SCALE).T.astype(bf16)
        o16[2 + b, pl.ds(c * (RC // PG), RC // PG)] = part.reshape(RC // PG, PG, HD)

        @pl.when(b == 0)
        def _():
            dq_copies(c)[0].start()

        @pl.when(b == 1)
        def _():
            dq_copies(c)[1].start()

    own_out = pltpu.make_async_copy(o16.at[0], out.at[:, hs], lsem.at[4])
    out_out = remote(o16.at[1], out.at[:, hs], osem.at[0], osem.at[1], seq=partner)
    plans = [schedule(xx) for xx in range(4)]

    @pl.loop(0, len(plans[0]))
    def _(i):
        code = jnp.int32(0)
        for n, column in enumerate(zip(*plans)):
            here = jnp.where(x == 0, column[0], jnp.where(x == 1, column[1], jnp.where(x == 2, column[2], column[3])))
            code = jnp.where(i == n, here, code)
        kind = code % 8
        b = code // 8 % 2
        tile = code // 16 % 4
        flags = code // 64

        def has(flag):
            return flags // flag % 2 == 1

        @pl.when(has(W_Q))
        def _():
            q_out.wait_recv()
            take_q(1)

        @pl.when(has(W_ROLL))
        def _():
            @pl.loop(0, 4)
            def _(zz):
                rows = p_column(1 - r, zz)
                remote(rows, rows, ppys.at[zz], ppyr.at[zz], roll=1 - r).wait_recv()

        @pl.when(has(W_TILE))
        def _():
            wait_tile(tile)

        @pl.when(has(W_DO))
        def _():
            do_out.wait_recv()
            take_do(1)

        @pl.when(kind == F_PROMPT)
        def _():
            forward_tile(b, (r + tile) % 2 * 512, 512, False)

        @pl.when(kind == F_FULL)
        def _():
            forward_tile(b, PRM + tile * TILE, TILE, False)

        @pl.when(kind == F_DIAG)
        def _():
            @pl.loop(0, 1 + z // 2)
            def _(half):
                forward_tile(b, PRM + tile * TILE + half * HALF, HALF, True)

        @pl.when(kind == F_END)
        def _():
            total = tot[b]
            normal = acc[b] / total
            lse[b] = mx[b] + jnp.log2(total)
            off[b] = jnp.sum(normal * do2[b].astype(f32).T, 0, keepdims=True)
            row_pos = block_of(b) * BLK + lax.broadcasted_iota(jnp.int32, (1, RB), 1) // PG
            o16[b] = jnp.where(row_pos < length[0], normal, 0.0).T.astype(bf16).reshape(BLK, PG, HD)
            acc[b] = jnp.zeros(acc.shape[1:], f32)

            @pl.when(b == 0)
            def _():
                own_out.start()

            @pl.when(b == 1)
            def _():
                out_out.start()

        @pl.when(kind == B_PROMPT)
        def _():
            backward_tile(b, 0, PRM, False)

        @pl.when((kind == B_FULL) & jnp.logical_not(has(SEND) & has(DQ)))
        def _():
            backward_tile(b, PRM + tile * TILE, TILE, False)

        @pl.when((kind == B_FULL) & has(SEND) & has(DQ))
        def _():
            @pl.loop(0, 2)
            def _(half):
                def after(c):
                    @pl.when(half == 1)
                    def _():
                        send_dq(b, c)

                backward_tile(b, PRM + tile * TILE + half * HALF, HALF, False, after)
                send_half(tile, half)

        @pl.when(kind == B_DIAG)
        def _():
            @pl.loop(0, 1 + z // 2)
            def _(half):
                backward_tile(b, PRM + tile * TILE + half * HALF, HALF, True)

                @pl.when(has(SEND) & has(DQ))
                def _():
                    send_half(tile, half)

            @pl.when(has(DQ))
            def _():
                for c in range(RB // RC):
                    send_dq(b, c)

        @pl.when(has(SEND) & jnp.logical_not(has(DQ)))
        def _():
            send_tile(tile)

        @pl.when(has(GPY))
        def _():
            finish_rows(0, PRM)
            gpy_out.start()

        @pl.when(flags >= PASS)
        def _():
            pass_tile(flags // PASS - 1)

    pass_rolls()
    pass_tile(x)
    pass_prompt()

    @pl.loop(1, 4)
    def _(d):
        xx = (x + d) % 4
        remote(gxp.at[:, pl.ds(0, 32), :], xrp.at[xx], gpxs.at[xx], gpxr.at[xx], seq=4 * xx + z).wait_recv()

    for h in range(2):
        total = (xrp[2 * h].astype(f32) + xrp[2 * h + 1].astype(f32)).astype(bf16)
        grads_out[h, BLK : BLK + 32] = total[0]
        grads_out[h, 2 * BLK + 32 :] = total[1]

    @pl.loop(1, 4)
    def _(d):
        xx = (x + d) % 4

        @pl.when(sees(xx))
        def _():
            remote(gx.at[xx], xr.at[xx], gxs.at[xx], gxr.at[xx], seq=4 * xx + z).wait_recv()

    for h in range(2):
        total = jnp.zeros(xr.shape[1:], f32)
        for xx in (2 * h, 2 * h + 1):
            total = total + jnp.where(x <= max(xx, 3 - xx), xr[xx].astype(f32), 0.0)
        grads_out[h, :BLK] = total[0].astype(bf16)
        grads_out[h, BLK + 32 : 2 * BLK + 32] = total[1].astype(bf16)

    py_copy(z).wait_send()
    gpy_out.wait_send()
    q_out.wait_send()
    do_out.wait_send()
    out_out.wait()
    own_out.wait()
    for c in range(RB // RC):
        for copy in dq_copies(c):
            copy.wait()

    @pl.loop(1, 4)
    def _(d):
        xx = (x + d) % 4
        zz = (z + d) % 4
        px_copy(xx).wait_send()
        pz_copy(zz).wait_send()
        py_copy(zz).wait_send()
        gpz_copy(zz).wait_send()
        gpx_copy(xx).wait_send()

        @pl.when(sees(xx))
        def _():
            kvx_copy(xx).wait_send()

        @pl.when(xx <= top)
        def _():
            gx_copy(xx).wait_send()

        @pl.loop(0, top + 1)
        def _(tile):
            @pl.when(uses(zz, tile, z))
            def _():
                kvz_copy(zz, tile).wait_send()

            @pl.when(gives(z, tile, zz))
            def _():
                gz_copy(zz, tile).wait_send()


def attention(lengths, q_rows, do_rows, kvp_rows):
    any_spec = pl.BlockSpec(memory_space=pl.ANY)
    vmem = pl.BlockSpec(memory_space=pltpu.VMEM)
    dma = pltpu.SemaphoreType.DMA
    return pl.pallas_call(
        kernel,
        out_shape=[
            jax.ShapeDtypeStruct((BLK, 2, PG, HD), bf16),
            jax.ShapeDtypeStruct((BLK, 2, PG, HD), bf16),
            jax.ShapeDtypeStruct((2, 2 * (BLK + 32), HD), bf16),
        ],
        in_specs=[pl.BlockSpec(memory_space=pltpu.SMEM)] + [any_spec] * 3,
        out_specs=[any_spec, any_spec, vmem],
        scratch_shapes=[
            pltpu.VMEM((2, 2, BLK, PG, HD), bf16),
            pltpu.VMEM((2, RB, HD), bf16),
            pltpu.VMEM((2, RB, HD), bf16),
            pltpu.VMEM((2, PRM + N * BLK, HD), bf16),
            pltpu.VMEM((2, HD, RB), f32),
            pltpu.VMEM((2, 1, RB), f32),
            pltpu.VMEM((2, 1, RB), f32),
            pltpu.VMEM((2, 1, RB), f32),
            pltpu.VMEM((2, 1, RB), f32),
            pltpu.VMEM((4, BLK, PG, HD), bf16),
            pltpu.VMEM((PRM + N * BLK, HD), f32),
            pltpu.VMEM((PRM + N * BLK, HD), f32),
            pltpu.VMEM((2, PRM + N * BLK, HD), bf16),
            pltpu.VMEM((4, 4, 2, BLK, HD), bf16),
            pltpu.VMEM((2, 512, HD), bf16),
            pltpu.VMEM((2, 512, HD), bf16),
            pltpu.VMEM((4, 2, 128, HD), bf16),
            pltpu.VMEM((4, 2, BLK, HD), bf16),
            pltpu.VMEM((2, 128, HD), bf16),
            pltpu.VMEM((4, 2, BLK, HD), bf16),
            pltpu.VMEM((4, 2, 32, HD), bf16),
            dma((8,)),
            dma((4,)),
            dma((4,)),
            dma((4, 4)),
            dma((4, 4)),
            dma((4,)),
            dma((4,)),
            dma((4,)),
            dma((4,)),
            dma((4,)),
            dma((4,)),
            dma((4,)),
            dma((2,)),
            dma((6,)),
            dma((4, 4)),
            dma((4, 4)),
            dma((2,)),
            dma((4,)),
            dma((4,)),
            dma((4,)),
            dma((4,)),
            dma((4,)),
            dma((4,)),
        ],
        compiler_params=pltpu.CompilerParams(
            collective_id=0, has_side_effects=True, vmem_limit_bytes=58 * 2**20
        ),
    )(lengths, q_rows, do_rows, kvp_rows)


def output_kernel(out_in, dq_in, grads, out, dq, d_keys, d_values, d_prompt_keys, d_prompt_values, held, g_held, k_held, pk_held, v_held, pv_held, sem, gsem):
    load_g = pltpu.make_async_copy(grads, g_held, gsem.at[4])
    load_g.start()
    pieces = [
        (source.at[rows], held.at[n, rows], target.at[rows])
        for rows in (pl.ds(0, BLK // 2), pl.ds(BLK // 2, BLK // 2))
        for n, (source, target) in enumerate(((out_in, out), (dq_in, dq)))
    ]
    loads = [pltpu.make_async_copy(a, b, sem.at[0, i]) for i, (a, b, _) in enumerate(pieces)]
    stores = [pltpu.make_async_copy(b, c, sem.at[1, i]) for i, (_, b, c) in enumerate(pieces)]
    for load in loads:
        load.start()
    for load, store in zip(loads, stores):
        load.wait()
        store.start()
    load_g.wait()
    first = 0
    parts = ((k_held, d_keys), (v_held, d_values), (pk_held, d_prompt_keys), (pv_held, d_prompt_values))
    for n, (kept, target) in enumerate((parts[0], parts[2], parts[1], parts[3])):
        count = target.shape[0]
        for h in range(2):
            kept[:, h, :] = g_held[h, first : first + count, :]
        first += count
        store = pltpu.make_async_copy(kept, target, gsem.at[n])
        store.start()
        stores.append(store)
    for store in stores:
        store.wait()


def write_outputs(out, dq, grads):
    any_spec = pl.BlockSpec(memory_space=pl.ANY)
    rows = jax.ShapeDtypeStruct((BLK, 2, PG, HD), bf16)
    keys = jax.ShapeDtypeStruct((BLK, 2, HD), bf16)
    prompt = jax.ShapeDtypeStruct((32, 2, HD), bf16)
    return pl.pallas_call(
        output_kernel,
        out_shape=[rows, rows, keys, keys, prompt, prompt],
        in_specs=[any_spec] * 3,
        out_specs=[any_spec] * 6,
        scratch_shapes=[
            pltpu.VMEM((2, BLK, 2, PG, HD), bf16),
            pltpu.VMEM((2, 2 * (BLK + 32), HD), bf16),
            pltpu.VMEM((BLK, 2, HD), bf16),
            pltpu.VMEM((32, 2, HD), bf16),
            pltpu.VMEM((BLK, 2, HD), bf16),
            pltpu.VMEM((32, 2, HD), bf16),
            pltpu.SemaphoreType.DMA((2, 4)),
            pltpu.SemaphoreType.DMA((5,)),
        ],
        compiler_params=pltpu.CompilerParams(vmem_limit_bytes=58 * 2**20),
    )(out, dq, grads)


def local(queries, rollout_keys, rollout_values, prompt_keys, prompt_values, grad_out, lengths):
    by_group = (BLK, 2, PG, HD)
    q_rows = queries.reshape(by_group)
    do_rows = grad_out.reshape(by_group)
    joined = jnp.concatenate([rollout_keys[0], prompt_keys, rollout_values[0], prompt_values])
    joined = lax.optimization_barrier(joined).reshape(2, BLK + 32, 2, HD)
    out, dq, grads = attention(lengths, q_rows, do_rows, joined.transpose(2, 0, 1, 3))
    out, dq, d_keys, d_values, d_prompt_keys, d_prompt_values = write_outputs(out, dq, grads)
    return (
        out.reshape(queries.shape),
        dq.reshape(queries.shape),
        d_keys[None],
        d_values[None],
        d_prompt_keys,
        d_prompt_values,
    )


def solution(mesh):
    rows = P("roll", "seq", "head", None)
    prompt = P(("seq", "roll"), "head", None)
    return jax.shard_map(
        local,
        mesh=mesh,
        in_specs=(rows, rows, rows, prompt, prompt, rows, P("roll")),
        out_specs=(rows, rows, rows, rows, prompt, prompt),
        check_vma=False,
    )
```
